128 devices in a mesh: fsdp: 4 (over z), ctx: 32 (over x, y, core).
Axes of the slice: x: 4, y: 4, z: 4, core: 2. Of those that a mesh axis runs over, the one named last changes fastest.
Arguments:
- hidden: bfloat16 [16384, 1536], P(('fsdp', 'ctx')), may hold values from -6 to 6
- segments: int32 [16384], P(('fsdp', 'ctx')), may hold values from 0 to 3, as said below
- norm_gain: float32 [1536], replicated, may hold values from 0.5 to 8
- in_weight: bfloat16 [1536, 6448], P(('fsdp', 'ctx')), may hold values from -0.6 to 0.6
- conv_weight: float32 [4, 3328], replicated, may hold values from -3 to 3
- conv_bias: float32 [3328], replicated, may hold values from -3 to 3
- dt_bias: float32 [48], replicated, may hold values from -1 to 0.5
- a_log: float32 [48], replicated, may hold values from -14 to -2
- skip_scale: float32 [48], replicated, may hold values from 0.5 to 2
- gate_gain: float32 [3072], replicated, may hold values from 0.25 to 1.75
- out_weight: bfloat16 [1536, 3072], P(('fsdp', 'ctx')), may hold values from -0.109375 to 0.109375
- cotangent: bfloat16 [16384, 1536], P(('fsdp', 'ctx')), may hold values from -30 to 30
- in_momentum: float32 [1536, 6448], P(('fsdp', 'ctx')), may hold values from -1536 to 1536
- out_momentum: float32 [1536, 3072], P(('fsdp', 'ctx')), may hold values from -1536 to 1536
- vector_momentum: float32 [21392], replicated, may hold values from -80 to 80
Outputs:
- block_output: bfloat16 [16384, 1536], P(('fsdp', 'ctx'))
- input_grad: float32 [16384, 1536], P(('fsdp', 'ctx'))
- in_grad: float32 [1536, 6448], P(('fsdp', 'ctx'))
- in_momentum_new: float32 [1536, 6448], P(('fsdp', 'ctx'))
- in_weight_new: float32 [1536, 6448], P(('fsdp', 'ctx'))
- out_grad: float32 [1536, 3072], P(('fsdp', 'ctx'))
- out_momentum_new: float32 [1536, 3072], P(('fsdp', 'ctx'))
- out_weight_new: float32 [1536, 3072], P(('fsdp', 'ctx'))
- vector_grad: float32 [21392], replicated
- vector_momentum_new: float32 [21392], replicated
- vector_new: float32 [21392], replicated
The draws below stay inside these ranges and needn't reach their ends.
Inputs may be any that keep to these rules, and one draw needn't show every extreme that they name: `segments`: within each sequence of 4096 positions the document numbers start at 0 and rise by one at each new document, never falling; there are 4 documents, each of 200 positions or more.
All inputs are finite; a program needn't handle non-finite values.
Results may differ from the reference program's by a relative error of at most 0.028.
Values may be sent and summed in bfloat16 or wider, within the bound.
No kernel may reach another device: no remote copies, remote signals or barrier semaphores. Data moves between devices by JAX's collectives and lax.ppermute only.
A program may use at most 320 MiB of HBM per device.

```python
import math
import jax
import jax.numpy as jnp
from jax import lax

D = 1536
H = 48
P_SIZE = 64
N = 128
K = 4
GROUP = 256
NS_STEPS = 5
E = 3072
C = 3328
PROJ = 6448
NV = 21392
SEQ = 4096
SEQS = 4
TOKENS = 16384
DOCS = 4
DOC_MIN = 200


def draw_segments(key, part):
    key = jax.random.fold_in(key, 11)
    spare = SEQ - DOCS * DOC_MIN
    cuts = jnp.sort(jax.random.randint(key, (SEQS, DOCS - 1), 0, spare + 1), axis=1)
    bounds = cuts + DOC_MIN * jnp.arange(1, DOCS)[None, :]
    position = jnp.arange(SEQ)
    numbers = jnp.sum((position[None, :, None] >= bounds[:, None, :]).astype(jnp.int32), axis=2)
    return numbers.reshape(-1).astype(jnp.int32)


def draw_norm_gain(key, part):
    key = jax.random.fold_in(key, 12)
    ramp = jnp.exp(math.log(3.0) * jnp.arange(D, dtype=jnp.float32) / (D - 1))
    factor = jax.random.uniform(key, (D,), jnp.float32, 0.8, 1.25)
    return (ramp * factor).astype(jnp.float32)


def draw_in_weight(key, part):
    key = jax.random.fold_in(key, 13)
    base = jnp.clip(jax.random.normal(key, (D, PROJ), jnp.float32), -6.0, 6.0)
    column = jnp.arange(PROJ)
    column_scale = jnp.where(column < 2 * E, 1.0, 0.3)
    return (base * column_scale[None, :] * D ** (-0.5)).astype(jnp.bfloat16)


def draw_a_log(key, part):
    key = jax.random.fold_in(key, 14)
    spread = jax.random.uniform(key, (H,), jnp.float32)
    lower = math.log(0.5 / SEQ)
    upper = math.log(1.0 / 30.0)
    return (lower + spread * (upper - lower) + math.log(2.0)).astype(jnp.float32)


def draw_cotangent(key, part):
    key = jax.random.fold_in(key, 15)
    base = jnp.clip(jax.random.normal(key, (TOKENS, D), jnp.float32), -6.0, 6.0)
    ramp = jnp.exp(math.log(3.0) * jnp.arange(D, dtype=jnp.float32) / (D - 1))
    return (base * ramp[None, :]).astype(jnp.bfloat16)


def block_scale(own_key, shape, cuts, least, largest):
    loudness, own = 1.0, jax.random.fold_in(own_key, 6)
    for dim, shards_of in cuts:
        draws = jnp.exp(jax.random.uniform(jax.random.fold_in(own, dim), (shards_of,), jnp.float32, least / len(cuts), largest / len(cuts)))
        loudness = loudness * jnp.repeat(draws, shape[dim] // shards_of).reshape([-1 if axis == dim else 1 for axis in range(len(shape))])
    return loudness


def centred(stream_key, shape, deviation, most, cuts=(), kind=jnp.bfloat16):
    result = deviation * jax.random.normal(stream_key, shape, jnp.float32)
    if cuts:
        result = result * block_scale(stream_key, shape, cuts, -0.22, 0.18)
    return jnp.clip(result, -most, most).astype(kind)


def setup_inputs(seed: int = 0) -> dict:
    key_of = jax.random.split(jax.random.key(seed), 16)
    return {
        "hidden": centred(key_of[0], (TOKENS, D), 1.0, 6.0, ((0, 128),)),
        "segments": draw_segments(jax.random.fold_in(key_of[15], 71), 0),
        "norm_gain": draw_norm_gain(jax.random.fold_in(key_of[15], 71), 0),
        "in_weight": draw_in_weight(jax.random.fold_in(key_of[15], 71), 0),
        "conv_weight": centred(key_of[4], (K, C), K ** -0.5, 3.0, (), jnp.float32),
        "conv_bias": centred(key_of[5], (C,), 0.5, 3.0, (), jnp.float32),
        "dt_bias": jnp.clip(jax.random.uniform(key_of[6], (H,), jnp.float32, -1.0, 0.5), -1.0, 0.5),
        "a_log": draw_a_log(jax.random.fold_in(key_of[15], 71), 0),
        "skip_scale": jnp.clip(jax.random.uniform(key_of[8], (H,), jnp.float32, 0.5, 2.0), 0.5, 2.0),
        "gate_gain": jnp.clip(1.0 + 0.15 * jax.random.normal(key_of[9], (E,), jnp.float32), 0.25, 1.75),
        "out_weight": centred(key_of[10], (D, E), E ** -0.5, 0.109375, ((0, 128),)),
        "cotangent": draw_cotangent(jax.random.fold_in(key_of[15], 71), 0),
        "in_momentum": centred(key_of[12], (D, PROJ), (2 * TOKENS ** 0.5), 1536.0, ((0, 128),), jnp.float32),
        "out_momentum": centred(key_of[13], (D, E), (2 * TOKENS ** 0.5), 1536.0, ((0, 128),), jnp.float32),
        "vector_momentum": centred(key_of[14], (NV,), (0.1 * TOKENS ** 0.5), 80.0, (), jnp.float32),
    }


EPSILON = 1e-05
NORM_FLOOR = 1e-07
POLY_FIRST = 3.4445
POLY_SECOND = -4.775
POLY_THIRD = 2.0315
MATRIX_MOMENTUM = 0.95
MATRIX_RATE = 0.5
VECTOR_MOMENTUM = 0.9
VECTOR_RATE = 0.05
HIGHEST = lax.Precision.HIGHEST

@jax.custom_vjp
def low(v):
    return lax.optimization_barrier(v.astype(jnp.bfloat16)).astype(jnp.float32)

@jax.custom_vjp
def low_back(v):
    return v

def low_keep(v):
    return (low(v), None)

def low_pass(kept, grad):
    return (grad,)

def back_keep(v):
    return (v, None)

def back_low(kept, grad):
    return (low(grad),)
low.defvjp(low_keep, low_pass)
low_back.defvjp(back_keep, back_low)

def rounded(values):
    return lax.optimization_barrier(values.astype(jnp.bfloat16)).astype(jnp.float32)

def rms_scale(values, gain_vec):
    return values * lax.rsqrt(lax.optimization_barrier(jnp.mean(values * values, axis=-1, keepdims=True)) + EPSILON) * gain_vec

def gate_norm(outputs, gate_in, gain_vec):
    product = outputs * jax.nn.silu(gate_in)
    return product * lax.rsqrt(lax.optimization_barrier(jnp.mean(product * product, axis=-1, keepdims=True)) + EPSILON) * gain_vec

def conv_section(conv_in, edge_rows, edge_ids, seg_ids, conv_taps, conv_shift, dt_raw, dt_shift, decay_log, inner_width, state_width, num_heads):
    row_count = conv_in.shape[0]
    taps = conv_taps.shape[0]
    extended = jnp.concatenate([edge_rows, conv_in], axis=0)
    ext_ids = jnp.concatenate([edge_ids, seg_ids], axis=0)
    conv_sum = jnp.zeros_like(conv_in) + conv_shift[None, :]
    for conv_lag in range(taps):
        offset = taps - 1 - conv_lag
        same_doc = (ext_ids[offset:offset + row_count] == seg_ids).astype(jnp.float32)
        conv_sum = conv_sum + conv_taps[conv_lag][None, :] * extended[offset:offset + row_count] * same_doc[:, None]
    active = jax.nn.silu(conv_sum)
    head_size = inner_width // num_heads
    values_in = active[:, :inner_width].reshape(row_count, num_heads, head_size)
    b_proj = active[:, inner_width:inner_width + state_width]
    c_proj = active[:, inner_width + state_width:]
    step_size = jax.nn.softplus(dt_raw + dt_shift[None, :])
    log_decay = -jnp.exp(decay_log)[None, :] * step_size
    return (values_in, b_proj, c_proj, log_decay, step_size)

def ssd_piece(chain, inputs, direct_scale):
    state_in, prev_id = chain
    values_in, b_proj, c_proj, log_decay, step_size, seg_ids = inputs
    row_count = seg_ids.shape[0]
    cumulative = jnp.cumsum(log_decay, axis=0)
    cum_heads = cumulative.T
    row_index = lax.broadcasted_iota(jnp.int32, (row_count, row_count), 0)
    col_index = lax.broadcasted_iota(jnp.int32, (row_count, row_count), 1)
    keep_mask = (row_index >= col_index) & (seg_ids[:, None] == seg_ids[None, :])
    gap_matrix = cum_heads[:, :, None] - cum_heads[:, None, :]
    decay_matrix = jnp.where(keep_mask[None], jnp.exp(jnp.where(keep_mask[None], gap_matrix, 0.0)), 0.0)
    scores = jnp.dot(c_proj, b_proj.T, precision=HIGHEST)
    mixing = decay_matrix * scores[None] * step_size.T[:, None, :]
    within = jnp.einsum('hts,shp->thp', mixing, values_in, precision=HIGHEST)
    keep_flag = (seg_ids == prev_id).astype(jnp.float32)
    carried = jnp.einsum('tn,hpn->thp', c_proj, state_in, precision=HIGHEST) * (jnp.exp(cumulative) * keep_flag[:, None])[:, :, None]
    last_cum = cumulative[-1]
    tail_weight = jnp.exp(last_cum[None, :] - cumulative) * (seg_ids == seg_ids[-1]).astype(jnp.float32)[:, None] * step_size
    fresh = jnp.einsum('sh,shp,sn->hpn', tail_weight, values_in, b_proj, precision=HIGHEST)
    link_gain = jnp.exp(last_cum) * (seg_ids[-1] == prev_id).astype(jnp.float32)
    new_state = link_gain[:, None, None] * state_in + fresh
    outputs = within + carried + direct_scale[None, :, None] * values_in
    return ((new_state, seg_ids[-1]), outputs)

def ssd_scan(values_in, b_proj, c_proj, log_decay, step_size, seg_ids, prev_id, state_in, direct_scale, piece_rows):
    row_count = seg_ids.shape[0]
    pieces = row_count // piece_rows

    def split_rows(array):
        return array.reshape((pieces, piece_rows) + array.shape[1:])

    def piece_step(chain, inputs):
        return ssd_piece(chain, inputs, direct_scale)
    stacked = (split_rows(values_in), split_rows(b_proj), split_rows(c_proj), split_rows(log_decay), split_rows(step_size), split_rows(seg_ids))
    (state_out, last_id), outputs = lax.scan(jax.checkpoint(piece_step), (state_in, prev_id), stacked)
    return (outputs.reshape((row_count,) + values_in.shape[1:]), state_out)

def orthogonal(momentum):
    current = momentum / (jnp.sqrt(jnp.sum(momentum * momentum)) + NORM_FLOOR)
    for iteration in range(NS_STEPS):
        low_rows = rounded(current)
        gram_matrix = rounded(jnp.dot(low_rows, low_rows.T, precision=HIGHEST))
        polynomial = rounded(POLY_SECOND * gram_matrix + POLY_THIRD * jnp.dot(gram_matrix, gram_matrix, precision=HIGHEST))
        current = POLY_FIRST * low_rows + jnp.dot(polynomial, low_rows, precision=HIGHEST)
    return current

def reference(hidden, segments, norm_gain, in_weight, conv_weight, conv_bias, dt_bias, a_log, skip_scale, gate_gain, out_weight, cotangent, in_momentum, out_momentum, vector_momentum):
    seg_all = segments.astype(jnp.float32).reshape(SEQS, SEQ)
    piece_rows = min(SEQ, GROUP)

    def forward(hidden_full, gain_norm, in_full, conv_taps, conv_shift, dt_shift, decay_log, direct_scale, gain_gate, out_full):

        def one_sequence(inputs):
            rows_in, seg_ids = inputs
            normed = low(rms_scale(rows_in, gain_norm))
            projected = low_back(jnp.dot(normed, in_full, precision=HIGHEST))
            gate_in = projected[:, :E]
            conv_in = projected[:, E:E + C]
            dt_raw = projected[:, E + C:]
            edge_rows = jnp.zeros((K - 1, C), jnp.float32)
            edge_ids = jnp.zeros((K - 1,), jnp.float32) - 1.0
            values_in, b_proj, c_proj, log_decay, step_size = conv_section(conv_in, edge_rows, edge_ids, seg_ids, conv_taps, conv_shift, dt_raw, dt_shift, decay_log, E, N, H)
            outputs, final_state = ssd_scan(values_in, b_proj, c_proj, log_decay, step_size, seg_ids, seg_ids[0] - 1.0, jnp.zeros((H, P_SIZE, N), jnp.float32), direct_scale, piece_rows)
            gated = low(gate_norm(outputs.reshape(SEQ, E), gate_in, gain_gate))
            return rows_in + jnp.dot(gated, out_full.T, precision=HIGHEST)
        results = lax.map(one_sequence, (hidden_full.reshape(SEQS, SEQ, D), seg_all))
        return results.reshape(TOKENS, D)
    primal, pullback = jax.vjp(forward, hidden.astype(jnp.float32), norm_gain, in_weight.astype(jnp.float32), conv_weight, conv_bias, dt_bias, a_log, skip_scale, gate_gain, out_weight.astype(jnp.float32))
    grads = pullback(cotangent.astype(jnp.float32))
    input_grad = grads[0]
    in_grad = grads[2]
    out_grad = grads[9]
    vector_grad = jnp.concatenate([grads[1], grads[3].reshape(-1), grads[4], grads[5], grads[6], grads[7], grads[8]])
    in_momentum_new = MATRIX_MOMENTUM * in_momentum + in_grad
    out_momentum_new = MATRIX_MOMENTUM * out_momentum + out_grad
    in_weight_new = in_weight.astype(jnp.float32) - MATRIX_RATE * (PROJ / D) ** 0.5 * orthogonal(in_momentum_new)
    out_weight_new = out_weight.astype(jnp.float32) - MATRIX_RATE * (E / D) ** 0.5 * orthogonal(out_momentum_new)
    vector_old = jnp.concatenate([norm_gain, conv_weight.reshape(-1), conv_bias, dt_bias, a_log, skip_scale, gate_gain])
    vector_momentum_new = VECTOR_MOMENTUM * vector_momentum + (1.0 - VECTOR_MOMENTUM) * vector_grad
    vector_new = vector_old - VECTOR_RATE * vector_momentum_new
    return (primal.astype(jnp.bfloat16), input_grad, in_grad, in_momentum_new, in_weight_new, out_grad, out_momentum_new, out_weight_new, vector_grad, vector_momentum_new, vector_new)
```

```python
import math

import jax
import jax.numpy as jnp
from jax import lax
from jax.experimental import pallas as pl
from jax.experimental.pallas import tpu as pltpu
from jax.sharding import Mesh, PartitionSpec as P

NS_STEPS = 5
TWO_PART_STEPS = 2
CHUNK = 128
EPSILON = 1e-05
NORM_FLOOR = 1e-07
POLY_FIRST = 3.4445
POLY_SECOND = -4.775
POLY_THIRD = 2.0315
MATRIX_MOMENTUM = 0.95
MATRIX_RATE = 0.5
VECTOR_MOMENTUM = 0.9
VECTOR_RATE = 0.05
HIGHEST = lax.Precision.HIGHEST
F32 = jnp.float32
BF16 = jnp.bfloat16

EVERY = ("z", "x", "y", "c")
TEAM = ("y", "c")
ROWS = ("z", "x")

D = 1536
H = 48
HEAD = 64
N = 128
E = 3072
CH = 3328
PROJ = 6448
G = 8
HG = H // G
EG = E // G
BG = 2 * N // G
IN_COLS = 2 * EG + 128
OUT_COLS = EG
BLOCK = IN_COLS + OUT_COLS
FORWARD_COLS = 2 * EG + 2 * N + 128


def dot(a, b, dims):
    return lax.dot_general(
        a.astype(BF16), b.astype(BF16), (dims, ((), ())), preferred_element_type=F32
    )


def esum(spec, a, b):
    return jnp.einsum(spec, a.astype(BF16), b.astype(BF16), preferred_element_type=F32)


def spread(per_head):
    return jnp.repeat(per_head, HEAD, axis=-1)


def per_head_sum(values):
    return jnp.sum(values.reshape(values.shape[:-1] + (HG, HEAD)), axis=-1)


def gram_kernel(x_ref, g_ref):
    parts, n, _ = x_ref.shape
    tile = 256

    def rows(i, _):
        at = pl.ds(pl.multiple_of(i * tile, tile), tile)
        total = jnp.zeros((tile, n), F32)
        for p in range(parts):
            total = total + lax.dot_general(
                x_ref[p, at, :],
                x_ref[p],
                (((1,), (1,)), ((), ())),
                preferred_element_type=F32,
            )
        g_ref[at, :] = total
        return 0

    lax.fori_loop(0, n // tile, rows, 0)


def gram(x):
    n = x.shape[1]
    return pl.pallas_call(
        gram_kernel,
        out_shape=jax.ShapeDtypeStruct((n, n), F32),
        in_specs=[pl.BlockSpec(memory_space=pltpu.VMEM)],
        out_specs=pl.BlockSpec(memory_space=pltpu.VMEM),
        compiler_params=pltpu.CompilerParams(vmem_limit_bytes=48 << 20),
        cost_estimate=pl.CostEstimate(
            flops=2 * n * n * x.shape[0] * x.shape[2],
            bytes_accessed=2 * x.size + 4 * n * n,
            transcendentals=0,
        ),
        name="gram",
    )(x)


def chain_kernel(inverse_ref, g_ref, pick_ref, t_ref, high, low, h_high, h_low, q_ref):
    n = g_ref.shape[0]
    tile = 256
    inverse = inverse_ref[0]

    def at(i):
        return pl.ds(pl.multiple_of(i * tile, tile), tile)

    def parts(value):
        top = value.astype(BF16)
        return top, (value - top.astype(F32)).astype(BF16)

    def times(a, b):
        return jnp.dot(a, b, preferred_element_type=F32)

    def load(i, _):
        high[at(i), :], low[at(i), :] = parts(g_ref[at(i), :] * (inverse * inverse))
        return 0

    lax.fori_loop(0, n // tile, load, 0)
    for step in range(NS_STEPS):
        both = step < TWO_PART_STEPS
        q = q_ref.at[step]

        def polynomial(i, _):
            own = high[at(i), :]
            square = times(own, high[...])
            q[at(i), :] = (POLY_SECOND * own.astype(F32) + POLY_THIRD * square).astype(BF16)
            return 0

        lax.fori_loop(0, n // tile, polynomial, 0)
        if step == NS_STEPS - 1:
            break

        def left(i, _):
            own = q[at(i), :]
            value = times(own, high[...]) + POLY_FIRST * high[at(i), :].astype(F32)
            if both:
                value = value + times(own, low[...]) + POLY_FIRST * low[at(i), :].astype(F32)
                h_high[at(i), :], h_low[at(i), :] = parts(value)
            else:
                h_high[at(i), :] = value.astype(BF16)
            return 0

        lax.fori_loop(0, n // tile, left, 0)

        def right(i, _):
            own = h_high[at(i), :]
            value = times(own, q[...]) + POLY_FIRST * own.astype(F32)
            if both:
                rest = h_low[at(i), :]
                value = value + times(rest, q[...]) + POLY_FIRST * rest.astype(F32)
            if step + 1 < TWO_PART_STEPS:
                high[at(i), :], low[at(i), :] = parts(value)
            else:
                high[at(i), :] = value.astype(BF16)
            return 0

        lax.fori_loop(0, n // tile, right, 0)

    t = pick_ref[...]
    for step in reversed(range(NS_STEPS)):
        top, rest = parts(t)
        t = POLY_FIRST * t + times(top, q_ref[step]) + times(rest, q_ref[step])
    t_ref[...] = t * inverse


def chain(inverse, g, pick):
    n = g.shape[0]
    whole = pl.BlockSpec(memory_space=pltpu.VMEM)
    return pl.pallas_call(
        chain_kernel,
        out_shape=jax.ShapeDtypeStruct(pick.shape, F32),
        in_specs=[pl.BlockSpec(memory_space=pltpu.SMEM), whole, whole],
        out_specs=whole,
        scratch_shapes=[pltpu.VMEM((n, n), BF16)] * 4 + [pltpu.VMEM((NS_STEPS, n, n), BF16)],
        compiler_params=pltpu.CompilerParams(vmem_limit_bytes=60 << 20),
        cost_estimate=pl.CostEstimate(
            flops=34 * n * n * n, bytes_accessed=4 * n * n, transcendentals=0
        ),
        name="chain",
    )(inverse, g, pick)


def shift_all(value, axis, direction):
    size = lax.axis_size(axis)
    return [
        lax.ppermute(
            value,
            axis,
            [(s, s + direction * k) for s in range(size) if 0 <= s + direction * k < size],
        )
        for k in range(1, size)
    ]


def pack(state, gain):
    row = jnp.pad(gain, (0, N - HG))[None, :]
    return jnp.concatenate([state, jnp.pad(row, ((0, 7), (0, 0)))], axis=0)


def incoming_state(state, gain, direction):
    packed = shift_all(pack(state, gain), "x", direction)
    total = jnp.zeros_like(state)
    for arrived in reversed(packed):
        far_gain = spread(arrived[EG, :HG])
        total = arrived[:EG] + far_gain[:, None] * total
    return total


def blocks_of_columns(in_rows, out_rows):
    count = in_rows.shape[0]
    kind = in_rows.dtype
    z = in_rows[:, :E].reshape(count, G, EG)
    xs = in_rows[:, E : 2 * E].reshape(count, G, EG)
    bc = in_rows[:, 2 * E : 2 * E + 2 * N].reshape(count, G, BG)
    r = in_rows[:, 2 * E + 2 * N :].reshape(count, G, HG)
    fill = jnp.zeros((count, G, 128 - BG - HG), kind)
    out = out_rows.reshape(count, G, EG)
    return jnp.concatenate([z, xs, bc, r, fill, out], axis=2).transpose(1, 0, 2)


def rows_of_blocks(blocks):
    count = blocks.shape[1]
    b = blocks.transpose(1, 0, 2)
    pieces = [
        b[:, :, :EG].reshape(count, E),
        b[:, :, EG : 2 * EG].reshape(count, E),
        b[:, :, 2 * EG : 2 * EG + BG].reshape(count, 2 * N),
        b[:, :, 2 * EG + BG : 2 * EG + BG + HG].reshape(count, H),
    ]
    return jnp.concatenate(pieces, axis=1), b[:, :, IN_COLS:].reshape(count, E)


def local(
    hidden,
    segments,
    norm_gain,
    in_weight,
    conv_weight,
    conv_bias,
    dt_bias,
    a_log,
    skip_scale,
    gate_gain,
    out_weight,
    cotangent,
    in_momentum,
    out_momentum,
    vector_momentum,
):
    zi, xi, yi, ci = (lax.axis_index(a) for a in EVERY)
    team = yi * 2 + ci
    rows = hidden.shape[0]
    count = in_weight.shape[0]
    tokens = rows * G
    pieces = tokens // CHUNK

    def mine(values, width, start=0, axis=-1):
        return lax.dynamic_slice_in_dim(values, start + team * width, width, axis % values.ndim)

    hidden_team = lax.all_gather(hidden, TEAM, axis=0, tiled=True)
    z_w = in_weight[:, :E].reshape(count, G, EG)
    xs_w = in_weight[:, E : 2 * E].reshape(count, G, EG)
    bc_w = jnp.broadcast_to(in_weight[:, None, 2 * E : 2 * E + 2 * N], (count, G, 2 * N))
    r_w = jnp.pad(
        in_weight[:, 2 * E + 2 * N :].reshape(count, G, HG), ((0, 0), (0, 0), (0, 128 - HG))
    )
    out_w = out_weight.reshape(count, G, EG)
    sent = jnp.concatenate([z_w, xs_w, bc_w, r_w, out_w], axis=2).transpose(1, 0, 2)
    sent = jnp.concatenate(
        [
            sent,
            blocks_of_columns(in_momentum.astype(BF16), out_momentum.astype(BF16)),
        ],
        axis=2,
    )
    got = lax.all_to_all(sent, TEAM, 0, 0, tiled=True).reshape(G * count, -1)
    width = FORWARD_COLS + OUT_COLS
    momentum_block = got[:, width:].astype(F32)
    weights = lax.all_gather(got[:, :width], ROWS, axis=0, tiled=True)
    w_forward = weights[:, :FORWARD_COLS]
    w_out = weights[:, FORWARD_COLS:]
    w_own = jnp.concatenate(
        [
            weights[:, : 2 * EG],
            mine(weights[:, 2 * EG : 2 * EG + 2 * N], BG),
            weights[:, 2 * EG + 2 * N : 2 * EG + 2 * N + HG],
            jnp.zeros((D, 128 - BG - HG), BF16),
        ],
        axis=1,
    )
    q_team = lax.all_gather(cotangent, TEAM, axis=0, tiled=True)
    ids = lax.all_gather(segments, ("x",) + TEAM, axis=0, tiled=True)
    ids = lax.dynamic_slice_in_dim(
        jnp.pad(ids, (8, 8), constant_values=-1), xi * tokens, tokens + 16, 0
    )
    seg = ids[8 : 8 + tokens]
    edge_hidden = lax.ppermute(
        hidden_team[tokens - 8 :], "x", [(s, s + 1) for s in range(lax.axis_size("x") - 1)]
    )

    def normed_of(values):
        scale = lax.rsqrt(jnp.mean(values * values, axis=-1, keepdims=True) + EPSILON)
        return (values * scale * norm_gain).astype(BF16)

    normed = normed_of(hidden_team.astype(F32))
    projected = dot(normed, w_forward, ((1,), (0,)))
    edge = dot(normed_of(edge_hidden.astype(F32)), w_forward[:, EG : 2 * EG + 2 * N], ((1,), (0,)))
    z = projected[:, :EG]
    conv_in = projected[:, EG : 2 * EG + 2 * N]
    r = projected[:, 2 * EG + 2 * N : 2 * EG + 2 * N + HG]

    taps = conv_weight.shape[0]
    tap_own = jnp.concatenate([mine(conv_weight[:, :E], EG), conv_weight[:, E:]], axis=1)
    bias_own = jnp.concatenate([mine(conv_bias[:E], EG), conv_bias[E:]])
    extended = jnp.concatenate([edge, conv_in], axis=0)
    conv = jnp.zeros_like(conv_in) + bias_own[None, :]
    for lag in range(taps):
        same = (ids[8 - lag : 8 - lag + tokens] == seg).astype(F32)
        conv = conv + tap_own[lag][None, :] * extended[8 - lag : 8 - lag + tokens] * same[:, None]
    act = jax.nn.silu(conv)
    xs = act[:, :EG]
    bm = act[:, EG : EG + N].reshape(pieces, CHUNK, N)
    cm = act[:, EG + N :].reshape(pieces, CHUNK, N)
    dt_shift = mine(dt_bias, HG)
    rate = jnp.exp(mine(a_log, HG))
    skip = mine(skip_scale, HG)
    dt = jax.nn.softplus(r + dt_shift[None, :])
    la = -rate[None, :] * dt

    def chunked(values):
        return values.reshape((pieces, CHUNK) + values.shape[1:])

    seg_c = chunked(seg)
    before = chunked(ids[7 : 7 + tokens])[:, 0]
    dt_c, la_c = chunked(dt), chunked(la)
    xs_c = chunked(xs)
    ti = lax.broadcasted_iota(jnp.int32, (CHUNK, CHUNK), 0)
    si = lax.broadcasted_iota(jnp.int32, (CHUNK, CHUNK), 1)
    lower = (ti >= si).astype(F32)
    cum = jnp.einsum("ts,csh->cth", lower, la_c, precision=HIGHEST)
    cum_h = cum.transpose(0, 2, 1)
    dt_h = dt_c.transpose(0, 2, 1)
    mask = (ti >= si)[None] & (seg_c[:, :, None] == seg_c[:, None, :])
    gap = cum_h[:, :, :, None] - cum_h[:, :, None, :]
    decay = jnp.exp(jnp.where(mask[:, None], gap, -1e30))
    scores = esum("ctn,csn->cts", cm, bm)
    mixing = (decay * scores[:, None]).astype(BF16)
    xs_heads = xs_c.reshape(pieces, CHUNK, HG, HEAD)
    xdt = xs_c * spread(dt_c)
    xdt_heads = xdt.reshape(pieces, CHUNK, HG, HEAD)
    within = esum("chts,cshp->cthp", mixing, xdt_heads).reshape(pieces, CHUNK, EG)
    keep = (seg_c == before[:, None]).astype(F32)
    last = cum[:, -1]
    tail = jnp.exp(last[:, None] - cum) * (seg_c == seg_c[:, -1:]).astype(F32)[:, :, None]
    tail_wide = spread(tail)
    x_tail = (xdt * tail_wide).astype(BF16)
    fresh = esum("csp,csn->cpn", x_tail, bm)
    gain = jnp.exp(last) * (seg_c[:, -1] == before).astype(F32)[:, None]
    gain_wide = spread(gain)
    starts = [jnp.zeros((EG, N), F32)]
    reach = [jnp.ones((HG,), F32)]
    for p in range(pieces):
        starts.append(gain_wide[p][:, None] * starts[-1] + fresh[p])
        reach.append(gain[p] * reach[-1])
    arrived = incoming_state(starts[-1], reach[-1], 1)
    states = jnp.stack([s + spread(g)[:, None] * arrived for s, g in zip(starts, reach)])
    carry_gain = spread(jnp.exp(cum) * keep[:, :, None])
    carried = esum("ctn,cpn->ctp", cm, states[:pieces]) * carry_gain
    y_part = (within + carried).reshape(tokens, EG)
    skip_wide = spread(skip)
    y = y_part + skip_wide * xs

    d_gated = dot(q_team, w_out, ((1,), (0,)))
    gate_own = mine(gate_gain, EG)
    sig_z = jax.nn.sigmoid(z)
    silu_z = z * sig_z
    g = y * silu_z
    d_scaled = d_gated * gate_own
    sums = lax.psum(
        jnp.stack([jnp.sum(g * g, axis=1), jnp.sum(d_scaled * g, axis=1)]).reshape(-1, 128), TEAM
    ).reshape(2, tokens)
    root = lax.rsqrt(sums[0] / E + EPSILON)
    slope = sums[1] * root * root * root / E
    unit = g * root[:, None]
    gated = (unit * gate_own).astype(BF16)
    mixed = lax.psum_scatter(
        dot(gated, w_out, ((1,), (1,))), TEAM, scatter_dimension=0, tiled=True
    )
    hidden_own = hidden.astype(F32)
    block_output = (hidden_own + mixed).astype(BF16)
    out_partial = dot(q_team, gated, ((0,), (0,)))
    out_sum = lax.psum_scatter(out_partial, ROWS, scatter_dimension=0, tiled=True)
    d_gate_gain = jnp.sum(d_gated * unit, axis=0)
    d_g = root[:, None] * d_scaled - g * slope[:, None]
    d_y = d_g * silu_z
    d_z = d_g * y * (sig_z + silu_z * (1.0 - sig_z))

    dy_c = chunked(d_y)
    dy_low = dy_c.astype(BF16)
    dy_heads = dy_low.reshape(pieces, CHUNK, HG, HEAD)
    dy_carry = (dy_c * carry_gain).astype(BF16)
    back = esum("ctp,ctn->cpn", dy_carry, cm)
    ends = [jnp.zeros((EG, N), F32)]
    reach_back = [jnp.ones((HG,), F32)]
    for p in reversed(range(pieces)):
        ends.append(back[p] + gain_wide[p][:, None] * ends[-1])
        reach_back.append(gain[p] * reach_back[-1])
    adjoint_in = incoming_state(ends[-1], reach_back[-1], -1)
    adjoints = jnp.stack(
        [s + spread(w)[:, None] * adjoint_in for s, w in zip(ends, reach_back)][:pieces][::-1]
    )
    u_intra = esum("chts,cthp->cshp", mixing, dy_heads).reshape(pieces, CHUNK, EG)
    u = u_intra + esum("csn,cpn->csp", bm, adjoints) * tail_wide
    d_xs = (u * spread(dt_c) + skip_wide * dy_c).reshape(tokens, EG)
    d_dt = per_head_sum(xs_c * u)
    pair = esum("cthp,cshp->chts", dy_heads, xdt_heads)
    d_scores = jnp.sum(decay * pair, axis=1)
    d_bm = esum("cts,ctn->csn", d_scores, cm) + esum("csp,cpn->csn", x_tail, adjoints)
    d_cm = esum("cts,csn->ctn", d_scores, bm) + esum("ctp,cpn->ctn", dy_carry, states[:pieces])
    ends_inner = jnp.sum(
        (adjoints * states[1:]).reshape(pieces, HG, HEAD * N), axis=2
    )
    flow = per_head_sum(dy_c * chunked(y_part)) - dt_c * d_dt
    upper = (si >= ti).astype(F32)
    d_la = jnp.einsum("ts,csh->cth", upper, flow, precision=HIGHEST) + ends_inner[:, None]
    linked = (ids[7 : 7 + tokens] == seg).astype(F32)
    d_la = d_la.reshape(tokens, HG) * linked[:, None]
    d_dt = d_dt.reshape(tokens, HG)
    d_skip = jnp.sum(per_head_sum(d_y * xs), axis=0)
    d_r = (d_dt - rate[None, :] * d_la) * jax.nn.sigmoid(r + dt_shift[None, :])
    d_dt_bias = jnp.sum(d_r, axis=0)
    d_a_log = jnp.sum(d_la * la, axis=0)

    d_bc = jnp.concatenate([d_bm, d_cm], axis=2).reshape(tokens, 2 * N).T
    d_bc = lax.all_to_all(d_bc.reshape(G, BG, tokens), TEAM, 0, 0, tiled=True)
    d_bc = jnp.sum(d_bc, axis=0).T
    conv_own = jnp.concatenate([conv[:, :EG], mine(conv[:, EG:], BG)], axis=1)
    ext_own = jnp.concatenate([extended[:, :EG], mine(extended[:, EG:], BG)], axis=1)
    tap_mine = jnp.concatenate([tap_own[:, :EG], mine(tap_own[:, EG:], BG)], axis=1)
    sig_c = jax.nn.sigmoid(conv_own)
    d_conv = jnp.concatenate([d_xs, d_bc], axis=1) * (sig_c + conv_own * sig_c * (1.0 - sig_c))
    next_conv = lax.ppermute(
        d_conv[:8], "x", [(s, s - 1) for s in range(1, lax.axis_size("x"))]
    )
    d_ext = jnp.concatenate([d_conv, next_conv], axis=0)
    d_v = jnp.zeros_like(d_conv)
    d_taps = []
    for lag in range(taps):
        ahead = (ids[8 + lag : 8 + lag + tokens] == seg).astype(F32)
        d_v = d_v + tap_mine[lag][None, :] * d_ext[lag : lag + tokens] * ahead[:, None]
        same = (ids[8 - lag : 8 - lag + tokens] == seg).astype(F32)
        d_taps.append(
            jnp.sum(d_conv * ext_own[8 - lag : 8 - lag + tokens] * same[:, None], axis=0)
        )
    d_bias = jnp.sum(d_conv, axis=0)
    d_projected = jnp.concatenate(
        [d_z, d_v, d_r, jnp.zeros((tokens, 128 - BG - HG), F32)], axis=1
    ).astype(BF16)
    in_partial = dot(normed, d_projected, ((0,), (0,)))
    in_parts = lax.all_to_all(
        in_partial.astype(BF16).reshape(16, G * count, IN_COLS), ROWS, 0, 0, tiled=True
    )
    in_sum = jnp.sum(in_parts.astype(F32), axis=0)
    d_normed = lax.psum_scatter(
        dot(d_projected, w_own, ((1,), (1,))), TEAM, scatter_dimension=0, tiled=True
    )
    scale_own = lax.rsqrt(jnp.mean(hidden_own * hidden_own, axis=-1, keepdims=True) + EPSILON)
    unit_own = hidden_own * scale_own
    d_unit = d_normed * norm_gain
    d_hidden = scale_own * (
        d_unit - unit_own * jnp.mean(d_unit * unit_own, axis=-1, keepdims=True)
    )
    input_grad = cotangent.astype(F32) + d_hidden
    d_norm_gain = jnp.sum(d_normed * unit_own, axis=0)

    def wide(values):
        return lax.all_gather(values.astype(BF16), ("y", "z", "x")).reshape(4, D, -1)

    x_out = wide(MATRIX_MOMENTUM * momentum_block[:, IN_COLS:] + out_sum)
    x_in = wide(MATRIX_MOMENTUM * momentum_block[:, :IN_COLS] + in_sum)
    gram_out = gram(x_out)
    gram_in = gram(x_in)
    swap = [(0, 1), (1, 0)]
    first = ci == 0
    other = lax.ppermute(jnp.where(first, gram_out, gram_in), "c", swap)
    gram_own = jnp.where(first, gram_in, gram_out) + other
    diagonal = lax.broadcasted_iota(jnp.int32, (D, D), 0) == lax.broadcasted_iota(
        jnp.int32, (D, D), 1
    )
    square = jnp.sum(jnp.where(diagonal, gram_own, 0.0))
    inverse = 1.0 / (jnp.sqrt(square) + NORM_FLOOR)
    chip_row = (zi * 4 + xi) * (G * count) + yi * (2 * count)
    pick = (
        lax.broadcasted_iota(jnp.int32, (2 * count, D), 1)
        == lax.broadcasted_iota(jnp.int32, (2 * count, D), 0) + chip_row
    ).astype(F32)
    t_own = chain(inverse.reshape(1), gram_own, pick)
    t_other = lax.ppermute(t_own, "c", swap)
    t_in = jnp.where(first, t_own, t_other)
    t_out = jnp.where(first, t_other, t_own)

    def applied(t, x):
        top = t.astype(BF16)
        rest = (t - top.astype(F32)).astype(BF16)
        both = esum("rk,ykn->yrn", jnp.concatenate([top, rest], axis=0), x)
        return both[:, : 2 * count] + both[:, 2 * count :]

    halves = jnp.concatenate([applied(t_in, x_in), applied(t_out, x_out)], axis=2)
    half_own = lax.dynamic_slice_in_dim(halves, ci * count, count, 1)
    half_sent = lax.dynamic_slice_in_dim(halves, (1 - ci) * count, count, 1)
    half_got = lax.ppermute(half_sent, "c", swap)
    both = jnp.stack(
        [jnp.where(first, half_own, half_got), jnp.where(first, half_got, half_own)], axis=1
    ).reshape(G, count, BLOCK)
    step_in, step_out = rows_of_blocks(both)
    in_weight_new = in_weight.astype(F32) - MATRIX_RATE * math.sqrt(PROJ / D) * step_in
    out_weight_new = out_weight.astype(F32) - MATRIX_RATE * math.sqrt(E / D) * step_out

    sums_block = jnp.concatenate([in_sum, out_sum], axis=1).reshape(G, count, BLOCK)
    in_grad, out_grad = rows_of_blocks(lax.all_to_all(sums_block, TEAM, 0, 0, tiled=True))
    in_momentum_new = MATRIX_MOMENTUM * in_momentum + in_grad
    out_momentum_new = MATRIX_MOMENTUM * out_momentum + out_grad

    vector = jnp.concatenate(
        [d_norm_gain, jnp.concatenate(d_taps), d_bias, d_gate_gain, d_dt_bias, d_a_log, d_skip]
    )
    vector = jnp.pad(vector, (0, -vector.shape[0] % 1024)).reshape(-1, 128)
    vector = jnp.sum(lax.all_gather(vector, ROWS), axis=0)
    vector = lax.all_gather(vector, TEAM).reshape(G, -1)
    own = EG + BG
    grad_gain = jnp.sum(vector[:, :D], axis=0)
    conv_parts = vector[:, D : D + (taps + 1) * own].reshape(G, taps + 1, own).transpose(1, 0, 2)
    conv_parts = jnp.concatenate(
        [
            conv_parts[:, :, :EG].reshape(taps + 1, E),
            conv_parts[:, :, EG:].reshape(taps + 1, 2 * N),
        ],
        axis=1,
    )
    rest = vector[:, D + (taps + 1) * own :]
    heads = rest[:, EG : EG + 3 * HG].reshape(G, 3, HG).transpose(1, 0, 2).reshape(-1)
    vector_grad = jnp.concatenate(
        [grad_gain, conv_parts.reshape(-1), heads, rest[:, :EG].reshape(-1)]
    )
    vector_old = jnp.concatenate(
        [norm_gain, conv_weight.reshape(-1), conv_bias, dt_bias, a_log, skip_scale, gate_gain]
    )
    vector_momentum_new = VECTOR_MOMENTUM * vector_momentum + (1.0 - VECTOR_MOMENTUM) * vector_grad
    vector_new = vector_old - VECTOR_RATE * vector_momentum_new
    return (
        block_output,
        input_grad,
        in_grad,
        in_momentum_new,
        in_weight_new,
        out_grad,
        out_momentum_new,
        out_weight_new,
        vector_grad,
        vector_momentum_new,
        vector_new,
    )


def solution(mesh):
    grid = Mesh(mesh.devices.reshape(4, 4, 4, 2), EVERY)
    split = P(EVERY, None)
    return jax.shard_map(
        local,
        mesh=grid,
        in_specs=(
            split,
            P(EVERY),
            P(),
            split,
            P(),
            P(),
            P(),
            P(),
            P(),
            P(),
            split,
            split,
            split,
            split,
            P(),
        ),
        out_specs=(split,) * 8 + (P(),) * 3,
        check_vma=False,
    )
```

```python
import math

import jax
import jax.numpy as jnp
from jax import lax
from jax.experimental import pallas as pl
from jax.experimental.pallas import tpu as pltpu
from jax.sharding import Mesh, PartitionSpec as P

NS_STEPS = 5
EPSILON = 1e-05
NORM_FLOOR = 1e-07
POLY_FIRST = 3.4445
POLY_SECOND = -4.775
POLY_THIRD = 2.0315
MATRIX_MOMENTUM = 0.95
MATRIX_RATE = 0.5
VECTOR_MOMENTUM = 0.9
VECTOR_RATE = 0.05
HIGHEST = lax.Precision.HIGHEST
F32 = jnp.float32
BF16 = jnp.bfloat16

EVERY = ("z", "x", "y", "c")
TEAM = ("y", "c")
ROWS = ("z", "x")

D = 1536
H = 48
HEAD = 64
N = 128
E = 3072
PROJ = 6448
TAPS = 4
G = 8
HG = H // G
EG = E // G
BG = 2 * N // G
TOKENS = 1024
CHUNK = 128
PIECES = TOKENS // CHUNK
EDGE = 16
LANES = 128
VG = EG + 2 * N
IN_COLS = 2 * EG + LANES
BLOCK = IN_COLS + EG
FORWARD_COLS = EG + VG + LANES
LATE_COLS = EG + LANES
STATE_ROWS = N + 8
TILE = 256
AHEAD, KEEP, TAIL, GAIN, SEGMENT = 4, 9, 10, 11, 12


def dot(a, b, dims):
    return lax.dot_general(
        a.astype(BF16), b.astype(BF16), (dims, ((), ())), preferred_element_type=F32
    )


NN = ((1,), (0,))
NT = ((1,), (1,))
TN = ((0,), (0,))


def parts(value):
    top = value.astype(BF16)
    return top, (value - top.astype(F32)).astype(BF16)


def dot3(a, b, dims=NN):
    a_top, a_rest = parts(a)
    b_top, b_rest = parts(b)
    return dot(a_top, b_top, dims) + (dot(a_top, b_rest, dims) + dot(a_rest, b_top, dims))


def lane_of(shape):
    return lax.broadcasted_iota(jnp.int32, shape, 1)


def widen(per_head):
    rows = per_head.shape[0]
    left = lane_of((rows, LANES)) < HEAD
    return jnp.concatenate(
        [
            jnp.where(
                left,
                jnp.broadcast_to(per_head[:, 2 * p : 2 * p + 1], (rows, LANES)),
                jnp.broadcast_to(per_head[:, 2 * p + 1 : 2 * p + 2], (rows, LANES)),
            )
            for p in range(HG // 2)
        ],
        axis=1,
    )


def head_sums(values, summer):
    top, rest = parts(values)
    return dot(top, summer, NN) + dot(rest, summer, NN)


def pair_lanes(p):
    return slice(p * LANES, (p + 1) * LANES)


def stacked_pair(values):
    left = lane_of(values.shape) < HEAD
    zero = jnp.zeros_like(values)
    return jnp.concatenate(
        [jnp.where(left, values, zero), jnp.where(left, zero, values)], axis=0
    )


def silu_parts(values):
    sig = jax.nn.sigmoid(values)
    return sig, values * sig


def softplus(values):
    return jnp.maximum(values, 0.0) + jnp.log1p(jnp.exp(-jnp.abs(values)))


def square_iota():
    shape = (CHUNK, CHUNK)
    return lax.broadcasted_iota(jnp.int32, shape, 0), lane_of(shape)


def same_document(flags, row):
    return flags[:, SEGMENT : SEGMENT + 1] == row


def in_order(core_ref, own_ref, other_ref):
    own, other = own_ref[0], other_ref[0]
    first = core_ref[1] == 0
    return jnp.concatenate(
        [jnp.where(first, own, other), jnp.where(first, other, own)], axis=0
    )


def project_kernel(
    core_ref, own_ref, other_ref, edge_ref, w_ref, gain_ref, normed_ref, z_ref, v_ref, r_ref
):
    def put(x, at):
        x = x.astype(F32)
        scale = lax.rsqrt(jnp.mean(x * x, axis=1, keepdims=True) + EPSILON)
        normed = (x * scale * gain_ref[...]).astype(BF16)
        normed_ref[at, :] = normed
        out = jnp.dot(normed, w_ref[...], preferred_element_type=F32)
        z_ref[at, :] = out[:, :EG]
        v_ref[at, :] = out[:, EG : EG + VG]
        r_ref[at, :] = out[:, EG + VG :]

    last = pl.num_programs(0) - 1

    @pl.when(pl.program_id(0) < last)
    def _():
        put(in_order(core_ref, own_ref, other_ref), pl.ds(0, 2 * CHUNK))

    @pl.when(pl.program_id(0) == last)
    def _():
        put(edge_ref[...], pl.ds(0, EDGE))


def incoming_kernel(core_ref, own_ref, other_ref, w_ref, q_ref, d_gated_ref):
    q = in_order(core_ref, own_ref, other_ref)
    q_ref[...] = q
    d_gated_ref[...] = jnp.dot(q, w_ref[...], preferred_element_type=F32)


def early_kernel(normed_ref, q_ref, dz_ref, gated_ref, out_ref):
    out_ref[:, :EG] = dot(normed_ref[0:TOKENS, :], dz_ref[...], TN)
    out_ref[:, EG:] = dot(q_ref[...], gated_ref[...], TN)


def forward_kernel(
    v_ref,
    before_ref,
    r_ref,
    flags_ref,
    ids_ref,
    taps_ref,
    head_ref,
    conv_ref,
    dt_ref,
    cum_ref,
    y_ref,
    start_ref,
    reach_ref,
    gain_ref,
    packed_ref,
    state,
    reach,
):
    c = pl.program_id(0)

    @pl.when(c == 0)
    def _():
        state[...] = jnp.zeros_like(state)
        reach[...] = jnp.ones_like(reach)

    flags = flags_ref[...]
    window = jnp.concatenate([before_ref[...], v_ref[...]], axis=0)
    conv = taps_ref[TAPS : TAPS + 1, :] + taps_ref[0:1, :] * window[8:]
    for lag in range(1, TAPS):
        conv = conv + taps_ref[lag : lag + 1, :] * (
            pltpu.roll(window, lag, 0)[8:] * flags[:, lag : lag + 1]
        )
    conv_ref[...] = conv
    act = conv * jax.nn.sigmoid(conv)
    xs, bm, cm = act[:, :EG], act[:, EG : EG + N], act[:, EG + N :]
    dt = softplus(r_ref[...] + head_ref[0:1, :])
    dt_ref[...] = dt
    ti, si = square_iota()
    lower = (ti >= si).astype(F32)
    cum = jnp.dot(lower, -head_ref[1:2, :] * dt, precision=HIGHEST, preferred_element_type=F32)
    cum_ref[...] = cum
    cum_t = cum.T
    last = cum[CHUNK - 1 : CHUNK, :]
    tail = jnp.exp(last - cum) * flags[:, TAIL : TAIL + 1]
    carry = jnp.exp(cum) * flags[:, KEEP : KEEP + 1]
    gain = widen(jnp.exp(last) * flags[0:1, GAIN : GAIN + 1])
    xdt = xs * widen(dt)
    scores = dot3(cm, bm, NT)
    mask = (ti >= si) & same_document(flags, ids_ref[pl.ds(c, 1), :])
    within = []
    for p in range(HG // 2):
        mix = [
            jnp.exp(jnp.where(mask, cum[:, h : h + 1] - cum_t[h : h + 1, :], -1e30)) * scores
            for h in (2 * p, 2 * p + 1)
        ]
        within.append(
            dot3(jnp.concatenate(mix, axis=1), stacked_pair(xdt[:, pair_lanes(p)]))
        )
    y_ref[...] = jnp.concatenate(within, axis=1) + widen(carry) * dot3(cm, state[...])
    start_ref[0] = state[...]
    reach_ref[...] = reach[...]
    gain_ref[...] = jnp.broadcast_to(gain, gain_ref.shape)
    state[...] = gain * state[...] + dot3(bm.T, xdt * widen(tail))
    reach[...] = gain * reach[...]

    @pl.when(c == PIECES - 1)
    def _():
        packed_ref[0:N, :] = state[...]
        packed_ref[N:, :] = reach[...]


def joined_states(first, second, third):
    return first[:N] + first[N : N + 1] * (second[:N] + second[N : N + 1] * third[:N])


def output_kernel(
    y_part_ref,
    conv_ref,
    cum_ref,
    flags_ref,
    z_ref,
    d_gated_ref,
    reach_ref,
    first_ref,
    second_ref,
    third_ref,
    rows_ref,
    y_ref,
    sums_ref,
    arrived_ref,
):
    c = pl.program_id(0)

    @pl.when(c == 0)
    def _():
        arrived_ref[...] = joined_states(first_ref[...], second_ref[...], third_ref[...])

    conv = conv_ref[...]
    act = conv * jax.nn.sigmoid(conv)
    carry = widen(jnp.exp(cum_ref[...]) * flags_ref[:, KEEP : KEEP + 1]) * reach_ref[0:1, :]
    y = (
        y_part_ref[...]
        + carry * dot3(act[:, EG + N :], arrived_ref[...])
        + rows_ref[0:1, :] * act[:, :EG]
    )
    y_ref[...] = y
    _, silu_z = silu_parts(z_ref[...])
    g = y * silu_z
    squares = jnp.sum(g * g, axis=1, keepdims=True)
    inner = jnp.sum(d_gated_ref[...] * rows_ref[1:2, :] * g, axis=1, keepdims=True)
    lane = lane_of((CHUNK, LANES))
    turned = jnp.where(lane == 0, squares, jnp.where(lane == 1, inner, 0.0)).T
    sums_ref[pl.ds(c, 1), :] = turned[0:1, :]
    sums_ref[pl.ds(PIECES + c, 1), :] = turned[1:2, :]


def gate_kernel(
    y_ref,
    z_ref,
    d_gated_ref,
    conv_ref,
    cum_ref,
    flags_ref,
    gain_ref,
    sums_ref,
    rows_ref,
    gated_ref,
    dz_ref,
    dy_ref,
    end_ref,
    reach_ref,
    d_gate_ref,
    packed_ref,
    state,
    reach,
):
    c = PIECES - 1 - pl.program_id(0)

    @pl.when(c == PIECES - 1)
    def _():
        state[...] = jnp.zeros_like(state)
        reach[...] = jnp.ones_like(reach)
        d_gate_ref[...] = jnp.zeros_like(d_gate_ref)

    ti, _ = square_iota()
    turned = jnp.where(
        ti == 0,
        sums_ref[pl.ds(c, 1), :],
        jnp.where(ti == 1, sums_ref[pl.ds(PIECES + c, 1), :], 0.0),
    ).T
    root = lax.rsqrt(turned[:, 0:1] * (1.0 / E) + EPSILON)
    slope = turned[:, 1:2] * (root * root * root) * (1.0 / E)
    gate = rows_ref[1:2, :]
    y = y_ref[...]
    sig, silu_z = silu_parts(z_ref[...])
    g = y * silu_z
    unit = g * root
    gated_ref[...] = (unit * gate).astype(BF16)
    d_gated = d_gated_ref[...]
    d_gate_ref[0:1, :] += jnp.sum(d_gated * unit, axis=0, keepdims=True)
    d_g = root * (d_gated * gate) - g * slope
    dy = d_g * silu_z
    dz_ref[...] = (d_g * y * (sig + silu_z * (1.0 - sig))).astype(BF16)
    dy_ref[...] = dy
    conv = conv_ref[:, EG + N :]
    cm = conv * jax.nn.sigmoid(conv)
    carry = widen(jnp.exp(cum_ref[...]) * flags_ref[:, KEEP : KEEP + 1])
    end_ref[0] = state[...]
    reach_ref[...] = reach[...]
    gain = gain_ref[0:1, :]
    state[...] = gain * state[...] + dot3(cm.T, dy * carry)
    reach[...] = gain * reach[...]

    @pl.when(c == 0)
    def _():
        packed_ref[0:N, :] = state[...]
        packed_ref[N:, :] = reach[...]


def inner_kernel(dy_ref, conv_ref, dt_ref, cum_ref, flags_ref, ids_ref, u_ref, d_bc_ref):
    c = pl.program_id(0)
    flags = flags_ref[...]
    conv = conv_ref[...]
    act = conv * jax.nn.sigmoid(conv)
    xs, bm, cm = act[:, :EG], act[:, EG : EG + N], act[:, EG + N :]
    cum = cum_ref[...]
    cum_t = cum.T
    dy = dy_ref[...]
    xdt = xs * widen(dt_ref[...])
    scores_t = dot3(bm, cm, NT)
    ti, si = square_iota()
    same = same_document(flags, ids_ref[pl.ds(c, 1), :])
    mask = (ti >= si) & same
    mask_t = (ti <= si) & same
    d_scores = jnp.zeros((CHUNK, CHUNK), F32)
    u = []
    for p in range(HG // 2):
        own = stacked_pair(dy[:, pair_lanes(p)])
        pairs = dot3(own, xdt[:, pair_lanes(p)], NT)
        mix_t = []
        for k in range(2):
            h = 2 * p + k
            gap = cum[:, h : h + 1] - cum_t[h : h + 1, :]
            d_scores = d_scores + jnp.exp(jnp.where(mask, gap, -1e30)) * (
                pairs[k * CHUNK : (k + 1) * CHUNK]
            )
            mix_t.append(jnp.exp(jnp.where(mask_t, -gap, -1e30)) * scores_t)
        u.append(dot3(jnp.concatenate(mix_t, axis=1), own))
    u_ref[...] = jnp.concatenate(u, axis=1)
    d_bc_ref[:, :N] = dot3(d_scores.T, cm)
    d_bc_ref[:, N:] = dot3(d_scores, bm)


def backward_kernel(
    u_ref,
    d_bc_ref,
    dy_ref,
    y_ref,
    conv_ref,
    dt_ref,
    cum_ref,
    r_ref,
    flags_ref,
    start_ref,
    reach_ref,
    arrived_ref,
    end_ref,
    reach_back_ref,
    first_ref,
    second_ref,
    third_ref,
    final_ref,
    v_ref,
    before_ref,
    rows_ref,
    taps_ref,
    head_ref,
    summer_ref,
    edge_flags_ref,
    dv_ref,
    d_edge_ref,
    d_bc_t_ref,
    dr_ref,
    wide_ref,
    heads_ref,
    following,
    flowing,
    adjoint_in,
):
    c = PIECES - 1 - pl.program_id(0)
    summer = summer_ref[...]

    @pl.when(c == PIECES - 1)
    def _():
        adjoint = joined_states(first_ref[...], second_ref[...], third_ref[...])
        adjoint_in[...] = adjoint
        final = final_ref[0:N, :] + final_ref[N : N + 1, :] * arrived_ref[...]
        inner = jnp.sum(adjoint * final, axis=0, keepdims=True)
        flowing[...] = head_sums(jnp.broadcast_to(inner, (8, EG)), summer)
        following[...] = jnp.zeros_like(following)
        wide_ref[...] = jnp.zeros_like(wide_ref)
        heads_ref[...] = jnp.zeros_like(heads_ref)

    flags = flags_ref[...]
    conv = conv_ref[...]
    sig, act = silu_parts(conv)
    xs, bm = act[:, :EG], act[:, EG : EG + N]
    cum = cum_ref[...]
    dt = dt_ref[...]
    dy = dy_ref[...]
    skip = rows_ref[0:1, :]
    rate = head_ref[1:2, :]
    last = cum[CHUNK - 1 : CHUNK, :]
    tail = widen(jnp.exp(last - cum) * flags[:, TAIL : TAIL + 1])
    carry = widen(jnp.exp(cum) * flags[:, KEEP : KEEP + 1])
    dt_wide = widen(dt)
    start = start_ref[0] + reach_ref[0:1, :] * arrived_ref[...]
    adjoint = end_ref[0] + reach_back_ref[0:1, :] * adjoint_in[...]
    u = u_ref[...] + tail * dot3(bm, adjoint)
    d_xs = u * dt_wide + skip * dy
    d_dt = head_sums(xs * u, summer)
    d_bc_t_ref[0:N, :] = (d_bc_ref[:, :N] + dot3(xs * dt_wide * tail, adjoint, NT)).T
    d_bc_t_ref[N:, :] = (d_bc_ref[:, N:] + dot3(dy * carry, start, NT)).T
    flow = head_sums(dy * (y_ref[...] - skip * xs), summer) - dt * d_dt
    ti, si = square_iota()
    upper = (si >= ti).astype(F32)
    d_la = jnp.dot(upper, flow, precision=HIGHEST, preferred_element_type=F32) + flowing[0:1, :]
    flowing[...] = jnp.broadcast_to(d_la[0:1, :], flowing.shape)
    d_la = d_la * flags[:, 1:2]
    d_r = (d_dt - rate * d_la) * jax.nn.sigmoid(r_ref[...] + head_ref[0:1, :])
    dr_ref[...] = d_r
    heads_ref[0:1, :] += jnp.sum(d_r, axis=0, keepdims=True)
    heads_ref[1:2, :] += jnp.sum(d_la * (-rate * dt), axis=0, keepdims=True)
    heads_ref[2:3, :] += jnp.sum(head_sums(dy * xs, summer), axis=0, keepdims=True)

    sig, conv = sig[:, :EG], conv[:, :EG]
    d_conv = d_xs * (sig + conv * sig * (1.0 - sig))
    window = jnp.concatenate([before_ref[...], v_ref[...]], axis=0)
    ahead = jnp.concatenate([d_conv, following[...]], axis=0)
    wide_ref[0:1, :] += jnp.sum(d_conv * window[8:], axis=0, keepdims=True)
    wide_ref[TAPS : TAPS + 1, :] += jnp.sum(d_conv, axis=0, keepdims=True)
    dv = taps_ref[0:1, :EG] * d_conv
    for lag in range(1, TAPS):
        wide_ref[lag : lag + 1, :] += jnp.sum(
            d_conv * pltpu.roll(window, lag, 0)[8:] * flags[:, lag : lag + 1],
            axis=0,
            keepdims=True,
        )
        dv = dv + taps_ref[lag : lag + 1, :EG] * (
            pltpu.roll(ahead, CHUNK + 8 - lag, 0)[:CHUNK] * flags[:, AHEAD + lag : AHEAD + lag + 1]
        )
    dv_ref[...] = dv.astype(BF16)
    following[...] = d_conv[0:8]

    @pl.when(c == 0)
    def _():
        d_edge_ref[...] = edge_rows(d_conv[0:8], taps_ref[:, :EG], edge_flags_ref[...])


def edge_rows(d_conv, taps, flags):
    zero = jnp.zeros_like(d_conv)
    ahead = jnp.concatenate([zero, d_conv], axis=0)
    total = zero
    for lag in range(1, TAPS):
        total = total + taps[lag : lag + 1, :] * (
            pltpu.roll(ahead, EDGE - lag, 0)[0:8] * flags[:, AHEAD + lag : AHEAD + lag + 1]
        )
    return jnp.concatenate([zero, total], axis=0).astype(BF16)


def shared_kernel(
    team_ref,
    got_ref,
    conv_b_ref,
    conv_c_ref,
    v_b_ref,
    v_c_ref,
    before_b_ref,
    before_c_ref,
    dr_ref,
    dv_ref,
    d_edge_ref,
    flags_ref,
    edge_flags_ref,
    taps_ref,
    late_ref,
    wide_ref,
    following,
):
    step = pl.program_id(0)
    turn = (2 * N - BG * team_ref[0]) % (2 * N)

    def own(b_ref, c_ref):
        both = jnp.concatenate([b_ref[...], c_ref[...]], axis=1)
        return pltpu.roll(both, turn, 1)[:, :LANES]

    @pl.when(step == 0)
    def _():
        following[...] = jnp.zeros_like(following)
        wide_ref[...] = jnp.zeros_like(wide_ref)

    @pl.when(step < PIECES)
    def _():
        flags = flags_ref[...]
        total = got_ref[0]
        for g in range(1, G):
            total = total + got_ref[g]
        d_act = jnp.concatenate([total, jnp.zeros((LANES - BG, CHUNK), F32)], axis=0).T
        conv = own(conv_b_ref, conv_c_ref)
        sig = jax.nn.sigmoid(conv)
        d_conv = d_act * (sig + conv * sig * (1.0 - sig))
        window = jnp.concatenate(
            [own(before_b_ref, before_c_ref), own(v_b_ref, v_c_ref)], axis=0
        )
        ahead = jnp.concatenate([d_conv, following[...]], axis=0)
        wide_ref[0:1, :] += jnp.sum(d_conv * window[8:], axis=0, keepdims=True)
        wide_ref[TAPS : TAPS + 1, :] += jnp.sum(d_conv, axis=0, keepdims=True)
        dv = taps_ref[0:1, :] * d_conv
        for lag in range(1, TAPS):
            wide_ref[lag : lag + 1, :] += jnp.sum(
                d_conv * pltpu.roll(window, lag, 0)[8:] * flags[:, lag : lag + 1],
                axis=0,
                keepdims=True,
            )
            dv = dv + taps_ref[lag : lag + 1, :] * (
                pltpu.roll(ahead, CHUNK + 8 - lag, 0)[:CHUNK]
                * flags[:, AHEAD + lag : AHEAD + lag + 1]
            )
        following[...] = d_conv[0:8]
        late_ref[:, :EG] = dv_ref[...]
        late_ref[:, EG:] = (dv + pltpu.roll(dr_ref[...], BG, 1)).astype(BF16)

    @pl.when(step == PIECES)
    def _():
        late_ref[0:EDGE, :EG] = d_edge_ref[...]
        late_ref[0:EDGE, EG:] = edge_rows(following[...], taps_ref[...], edge_flags_ref[...])


def triangle(n):
    return [(i, j) for i in range(n // TILE) for j in range(i, n // TILE)]


def gram_kernel(which_ref, x_ref, out_ref):
    n = x_ref.shape[1]
    count = n // TILE
    order = triangle(n)

    @pl.when(pl.program_id(0) == 0)
    def _():
        out_ref[...] = jnp.zeros_like(out_ref)

    def add(columns):
        for i in range(count):

            def taken(at):
                return jnp.concatenate([x_ref[0, at, columns], x_ref[1, at, columns]], axis=1)

            product = dot(
                taken(pl.ds(i * TILE, TILE)), taken(pl.ds(i * TILE, n - i * TILE)), NT
            )
            for j in range(i, count):
                out_ref[order.index((i, j))] += product[:, (j - i) * TILE : (j - i + 1) * TILE]

    @pl.when(which_ref[0] == 1)
    def _():
        add(slice(0, IN_COLS))

    @pl.when(which_ref[0] == 0)
    def _():
        add(slice(IN_COLS, BLOCK))


def chain_kernel(own_ref, got_ref, pick_ref, t_ref, high, low, h_high, h_low, q_ref):
    n = high.shape[0]
    count = n // TILE
    order = triangle(n)

    def at(i):
        return pl.ds(i * TILE, TILE) if isinstance(i, int) else pl.ds(pl.multiple_of(i * TILE, TILE), TILE)

    def times(a, b):
        return jnp.dot(a, b, preferred_element_type=F32)

    diagonal = lax.broadcasted_iota(jnp.int32, (TILE, TILE), 0) == lax.broadcasted_iota(jnp.int32, (TILE, TILE), 1)
    square = jnp.zeros((1, 1), F32)
    for b, (i, j) in enumerate(order):
        if i == j:
            square = square + jnp.sum(jnp.where(diagonal, own_ref[b] + got_ref[b], 0.0), keepdims=True)
    inverse = 1.0 / (jnp.sqrt(square) + NORM_FLOOR)
    scale = inverse * inverse

    def put(value, i, j, top_ref, rest_ref):
        top = value.astype(BF16)
        top_ref[at(i), at(j)] = top
        if i != j:
            top_ref[at(j), at(i)] = top.T
        if rest_ref is not None:
            rest_ref[at(i), at(j)] = (value - top.astype(F32)).astype(BF16)

    def put_row(value, i, top_ref, rest_ref):
        for j in range(i, count):
            put(value[:, (j - i) * TILE : (j - i + 1) * TILE], i, j, top_ref, rest_ref)

    for b, (i, j) in enumerate(order):
        put((own_ref[b] + got_ref[b]) * scale, i, j, high, low)

    def polynomial(q):
        for i in range(count):
            rest = pl.ds(i * TILE, n - i * TILE)
            value = times(high[at(i), :], high[:, rest])
            put_row(POLY_SECOND * high[at(i), rest].astype(F32) + POLY_THIRD * value, i, q, None)

    def whole(top_ref, rest_ref, i, rest):
        return top_ref[at(i), rest].astype(F32) + rest_ref[at(i), rest].astype(F32)

    def iterate(step, _):
        q = q_ref.at[step]
        polynomial(q)
        for i in range(count):
            rest = pl.ds(i * TILE, n - i * TILE)
            value = times(q[at(i), :], high[:, rest]) + POLY_FIRST * whole(high, low, i, rest)
            put_row(value, i, h_high, h_low)
        for i in range(count):
            rest = pl.ds(i * TILE, n - i * TILE)
            value = times(h_high[at(i), :], q[:, rest]) + POLY_FIRST * whole(h_high, h_low, i, rest)
            put_row(value, i, high, low)
        return 0

    def thin(t, matrix):
        top, rest = parts(t)
        both = times(jnp.concatenate([top, rest], axis=0), matrix)
        return both[: t.shape[0]] + both[t.shape[0] :]

    def multiplied(t, step):
        return POLY_FIRST * t + thin(t, q_ref[step])

    def last_gram(t):
        return multiplied(thin(multiplied(t, NS_STEPS - 2), high[...]), NS_STEPS - 2)

    lax.fori_loop(0, NS_STEPS - 2, iterate, 0)
    polynomial(q_ref.at[NS_STEPS - 2])
    pick = pick_ref[...]
    once = last_gram(pick)
    t = POLY_FIRST * pick + POLY_SECOND * once + POLY_THIRD * last_gram(once)
    for step in reversed(range(NS_STEPS - 1)):
        t = multiplied(t, step)
    t_ref[...] = t * inverse


VMEM = pltpu.CompilerParams(vmem_limit_bytes=60 << 20)


def spec(shape, index=None):
    return pl.BlockSpec(shape, index if index is not None else (lambda c: (0,) * len(shape)))


def rows(width, height=CHUNK):
    return spec((height, width), lambda c: (c, 0))


def rows_back(width, height=CHUNK):
    return spec((height, width), lambda c: (PIECES - 1 - c, 0))


def previous(c):
    return jnp.where(c == 0, (TOKENS + EDGE) // 8 - 1, c * (CHUNK // 8) - 1)


def shaped(*shape, dtype=F32):
    return jax.ShapeDtypeStruct(shape, dtype)


def cost(flops, moved):
    return pl.CostEstimate(flops=flops, bytes_accessed=moved, transcendentals=0)


def piece_of(kind):
    size = 4

    def index(c, place):
        return ((place[0] - jnp.minimum(c, size - 1) + size) % size, 0, 0)

    return pl.BlockSpec((1, CHUNK, D), index)


def project(place, own, other, edge, weights, gain):
    total = TOKENS + EDGE
    block = 2 * CHUNK

    def out(width):
        return pl.BlockSpec((block, width), lambda c, place: (c, 0))

    def whole(*shape):
        return pl.BlockSpec(shape, lambda c, place: (0, 0))

    return pl.pallas_call(
        project_kernel,
        grid_spec=pltpu.PrefetchScalarGridSpec(
            num_scalar_prefetch=1,
            grid=(TOKENS // block + 1,),
            in_specs=[
                piece_of("own"),
                piece_of("other"),
                whole(EDGE, D),
                whole(D, FORWARD_COLS),
                whole(1, D),
            ],
            out_specs=[out(D), out(EG), out(VG), out(LANES)],
        ),
        out_shape=[
            shaped(total, D, dtype=BF16),
            shaped(total, EG),
            shaped(total, VG),
            shaped(total, LANES),
        ],
        compiler_params=VMEM,
        cost_estimate=cost(2 * total * D * FORWARD_COLS, 16 << 20),
        name="project",
    )(place, own, other, edge, weights, gain)


def incoming(place, own, other, weights):
    block = 2 * CHUNK

    def out(width):
        return pl.BlockSpec((block, width), lambda c, place: (c, 0))

    return pl.pallas_call(
        incoming_kernel,
        grid_spec=pltpu.PrefetchScalarGridSpec(
            num_scalar_prefetch=1,
            grid=(TOKENS // block,),
            in_specs=[
                piece_of("own"),
                piece_of("other"),
                pl.BlockSpec((D, EG), lambda c, place: (0, FORWARD_COLS // EG)),
            ],
            out_specs=[out(D), out(EG)],
        ),
        out_shape=[shaped(TOKENS, D, dtype=BF16), shaped(TOKENS, EG)],
        compiler_params=VMEM,
        cost_estimate=cost(2 * TOKENS * D * EG, 9 << 20),
        name="incoming",
    )(place, own, other, weights)


def early_products(normed, q, dz, gated):
    return pl.pallas_call(
        early_kernel,
        grid=(D // TILE,),
        in_specs=[
            spec((TOKENS + EDGE, TILE), lambda c: (0, c)),
            spec((TOKENS, TILE), lambda c: (0, c)),
            spec((TOKENS, EG)),
            spec((TOKENS, EG)),
        ],
        out_specs=rows(2 * EG, TILE),
        out_shape=shaped(D, 2 * EG),
        compiler_params=VMEM,
        cost_estimate=cost(4 * TOKENS * D * EG, 13 << 20),
        name="early",
    )(normed, q, dz, gated)


def forward(v, r, flags, ids, taps, head):
    return pl.pallas_call(
        forward_kernel,
        grid=(PIECES,),
        in_specs=[
            rows(VG),
            spec((8, VG), lambda c: (previous(c), 0)),
            rows(LANES),
            rows(LANES),
            spec((8, LANES)),
            spec((8, VG)),
            spec((8, LANES)),
        ],
        out_specs=[
            rows(VG),
            rows(LANES),
            rows(LANES),
            rows(EG),
            spec((1, N, EG), lambda c: (c, 0, 0)),
            rows(EG, 8),
            rows(EG, 8),
            spec((STATE_ROWS, EG)),
        ],
        out_shape=[
            shaped(TOKENS, VG),
            shaped(TOKENS, LANES),
            shaped(TOKENS, LANES),
            shaped(TOKENS, EG),
            shaped(PIECES, N, EG),
            shaped(PIECES * 8, EG),
            shaped(PIECES * 8, EG),
            shaped(STATE_ROWS, EG),
        ],
        scratch_shapes=[pltpu.VMEM((N, EG), F32), pltpu.VMEM((8, EG), F32)],
        compiler_params=VMEM,
        cost_estimate=cost(3 << 30, 14 << 20),
        name="forward",
    )(v, v, r, flags, ids, taps, head)


def outputs(y_part, conv, cum, flags, z, d_gated, reach, arrivals, wide):
    return pl.pallas_call(
        output_kernel,
        grid=(PIECES,),
        in_specs=[rows(EG), rows(VG), rows(LANES), rows(LANES), rows(EG), rows(EG), rows(EG, 8)]
        + [spec((STATE_ROWS, EG))] * 3
        + [spec((8, EG))],
        out_specs=[rows(EG), spec((2 * PIECES, LANES)), spec((N, EG))],
        out_shape=[shaped(TOKENS, EG), shaped(2 * PIECES, LANES), shaped(N, EG)],
        compiler_params=VMEM,
        cost_estimate=cost(1 << 28, 12 << 20),
        name="outputs",
    )(y_part, conv, cum, flags, z, d_gated, reach, *arrivals, wide)


def gate(y, z, d_gated, conv, cum, flags, gain, sums, wide):
    return pl.pallas_call(
        gate_kernel,
        grid=(PIECES,),
        in_specs=[rows_back(EG)] * 3
        + [rows_back(VG), rows_back(LANES), rows_back(LANES), rows_back(EG, 8)]
        + [spec((2 * PIECES, LANES)), spec((8, EG))],
        out_specs=[rows_back(EG)] * 3
        + [
            spec((1, N, EG), lambda c: (PIECES - 1 - c, 0, 0)),
            rows_back(EG, 8),
            spec((8, EG)),
            spec((STATE_ROWS, EG)),
        ],
        out_shape=[
            shaped(TOKENS, EG, dtype=BF16),
            shaped(TOKENS, EG, dtype=BF16),
            shaped(TOKENS, EG),
            shaped(PIECES, N, EG),
            shaped(PIECES * 8, EG),
            shaped(8, EG),
            shaped(STATE_ROWS, EG),
        ],
        scratch_shapes=[pltpu.VMEM((N, EG), F32), pltpu.VMEM((8, EG), F32)],
        compiler_params=VMEM,
        cost_estimate=cost(1 << 28, 14 << 20),
        name="gate",
    )(y, z, d_gated, conv, cum, flags, gain, sums, wide)


def inner(dy, conv, dt, cum, flags, ids):
    return pl.pallas_call(
        inner_kernel,
        grid=(PIECES,),
        in_specs=[rows(EG), rows(VG), rows(LANES), rows(LANES), rows(LANES), spec((8, LANES))],
        out_specs=[rows(EG), rows(2 * N)],
        out_shape=[shaped(TOKENS, EG), shaped(TOKENS, 2 * N)],
        compiler_params=VMEM,
        cost_estimate=cost(3 << 30, 9 << 20),
        name="inner",
    )(dy, conv, dt, cum, flags, ids)


def backward(
    u, d_bc, dy, y, conv, dt, cum, r, flags, starts, reach, arrived, ends, reach_back, arrivals,
    final, v, wide, taps, head, summer, edge_flags,
):
    def back_state():
        return spec((1, N, EG), lambda c: (PIECES - 1 - c, 0, 0))

    return pl.pallas_call(
        backward_kernel,
        grid=(PIECES,),
        in_specs=[
            rows_back(EG),
            rows_back(2 * N),
            rows_back(EG),
            rows_back(EG),
            rows_back(VG),
            rows_back(LANES),
            rows_back(LANES),
            rows_back(LANES),
            rows_back(LANES),
            back_state(),
            rows_back(EG, 8),
            spec((N, EG)),
            back_state(),
            rows_back(EG, 8),
        ]
        + [spec((STATE_ROWS, EG))] * 4
        + [
            rows_back(EG),
            spec((8, EG), lambda c: (previous(PIECES - 1 - c), 0)),
            spec((8, EG)),
            spec((8, VG)),
            spec((8, LANES)),
            spec((EG, LANES)),
            spec((8, LANES)),
        ],
        out_specs=[
            rows_back(EG),
            spec((EDGE, EG)),
            spec((2 * N, CHUNK), lambda c: (0, PIECES - 1 - c)),
            rows_back(LANES),
            spec((8, EG)),
            spec((8, LANES)),
        ],
        out_shape=[
            shaped(TOKENS, EG, dtype=BF16),
            shaped(EDGE, EG, dtype=BF16),
            shaped(2 * N, TOKENS),
            shaped(TOKENS, LANES),
            shaped(8, EG),
            shaped(8, LANES),
        ],
        scratch_shapes=[
            pltpu.VMEM((8, EG), F32),
            pltpu.VMEM((8, LANES), F32),
            pltpu.VMEM((N, EG), F32),
        ],
        compiler_params=VMEM,
        cost_estimate=cost(3 << 29, 20 << 20),
        name="backward",
    )(
        u, d_bc, dy, y, conv, dt, cum, r, flags, starts, reach, arrived, ends, reach_back,
        *arrivals, final, v, v, wide, taps, head, summer, edge_flags,
    )


def shared(team, got, conv, v, dr, dv, d_edge, flags, edge_flags, taps):
    def turned(step):
        return jnp.maximum(PIECES - 1 - step, 0)

    def lanes_of(block):
        return spec((CHUNK, LANES), lambda c: (turned(c), block))

    def before(block):
        return spec((8, LANES), lambda c: (previous(turned(c)), block))

    b, c_block = EG // LANES, EG // LANES + 1
    return pl.pallas_call(
        shared_kernel,
        grid=(PIECES + 1,),
        in_specs=[
            pl.BlockSpec(memory_space=pltpu.SMEM),
            spec((G, BG, CHUNK), lambda c: (0, 0, turned(c))),
            lanes_of(b),
            lanes_of(c_block),
            lanes_of(b),
            lanes_of(c_block),
            before(b),
            before(c_block),
            lanes_of(0),
            spec((CHUNK, EG), lambda c: (turned(c), 0)),
            spec((EDGE, EG)),
            lanes_of(0),
            spec((8, LANES)),
            spec((8, LANES)),
        ],
        out_specs=[
            spec((CHUNK, LATE_COLS), lambda c: (jnp.where(c == PIECES, PIECES, turned(c)), 0)),
            spec((8, LANES)),
        ],
        out_shape=[shaped(TOKENS + EDGE, LATE_COLS, dtype=BF16), shaped(8, LANES)],
        scratch_shapes=[pltpu.VMEM((8, LANES), F32)],
        compiler_params=VMEM,
        cost_estimate=cost(1 << 27, 6 << 20),
        name="shared",
    )(team, got, conv, conv, v, v, v, v, dr, dv, d_edge, flags, edge_flags, taps)


def gram(which, x):
    n = x.shape[1]
    blocks = len(triangle(n))
    return pl.pallas_call(
        gram_kernel,
        grid=(x.shape[0] // 2,),
        in_specs=[
            pl.BlockSpec(memory_space=pltpu.SMEM),
            spec((2,) + x.shape[1:], lambda y: (y, 0, 0)),
        ],
        out_specs=spec((blocks, TILE, TILE)),
        out_shape=shaped(blocks, TILE, TILE),
        compiler_params=VMEM,
        cost_estimate=cost(n * n * x.shape[0] * x.shape[2] * 3 // 5, 22 << 20),
        name="gram",
    )(which.astype(jnp.int32).reshape(1), x)


def chain(own, got, pick):
    n = pick.shape[1]
    whole = pl.BlockSpec(memory_space=pltpu.VMEM)
    return pl.pallas_call(
        chain_kernel,
        out_shape=jax.ShapeDtypeStruct(pick.shape, F32),
        in_specs=[whole, whole, whole],
        out_specs=whole,
        scratch_shapes=[pltpu.VMEM((n, n), BF16)] * 4 + [pltpu.VMEM((NS_STEPS - 1, n, n), BF16)],
        compiler_params=pltpu.CompilerParams(vmem_limit_bytes=62 << 20),
        cost_estimate=cost(14 * n * n * n, 11 << 20),
        name="chain",
    )(own, got, pick)


def summaries(packed, direction):
    size = lax.axis_size("x")
    return [
        lax.ppermute(
            packed,
            "x",
            [(s, s + direction * k) for s in range(size) if 0 <= s + direction * k < size],
        )
        for k in range(1, size)
    ]


def blocks_of_columns(in_rows, out_rows):
    count = in_rows.shape[0]
    kind = in_rows.dtype
    z = in_rows[:, :E].reshape(count, G, EG)
    xs = in_rows[:, E : 2 * E].reshape(count, G, EG)
    bc = in_rows[:, 2 * E : 2 * E + 2 * N].reshape(count, G, BG)
    r = in_rows[:, 2 * E + 2 * N :].reshape(count, G, HG)
    fill = jnp.zeros((count, G, LANES - BG - HG), kind)
    out = out_rows.reshape(count, G, EG)
    return jnp.concatenate([z, xs, bc, r, fill, out], axis=2).transpose(1, 0, 2)


def rows_of_blocks(blocks):
    count = blocks.shape[1]
    b = blocks.transpose(1, 0, 2)
    pieces = [
        b[:, :, :EG].reshape(count, E),
        b[:, :, EG : 2 * EG].reshape(count, E),
        b[:, :, 2 * EG : 2 * EG + BG].reshape(count, 2 * N),
        b[:, :, 2 * EG + BG : 2 * EG + BG + HG].reshape(count, H),
    ]
    return jnp.concatenate(pieces, axis=1), b[:, :, IN_COLS:].reshape(count, E)


def along_y(own):
    size = lax.axis_size("y")
    return [own] + [
        lax.ppermute(own, "y", [(s, (s + k) % size) for s in range(size)]) for k in range(1, size)
    ]


def team_sum(values):
    values = values + lax.ppermute(values, "c", [(0, 1), (1, 0)])
    return sum(along_y(values))


def after(value, *others):
    return lax.optimization_barrier((value,) + others)[0]


def local(
    hidden,
    segments,
    norm_gain,
    in_weight,
    conv_weight,
    conv_bias,
    dt_bias,
    a_log,
    skip_scale,
    gate_gain,
    out_weight,
    cotangent,
    in_momentum,
    out_momentum,
    vector_momentum,
):
    zi, xi, yi, ci = (lax.axis_index(a) for a in EVERY)
    team = yi * 2 + ci
    count = in_weight.shape[0]
    team_count = G * count
    swap = [(0, 1), (1, 0)]
    first = ci == 0

    def mine(values, width, start=0, axis=-1):
        return lax.dynamic_slice_in_dim(values, start + team * width, width, axis % values.ndim)

    z_w = in_weight[:, :E].reshape(count, G, EG)
    xs_w = in_weight[:, E : 2 * E].reshape(count, G, EG)
    bc_w = jnp.broadcast_to(in_weight[:, None, 2 * E : 2 * E + 2 * N], (count, G, 2 * N))
    r_w = jnp.pad(
        in_weight[:, 2 * E + 2 * N :].reshape(count, G, HG), ((0, 0), (0, 0), (0, LANES - HG))
    )
    out_w = out_weight.reshape(count, G, EG)
    sent = jnp.concatenate([z_w, xs_w, bc_w, r_w, out_w], axis=2).transpose(1, 0, 2)
    got = lax.all_to_all(sent, TEAM, 0, 0, tiled=True).reshape(team_count, -1)
    weights = lax.all_gather(got, ROWS, axis=0, tiled=True)

    numbers = jnp.pad(segments.astype(BF16)[:, None], ((0, 0), (0, LANES - 1)))
    pieces = along_y(jnp.concatenate([hidden, numbers], axis=1))
    momentum_block = lax.all_to_all(
        blocks_of_columns(
            *(after(m, got).astype(BF16) for m in (in_momentum, out_momentum))
        ),
        TEAM,
        0,
        0,
        tiled=True,
    ).reshape(team_count, BLOCK)
    conv_all = jnp.concatenate([conv_weight, conv_bias[None, :]], axis=0)
    taps = jnp.pad(
        jnp.concatenate([mine(conv_all[:, :E], EG), conv_all[:, E:]], axis=1),
        ((0, 8 - TAPS - 1), (0, 0)),
    )
    taps_shared = jnp.pad(mine(conv_all[:, E:], BG), ((0, 8 - TAPS - 1), (0, LANES - BG)))
    head = jnp.pad(
        jnp.stack([mine(dt_bias, HG), jnp.exp(mine(a_log, HG))]), ((0, 6), (0, LANES - HG))
    )
    wide = jnp.pad(
        jnp.stack([jnp.repeat(mine(skip_scale, HG), HEAD), mine(gate_gain, EG)]), ((0, 6), (0, 0))
    )
    summer = (
        lax.broadcasted_iota(jnp.int32, (EG, LANES), 0) // HEAD
        == lax.broadcasted_iota(jnp.int32, (EG, LANES), 1)
    ).astype(BF16)
    pieces, momentum_block, taps, taps_shared, head, wide, summer = lax.optimization_barrier(
        (pieces, momentum_block, taps, taps_shared, head, wide, summer)
    )
    own_rows = jnp.stack(pieces)
    other_rows = lax.ppermute(own_rows, "c", swap)
    q_own = jnp.stack(along_y(after(cotangent, own_rows)))
    q_other = lax.ppermute(q_own, "c", swap)
    place = jnp.stack([yi, ci]).astype(jnp.int32)
    size_x, size_y = lax.axis_size("x"), lax.axis_size("y")
    end_rows = lax.dynamic_index_in_dim(
        jnp.where(first, other_rows[:, CHUNK - EDGE :], own_rows[:, CHUNK - EDGE :]),
        (yi + 1) % size_y,
        0,
        False,
    )
    edge_rows_in = lax.ppermute(end_rows, "x", [(s, s + 1) for s in range(size_x - 1)])
    by_distance = jnp.stack([own_rows[:, :, D], other_rows[:, :, D]]).astype(F32)
    by_core = jnp.where(first, by_distance, by_distance[::-1])
    team_ids = by_core[:, (yi - jnp.arange(size_y)) % size_y].transpose(1, 0, 2).reshape(-1)
    next_ids = lax.ppermute(team_ids[:LANES], "x", [(s, s - 1) for s in range(1, size_x)])
    ids = jnp.concatenate(
        [
            jnp.where(xi == 0, -1.0, edge_rows_in[EDGE - 8 :, D].astype(F32)),
            team_ids,
            jnp.where(xi == size_x - 1, -1.0, next_ids[:8]),
        ]
    )

    def flag_lanes(at, size):
        own = ids[at : at + size]
        same = [(ids[at - k : at - k + size] == own).astype(F32) for k in range(TAPS)]
        ahead = [(ids[at + k : at + k + size] == own).astype(F32) for k in range(TAPS)]
        return own, same + ahead

    own_ids, lanes = flag_lanes(8, TOKENS)
    by_piece = own_ids.reshape(PIECES, CHUNK)
    before = ids[7 : 7 + TOKENS].reshape(PIECES, CHUNK)[:, :1]
    last = by_piece[:, CHUNK - 1 :]
    lanes = lanes + [
        jnp.zeros((TOKENS,), F32),
        (by_piece == before).astype(F32).reshape(-1),
        (by_piece == last).astype(F32).reshape(-1),
        jnp.broadcast_to((last == before).astype(F32), (PIECES, CHUNK)).reshape(-1),
        own_ids,
    ]
    flags = jnp.pad(jnp.stack(lanes, axis=1), ((0, 0), (0, LANES - len(lanes))))
    edge_ids = jnp.pad(ids, (8, 0), constant_values=-1.0)[: 8 + 16]
    edge_own = edge_ids[8:16]
    edge_flags = jnp.pad(
        jnp.stack(
            [jnp.zeros((8,), F32)] * AHEAD
            + [(edge_ids[8 + k : 16 + k] == edge_own).astype(F32) for k in range(TAPS)],
            axis=1,
        ),
        ((0, 0), (0, LANES - AHEAD - TAPS)),
    )

    normed, z, v, r = project(
        place, own_rows, other_rows, edge_rows_in, weights, norm_gain[None, :]
    )
    conv, dt, cum, y_part, starts, reach, gain, packed = forward(v, r, flags, by_piece, taps, head)
    arrivals = summaries(packed, 1)
    q_team, d_gated = incoming(place, q_own, q_other, weights)
    y, sums, arrived = outputs(y_part, conv, cum, flags, z, d_gated, reach, arrivals, wide)
    sums = team_sum(sums)
    gated, dz, dy, ends, reach_back, d_gate, packed_back = gate(
        y, z, d_gated, conv, cum, flags, gain, sums, wide
    )
    arrivals_back = summaries(packed_back, -1)
    early = early_products(normed, q_team, dz, gated)
    early_sum = lax.psum_scatter(early, ROWS, scatter_dimension=0, tiled=True)

    u, d_bc = inner(dy, conv, dt, cum, flags, by_piece)
    dv, d_edge, d_bc_t, dr, wide_sums, head_sums_out = backward(
        u, d_bc, dy, y, conv, dt, cum, r, flags, starts, reach, arrived, ends, reach_back,
        arrivals_back, packed, v, wide, taps, head, summer, edge_flags,
    )
    d_bc_got = lax.all_to_all(d_bc_t.reshape(G, BG, TOKENS), TEAM, 0, 0, tiled=True)
    late, shared_sums = shared(
        team.reshape(1), d_bc_got, conv, v, dr, dv, d_edge, flags, edge_flags, taps_shared
    )
    late_partial = dot(normed, late, TN).astype(BF16)
    late_parts = lax.all_to_all(
        late_partial.reshape(16, team_count, LATE_COLS), ROWS, 0, 0, tiled=True
    )
    late_sum = jnp.sum(late_parts.astype(F32), axis=0)

    sums_block = jnp.concatenate([early_sum[:, :EG], late_sum, early_sum[:, EG:]], axis=1)
    momenta = MATRIX_MOMENTUM * momentum_block.astype(F32) + sums_block
    x_all = lax.all_gather(momenta.astype(BF16), ("y", "z", "x")).reshape(4, D, BLOCK)

    late_back = lax.ppermute(
        late[TOKENS:], "x", [(s, s - 1) for s in range(1, lax.axis_size("x"))]
    )
    late, late_back, dz, gated, late_sum = lax.optimization_barrier(
        (late, late_back, dz, gated, late_sum)
    )
    d_projected = jnp.concatenate(
        [
            dz,
            jnp.concatenate(
                [late[: TOKENS - EDGE], late[TOKENS - EDGE : TOKENS] + late_back], axis=0
            ),
        ],
        axis=1,
    )
    w_own = jnp.concatenate(
        [
            weights[:, : 2 * EG],
            mine(weights[:, 2 * EG : 2 * EG + 2 * N], BG),
            weights[:, 2 * EG + 2 * N : 2 * EG + 2 * N + HG],
            jnp.zeros((D, LANES - BG - HG), BF16),
        ],
        axis=1,
    )
    d_normed_part = dot(d_projected, w_own, NT)
    d_norm_gain = jnp.sum(d_normed_part * normed[:TOKENS].astype(F32), axis=0) / norm_gain
    mixed_part = dot(gated, weights[:, FORWARD_COLS:], NT)

    vector = jnp.concatenate(
        [
            d_norm_gain,
            jnp.concatenate(
                [wide_sums[: TAPS + 1], shared_sums[: TAPS + 1, :BG]], axis=1
            ).reshape(-1),
            d_gate[0],
            head_sums_out[:3, :HG].reshape(-1),
        ]
    )
    vector = jnp.pad(vector, (0, -vector.shape[0] % 1024)).reshape(-1, LANES)
    vector = jnp.sum(lax.all_gather(vector, ROWS), axis=0)
    vector = lax.all_gather(vector, TEAM).reshape(G, -1)
    own = EG + BG
    grad_gain = jnp.sum(vector[:, :D], axis=0)
    conv_parts = vector[:, D : D + (TAPS + 1) * own].reshape(G, TAPS + 1, own).transpose(1, 0, 2)
    conv_parts = jnp.concatenate(
        [
            conv_parts[:, :, :EG].reshape(TAPS + 1, E),
            conv_parts[:, :, EG:].reshape(TAPS + 1, 2 * N),
        ],
        axis=1,
    )
    rest = vector[:, D + (TAPS + 1) * own :]
    heads = rest[:, EG : EG + 3 * HG].reshape(G, 3, HG).transpose(1, 0, 2).reshape(-1)
    vector_grad = jnp.concatenate(
        [grad_gain, conv_parts.reshape(-1), heads, rest[:, :EG].reshape(-1)]
    )
    vector_old = jnp.concatenate(
        [norm_gain, conv_weight.reshape(-1), conv_bias, dt_bias, a_log, skip_scale, gate_gain]
    )
    vector_momentum_new = VECTOR_MOMENTUM * vector_momentum + (1.0 - VECTOR_MOMENTUM) * vector_grad
    vector_new = vector_old - VECTOR_RATE * vector_momentum_new
    grad_rows = lax.all_to_all(
        sums_block.reshape(G, count, BLOCK), TEAM, 0, 0, tiled=True
    )
    in_grad, out_grad = rows_of_blocks(grad_rows)
    in_momentum_new = MATRIX_MOMENTUM * in_momentum + in_grad
    out_momentum_new = MATRIX_MOMENTUM * out_momentum + out_grad

    x_all, d_normed_part, mixed_part, vector_grad, in_grad = lax.optimization_barrier(
        (x_all, d_normed_part, mixed_part, vector_grad, in_grad)
    )
    gram_sent = gram(ci == 1, x_all)
    gram_got = lax.ppermute(gram_sent, "c", swap)
    gram_own = gram(first, after(x_all, gram_sent))
    chip_row = (zi * 4 + xi) * team_count + yi * (2 * count)
    pick = (
        lax.broadcasted_iota(jnp.int32, (2 * count, D), 1)
        == lax.broadcasted_iota(jnp.int32, (2 * count, D), 0) + chip_row
    ).astype(F32)
    t_own = chain(gram_own, gram_got, pick)
    d_normed = lax.psum_scatter(d_normed_part, TEAM, scatter_dimension=0, tiled=True)
    mixed = lax.psum_scatter(mixed_part, TEAM, scatter_dimension=0, tiled=True)
    hidden_own = hidden.astype(F32)
    block_output = (hidden_own + mixed).astype(BF16)
    scale_own = lax.rsqrt(jnp.mean(hidden_own * hidden_own, axis=-1, keepdims=True) + EPSILON)
    unit_own = hidden_own * scale_own
    d_unit = d_normed * norm_gain
    d_hidden = scale_own * (
        d_unit - unit_own * jnp.mean(d_unit * unit_own, axis=-1, keepdims=True)
    )
    input_grad = cotangent.astype(F32) + d_hidden

    t_other = lax.ppermute(t_own, "c", swap)
    t_in = jnp.where(first, t_own, t_other)
    t_out = jnp.where(first, t_other, t_own)

    def applied(t, x):
        both = jnp.einsum(
            "rk,ykn->yrn", jnp.concatenate(parts(t), axis=0), x, preferred_element_type=F32
        )
        return both[:, : 2 * count] + both[:, 2 * count :]

    halves = jnp.concatenate(
        [applied(t_in, x_all[:, :, :IN_COLS]), applied(t_out, x_all[:, :, IN_COLS:])], axis=2
    )
    half_own = lax.dynamic_slice_in_dim(halves, ci * count, count, 1)
    half_sent = lax.dynamic_slice_in_dim(halves, (1 - ci) * count, count, 1)
    half_got = lax.ppermute(half_sent, "c", swap)
    both = jnp.stack(
        [jnp.where(first, half_own, half_got), jnp.where(first, half_got, half_own)], axis=1
    ).reshape(G, count, BLOCK)
    step_in, step_out = rows_of_blocks(both)
    in_weight_new = in_weight.astype(F32) - MATRIX_RATE * math.sqrt(PROJ / D) * step_in
    out_weight_new = out_weight.astype(F32) - MATRIX_RATE * math.sqrt(E / D) * step_out
    return (
        block_output,
        input_grad,
        in_grad,
        in_momentum_new,
        in_weight_new,
        out_grad,
        out_momentum_new,
        out_weight_new,
        vector_grad,
        vector_momentum_new,
        vector_new,
    )


def solution(mesh):
    grid = Mesh(mesh.devices.reshape(4, 4, 4, 2), EVERY)
    split = P(EVERY, None)
    return jax.shard_map(
        local,
        mesh=grid,
        in_specs=(
            split,
            P(EVERY),
            P(),
            split,
            P(),
            P(),
            P(),
            P(),
            P(),
            P(),
            split,
            split,
            split,
            split,
            P(),
        ),
        out_specs=(split,) * 8 + (P(),) * 3,
        check_vma=False,
    )
```

```python
import math

import jax
import jax.numpy as jnp
from jax import lax
from jax.experimental import pallas as pl
from jax.experimental.pallas import tpu as pltpu
from jax.sharding import Mesh, PartitionSpec as P

NS_STEPS = 5
EPSILON = 1e-05
NORM_FLOOR = 1e-07
POLY_FIRST = 3.4445
POLY_SECOND = -4.775
POLY_THIRD = 2.0315
MATRIX_MOMENTUM = 0.95
MATRIX_RATE = 0.5
VECTOR_MOMENTUM = 0.9
VECTOR_RATE = 0.05
HIGHEST = lax.Precision.HIGHEST
F32 = jnp.float32
BF16 = jnp.bfloat16

EVERY = ("z", "x", "y", "c")
TEAM = ("y", "c")
ROWS = ("z", "x")

D = 1536
H = 48
HEAD = 64
N = 128
E = 3072
PROJ = 6448
TAPS = 4
G = 8
HG = H // G
EG = E // G
BG = 2 * N // G
TOKENS = 1024
CHUNK = 128
PIECES = TOKENS // CHUNK
AT_ONCE = 4
STEPS = PIECES // AT_ONCE
SPAN = AT_ONCE * CHUNK
EDGE = 16
LANES = 128
VG = EG + 2 * N
IN_COLS = 2 * EG + LANES
BLOCK = IN_COLS + EG
FORWARD_COLS = EG + VG + LANES
LATE_COLS = EG + LANES
STATE_ROWS = N + 8
TILE = 256
AHEAD, KEEP, TAIL, GAIN, SEGMENT = 4, 9, 10, 11, 12


def dot(a, b, dims):
    return lax.dot_general(
        a.astype(BF16), b.astype(BF16), (dims, ((), ())), preferred_element_type=F32
    )


NN = ((1,), (0,))
NT = ((1,), (1,))
TN = ((0,), (0,))


def parts(value):
    top = value.astype(BF16)
    return top, (value - top.astype(F32)).astype(BF16)


def dot3(a, b, dims=NN):
    a_top, a_rest = parts(a)
    b_top, b_rest = parts(b)
    return dot(a_top, b_top, dims) + (dot(a_top, b_rest, dims) + dot(a_rest, b_top, dims))


def lane_of(shape):
    return lax.broadcasted_iota(jnp.int32, shape, 1)


def piece_rows(k, height=CHUNK):
    return pl.ds(k * height, height)


def widen(per_head):
    rows = per_head.shape[0]
    left = lane_of((rows, LANES)) < HEAD
    return jnp.concatenate(
        [
            jnp.where(
                left,
                jnp.broadcast_to(per_head[:, 2 * p : 2 * p + 1], (rows, LANES)),
                jnp.broadcast_to(per_head[:, 2 * p + 1 : 2 * p + 2], (rows, LANES)),
            )
            for p in range(HG // 2)
        ],
        axis=1,
    )


def head_sums(values, summer):
    top, rest = parts(values)
    return dot(top, summer, NN) + dot(rest, summer, NN)


def pair_lanes(p):
    return slice(p * LANES, (p + 1) * LANES)


def stacked_pair(values):
    left = lane_of(values.shape) < HEAD
    zero = jnp.zeros_like(values)
    return jnp.concatenate(
        [jnp.where(left, values, zero), jnp.where(left, zero, values)], axis=0
    )


def running(mask, values):
    top, rest = parts(values)
    least = values - top.astype(F32) - rest.astype(F32)
    return dot(mask, top, NN) + (dot(mask, rest, NN) + dot(mask, least, NN))


def silu_parts(values):
    sig = jax.nn.sigmoid(values)
    return sig, values * sig


def softplus(values):
    return jnp.maximum(values, 0.0) + jnp.log1p(jnp.exp(-jnp.abs(values)))


def square_iota():
    shape = (CHUNK, CHUNK)
    return lax.broadcasted_iota(jnp.int32, shape, 0), lane_of(shape)


def same_document(flags, row):
    return flags[:, SEGMENT : SEGMENT + 1] == row


def in_order(core_ref, own_ref, other_ref):
    own, other = own_ref[0], other_ref[0]
    first = core_ref[1] == 0
    return jnp.concatenate(
        [jnp.where(first, own, other), jnp.where(first, other, own)], axis=0
    )


def project_kernel(
    core_ref, own_ref, other_ref, edge_ref, w_ref, gain_ref, normed_ref, z_ref, v_ref, r_ref
):
    def put(x, at):
        x = x.astype(F32)
        scale = lax.rsqrt(jnp.mean(x * x, axis=1, keepdims=True) + EPSILON)
        normed = (x * scale * gain_ref[...]).astype(BF16)
        normed_ref[at, :] = normed
        out = jnp.dot(normed, w_ref[...], preferred_element_type=F32)
        z_ref[at, :] = out[:, :EG]
        v_ref[at, :] = out[:, EG : EG + VG]
        r_ref[at, :] = out[:, EG + VG :]

    last = pl.num_programs(0) - 1

    @pl.when(pl.program_id(0) < last)
    def _():
        put(in_order(core_ref, own_ref, other_ref), pl.ds(0, 2 * CHUNK))

    @pl.when(pl.program_id(0) == last)
    def _():
        put(edge_ref[...], pl.ds(0, EDGE))


def incoming_kernel(core_ref, own_ref, other_ref, w_ref, q_ref, d_gated_ref):
    q = in_order(core_ref, own_ref, other_ref)
    q_ref[...] = q
    d_gated_ref[...] = jnp.dot(q, w_ref[...], preferred_element_type=F32)


def early_kernel(normed_ref, q_ref, dz_ref, gated_ref, out_ref):
    out_ref[:, :EG] = dot(normed_ref[0:TOKENS, :], dz_ref[...], TN).astype(BF16)
    out_ref[:, EG:] = dot(q_ref[...], gated_ref[...], TN).astype(BF16)


def forward_kernel(
    v_ref,
    before_ref,
    r_ref,
    flags_ref,
    ids_ref,
    taps_ref,
    head_ref,
    conv_ref,
    dt_ref,
    cum_ref,
    y_ref,
    start_ref,
    reach_ref,
    gain_ref,
    packed_ref,
    state,
    reach,
):
    step = pl.program_id(0)

    @pl.when(step == 0)
    def _():
        state[...] = jnp.zeros_like(state)
        reach[...] = jnp.ones_like(reach)

    for k in range(AT_ONCE):
        c = step * AT_ONCE + k
        at, at8 = piece_rows(k), piece_rows(k, 8)
        flags = flags_ref[at, :]
        window = jnp.concatenate([before_ref[...] if k == 0 else v_ref[pl.ds(k * CHUNK - 8, 8), :], v_ref[at, :]], axis=0)
        conv = taps_ref[TAPS : TAPS + 1, :] + taps_ref[0:1, :] * window[8:]
        for lag in range(1, TAPS):
            conv = conv + taps_ref[lag : lag + 1, :] * (
                pltpu.roll(window, lag, 0)[8:] * flags[:, lag : lag + 1]
            )
        conv_ref[at, :] = conv
        act = conv * jax.nn.sigmoid(conv)
        xs, bm, cm = act[:, :EG], act[:, EG : EG + N], act[:, EG + N :]
        dt = softplus(r_ref[at, :] + head_ref[0:1, :])
        dt_ref[at, :] = dt
        ti, si = square_iota()
        lower = (ti >= si).astype(F32)
        cum = running(lower, -head_ref[1:2, :] * dt)
        cum_ref[at, :] = cum
        cum_t = cum.T
        last = cum[CHUNK - 1 : CHUNK, :]
        tail = jnp.exp(last - cum) * flags[:, TAIL : TAIL + 1]
        carry = jnp.exp(cum) * flags[:, KEEP : KEEP + 1]
        gain = widen(jnp.exp(last) * flags[0:1, GAIN : GAIN + 1])
        xdt = xs * widen(dt)
        scores = dot3(cm, bm, NT)
        mask = (ti >= si) & same_document(flags, ids_ref[pl.ds(c, 1), :])
        within = []
        for p in range(HG // 2):
            mix = [
                jnp.exp(jnp.where(mask, cum[:, h : h + 1] - cum_t[h : h + 1, :], -1e30)) * scores
                for h in (2 * p, 2 * p + 1)
            ]
            within.append(
                dot3(jnp.concatenate(mix, axis=1), stacked_pair(xdt[:, pair_lanes(p)]))
            )
        y_ref[at, :] = jnp.concatenate(within, axis=1) + widen(carry) * dot3(cm, state[...])
        start_ref[k] = state[...]
        reach_ref[at8, :] = reach[...]
        gain_ref[at8, :] = jnp.broadcast_to(gain, (8, EG))
        state[...] = gain * state[...] + dot3(bm.T, xdt * widen(tail))
        reach[...] = gain * reach[...]

    @pl.when(step == STEPS - 1)
    def _():
        packed_ref[0:N, :] = state[...]
        packed_ref[N:, :] = reach[...]


def joined_states(first, second, third):
    return first[:N] + first[N : N + 1] * (second[:N] + second[N : N + 1] * third[:N])


def output_kernel(
    y_part_ref,
    conv_ref,
    cum_ref,
    flags_ref,
    z_ref,
    d_gated_ref,
    reach_ref,
    first_ref,
    second_ref,
    third_ref,
    rows_ref,
    y_ref,
    sums_ref,
    arrived_ref,
):
    step = pl.program_id(0)

    @pl.when(step == 0)
    def _():
        arrived_ref[...] = joined_states(first_ref[...], second_ref[...], third_ref[...])

    for k in range(AT_ONCE):
        c = step * AT_ONCE + k
        at = piece_rows(k)
        conv = conv_ref[at, :]
        act = conv * jax.nn.sigmoid(conv)
        carry = widen(jnp.exp(cum_ref[at, :]) * flags_ref[at, KEEP : KEEP + 1]) * reach_ref[pl.ds(8 * k, 1), :]
        y = (
            y_part_ref[at, :]
            + carry * dot3(act[:, EG + N :], arrived_ref[...])
            + rows_ref[0:1, :] * act[:, :EG]
        )
        y_ref[at, :] = y
        _, silu_z = silu_parts(z_ref[at, :])
        g = y * silu_z
        squares = jnp.sum(g * g, axis=1, keepdims=True)
        inner = jnp.sum(d_gated_ref[at, :] * rows_ref[1:2, :] * g, axis=1, keepdims=True)
        lane = lane_of((CHUNK, LANES))
        turned = jnp.where(lane == 0, squares, jnp.where(lane == 1, inner, 0.0)).T
        sums_ref[pl.ds(c, 1), :] = turned[0:1, :]
        sums_ref[pl.ds(PIECES + c, 1), :] = turned[1:2, :]


def gate_kernel(
    y_ref,
    z_ref,
    d_gated_ref,
    conv_ref,
    cum_ref,
    flags_ref,
    gain_ref,
    sums_ref,
    rows_ref,
    gated_ref,
    dz_ref,
    dy_ref,
    end_ref,
    reach_ref,
    d_gate_ref,
    packed_ref,
    state,
    reach,
):
    step = STEPS - 1 - pl.program_id(0)

    @pl.when(step == STEPS - 1)
    def _():
        state[...] = jnp.zeros_like(state)
        reach[...] = jnp.ones_like(reach)
        d_gate_ref[...] = jnp.zeros_like(d_gate_ref)

    for k in reversed(range(AT_ONCE)):
        c = step * AT_ONCE + k
        at, at8 = piece_rows(k), piece_rows(k, 8)
        ti, _ = square_iota()
        turned = jnp.where(
            ti == 0,
            sums_ref[pl.ds(c, 1), :],
            jnp.where(ti == 1, sums_ref[pl.ds(PIECES + c, 1), :], 0.0),
        ).T
        root = lax.rsqrt(turned[:, 0:1] * (1.0 / E) + EPSILON)
        slope = turned[:, 1:2] * (root * root * root) * (1.0 / E)
        gate = rows_ref[1:2, :]
        y = y_ref[at, :]
        sig, silu_z = silu_parts(z_ref[at, :])
        g = y * silu_z
        unit = g * root
        gated_ref[at, :] = (unit * gate).astype(BF16)
        d_gated = d_gated_ref[at, :]
        d_gate_ref[0:1, :] += jnp.sum(d_gated * unit, axis=0, keepdims=True)
        d_g = root * (d_gated * gate) - g * slope
        dy = d_g * silu_z
        dz_ref[at, :] = (d_g * y * (sig + silu_z * (1.0 - sig))).astype(BF16)
        dy_ref[at, :] = dy
        conv = conv_ref[at, EG + N :]
        cm = conv * jax.nn.sigmoid(conv)
        carry = widen(jnp.exp(cum_ref[at, :]) * flags_ref[at, KEEP : KEEP + 1])
        end_ref[k] = state[...]
        reach_ref[at8, :] = reach[...]
        gain = gain_ref[pl.ds(8 * k, 1), :]
        state[...] = gain * state[...] + dot3(cm.T, dy * carry)
        reach[...] = gain * reach[...]

    @pl.when(step == 0)
    def _():
        packed_ref[0:N, :] = state[...]
        packed_ref[N:, :] = reach[...]


def inner_kernel(dy_ref, conv_ref, dt_ref, cum_ref, flags_ref, ids_ref, u_ref, d_bc_ref):
    for k in range(AT_ONCE):
        c = pl.program_id(0) * AT_ONCE + k
        at = piece_rows(k)
        flags = flags_ref[at, :]
        conv = conv_ref[at, :]
        act = conv * jax.nn.sigmoid(conv)
        xs, bm, cm = act[:, :EG], act[:, EG : EG + N], act[:, EG + N :]
        cum = cum_ref[at, :]
        cum_t = cum.T
        dy = dy_ref[at, :]
        xdt = xs * widen(dt_ref[at, :])
        scores_t = dot3(bm, cm, NT)
        ti, si = square_iota()
        same = same_document(flags, ids_ref[pl.ds(c, 1), :])
        mask = (ti >= si) & same
        mask_t = (ti <= si) & same
        d_scores = jnp.zeros((CHUNK, CHUNK), F32)
        u = []
        for p in range(HG // 2):
            own = stacked_pair(dy[:, pair_lanes(p)])
            pairs = dot3(own, xdt[:, pair_lanes(p)], NT)
            mix_t = []
            for k in range(2):
                h = 2 * p + k
                gap = cum[:, h : h + 1] - cum_t[h : h + 1, :]
                d_scores = d_scores + jnp.exp(jnp.where(mask, gap, -1e30)) * (
                    pairs[k * CHUNK : (k + 1) * CHUNK]
                )
                mix_t.append(jnp.exp(jnp.where(mask_t, -gap, -1e30)) * scores_t)
            u.append(dot(jnp.concatenate(mix_t, axis=1), own, NN))
        u_ref[at, :] = jnp.concatenate(u, axis=1)
        d_bc_ref[at, :N] = dot3(d_scores.T, cm)
        d_bc_ref[at, N:] = dot3(d_scores, bm)


def backward_kernel(
    core_ref,
    u_ref,
    d_bc_ref,
    dy_ref,
    y_ref,
    conv_ref,
    dt_ref,
    cum_ref,
    r_ref,
    flags_ref,
    start_ref,
    reach_ref,
    arrived_ref,
    end_ref,
    reach_back_ref,
    first_ref,
    second_ref,
    third_ref,
    final_ref,
    v_ref,
    before_ref,
    rows_ref,
    taps_ref,
    head_ref,
    summer_ref,
    edge_flags_ref,
    dv_ref,
    d_edge_ref,
    kept_ref,
    sent_ref,
    dr_ref,
    wide_ref,
    heads_ref,
    following,
    flowing,
    adjoint_in,
):
    step = STEPS - 1 - pl.program_id(0)
    summer = summer_ref[...]

    @pl.when(step == STEPS - 1)
    def _():
        adjoint = joined_states(first_ref[...], second_ref[...], third_ref[...])
        adjoint_in[...] = adjoint
        final = final_ref[0:N, :] + final_ref[N : N + 1, :] * arrived_ref[...]
        inner = jnp.sum(adjoint * final, axis=0, keepdims=True)
        flowing[...] = head_sums(jnp.broadcast_to(inner, (8, EG)), summer)
        following[...] = jnp.zeros_like(following)
        wide_ref[...] = jnp.zeros_like(wide_ref)
        heads_ref[...] = jnp.zeros_like(heads_ref)

    for k in reversed(range(AT_ONCE)):
        at = piece_rows(k)
        flags = flags_ref[at, :]
        conv = conv_ref[at, :]
        sig, act = silu_parts(conv)
        xs, bm = act[:, :EG], act[:, EG : EG + N]
        cum = cum_ref[at, :]
        dt = dt_ref[at, :]
        dy = dy_ref[at, :]
        skip = rows_ref[0:1, :]
        rate = head_ref[1:2, :]
        last = cum[CHUNK - 1 : CHUNK, :]
        tail = widen(jnp.exp(last - cum) * flags[:, TAIL : TAIL + 1])
        carry = widen(jnp.exp(cum) * flags[:, KEEP : KEEP + 1])
        dt_wide = widen(dt)
        start = start_ref[k] + reach_ref[pl.ds(8 * k, 1), :] * arrived_ref[...]
        adjoint = end_ref[k] + reach_back_ref[pl.ds(8 * k, 1), :] * adjoint_in[...]
        u = u_ref[at, :] + tail * dot3(bm, adjoint)
        d_xs = u * dt_wide + skip * dy
        d_dt = head_sums(xs * u, summer)
        d_bm = d_bc_ref[at, :N] + dot3(xs * dt_wide * tail, adjoint, NT)
        d_cm = d_bc_ref[at, N:] + dot3(dy * carry, start, NT)
        turned = jnp.concatenate([d_bm.T, d_cm.T], axis=0)
        of_core = [
            jnp.concatenate(
                [turned[(2 * y + c) * BG : (2 * y + c + 1) * BG] for y in range(G // 2)], axis=0
            )
            for c in range(2)
        ]
        first = core_ref[1] == 0
        kept_ref[:, at] = jnp.where(first, of_core[0], of_core[1])
        sent_ref[:, at] = jnp.where(first, of_core[1], of_core[0])
        flow = head_sums(dy * (y_ref[at, :] - skip * xs), summer) - dt * d_dt
        ti, si = square_iota()
        upper = (si >= ti).astype(F32)
        d_la = running(upper, flow) + flowing[0:1, :]
        flowing[...] = jnp.broadcast_to(d_la[0:1, :], flowing.shape)
        d_la = d_la * flags[:, 1:2]
        d_r = (d_dt - rate * d_la) * jax.nn.sigmoid(r_ref[at, :] + head_ref[0:1, :])
        dr_ref[at, :] = d_r
        heads_ref[0:1, :] += jnp.sum(d_r, axis=0, keepdims=True)
        heads_ref[1:2, :] += jnp.sum(d_la * (-rate * dt), axis=0, keepdims=True)
        heads_ref[2:3, :] += jnp.sum(head_sums(dy * xs, summer), axis=0, keepdims=True)

        sig, conv = sig[:, :EG], conv[:, :EG]
        d_conv = d_xs * (sig + conv * sig * (1.0 - sig))
        window = jnp.concatenate([before_ref[...] if k == 0 else v_ref[pl.ds(k * CHUNK - 8, 8), :], v_ref[at, :]], axis=0)
        ahead = jnp.concatenate([d_conv, following[...]], axis=0)
        wide_ref[0:1, :] += jnp.sum(d_conv * window[8:], axis=0, keepdims=True)
        wide_ref[TAPS : TAPS + 1, :] += jnp.sum(d_conv, axis=0, keepdims=True)
        dv = taps_ref[0:1, :EG] * d_conv
        for lag in range(1, TAPS):
            wide_ref[lag : lag + 1, :] += jnp.sum(
                d_conv * pltpu.roll(window, lag, 0)[8:] * flags[:, lag : lag + 1],
                axis=0,
                keepdims=True,
            )
            dv = dv + taps_ref[lag : lag + 1, :EG] * (
                pltpu.roll(ahead, CHUNK + 8 - lag, 0)[:CHUNK] * flags[:, AHEAD + lag : AHEAD + lag + 1]
            )
        dv_ref[at, :] = dv.astype(BF16)
        following[...] = d_conv[0:8]

    @pl.when(step == 0)
    def _():
        d_edge_ref[...] = edge_rows(following[...], taps_ref[:, :EG], edge_flags_ref[...])


def edge_rows(d_conv, taps, flags):
    zero = jnp.zeros_like(d_conv)
    ahead = jnp.concatenate([zero, d_conv], axis=0)
    total = zero
    for lag in range(1, TAPS):
        total = total + taps[lag : lag + 1, :] * (
            pltpu.roll(ahead, EDGE - lag, 0)[0:8] * flags[:, AHEAD + lag : AHEAD + lag + 1]
        )
    return jnp.concatenate([zero, total], axis=0).astype(BF16)


def shared_kernel(
    team_ref,
    got_refs,
    conv_b_ref,
    conv_c_ref,
    v_b_ref,
    v_c_ref,
    before_b_ref,
    before_c_ref,
    dr_ref,
    dv_ref,
    d_edge_ref,
    flags_ref,
    edge_flags_ref,
    taps_ref,
    late_ref,
    wide_ref,
    following,
):
    step = pl.program_id(0)
    turn = (2 * N - BG * team_ref[0]) % (2 * N)

    def own(b, c):
        return pltpu.roll(jnp.concatenate([b, c], axis=1), turn, 1)[:, :LANES]

    def before(k):
        if k == 0:
            return own(before_b_ref[...], before_c_ref[...])
        last = pl.ds(k * CHUNK - 8, 8)
        return own(v_b_ref[last, :], v_c_ref[last, :])

    @pl.when(step == 0)
    def _():
        following[...] = jnp.zeros_like(following)
        wide_ref[...] = jnp.zeros_like(wide_ref)

    def piece(k):
        at = piece_rows(k)
        flags = flags_ref[at, :]
        total = sum(ref[:, at] for ref in got_refs)
        d_act = jnp.concatenate([total, jnp.zeros((LANES - BG, CHUNK), F32)], axis=0).T
        conv = own(conv_b_ref[at, :], conv_c_ref[at, :])
        sig = jax.nn.sigmoid(conv)
        d_conv = d_act * (sig + conv * sig * (1.0 - sig))
        window = jnp.concatenate(
            [before(k), own(v_b_ref[at, :], v_c_ref[at, :])], axis=0
        )
        ahead = jnp.concatenate([d_conv, following[...]], axis=0)
        wide_ref[0:1, :] += jnp.sum(d_conv * window[8:], axis=0, keepdims=True)
        wide_ref[TAPS : TAPS + 1, :] += jnp.sum(d_conv, axis=0, keepdims=True)
        dv = taps_ref[0:1, :] * d_conv
        for lag in range(1, TAPS):
            wide_ref[lag : lag + 1, :] += jnp.sum(
                d_conv * pltpu.roll(window, lag, 0)[8:] * flags[:, lag : lag + 1],
                axis=0,
                keepdims=True,
            )
            dv = dv + taps_ref[lag : lag + 1, :] * (
                pltpu.roll(ahead, CHUNK + 8 - lag, 0)[:CHUNK]
                * flags[:, AHEAD + lag : AHEAD + lag + 1]
            )
        following[...] = d_conv[0:8]
        late_ref[at, :EG] = dv_ref[at, :]
        late_ref[at, EG:] = (dv + pltpu.roll(dr_ref[at, :], BG, 1)).astype(BF16)

    @pl.when(step < STEPS)
    def _():
        for k in reversed(range(AT_ONCE)):
            piece(k)

    @pl.when(step == STEPS)
    def _():
        late_ref[0:EDGE, :EG] = d_edge_ref[...]
        late_ref[0:EDGE, EG:] = edge_rows(following[...], taps_ref[...], edge_flags_ref[...])


def triangle(n):
    return [(i, j) for i in range(n // TILE) for j in range(i, n // TILE)]


def gram_kernel(which_ref, x_ref, out_ref, held, total, in_sems, out_sems):
    parts_of_x, n, _ = x_ref.shape
    count = n // TILE
    order = triangle(n)

    def at(i):
        return pl.ds(i * TILE, TILE)

    def run(columns):
        width = columns.stop - columns.start
        arriving = [
            pltpu.make_async_copy(
                x_ref.at[y, :, columns], held.at[y, :, pl.ds(0, width)], in_sems.at[y]
            )
            for y in range(parts_of_x)
        ]
        leaving = []
        for copy in arriving:
            copy.start()
        for y in range(0, parts_of_x, 2):
            for copy in (arriving[y], arriving[y + 1]):
                copy.wait()
            for i in range(count):

                def taken(rows):
                    return jnp.concatenate(
                        [held[y, rows, :width], held[y + 1, rows, :width]], axis=1
                    )

                product = dot(taken(at(i)), taken(pl.ds(i * TILE, n - i * TILE)), NT)
                own = order.index((i, i))
                for j in range(i, count):
                    block = product[:, (j - i) * TILE : (j - i + 1) * TILE]
                    b = own + j - i
                    total[b] = block if y == 0 else total[b] + block
                if y + 2 == parts_of_x:
                    blocks = pl.ds(own, count - i)
                    leaving.append(
                        pltpu.make_async_copy(
                            total.at[blocks], out_ref.at[blocks], out_sems.at[i]
                        )
                    )
                    leaving[-1].start()
        for copy in leaving:
            copy.wait()

    @pl.when(which_ref[0] == 1)
    def _():
        run(slice(0, IN_COLS))

    @pl.when(which_ref[0] != 1)
    def _():
        run(slice(IN_COLS, BLOCK))


def chain_kernel(own_ref, got_ref, pick_ref, t_ref, high, low, h_high, h_low, q_ref):
    n = high.shape[0]
    count = n // TILE
    order = triangle(n)

    def at(i):
        return pl.ds(i * TILE, TILE) if isinstance(i, int) else pl.ds(pl.multiple_of(i * TILE, TILE), TILE)

    def times(a, b):
        return jnp.dot(a, b, preferred_element_type=F32)

    diagonal = lax.broadcasted_iota(jnp.int32, (TILE, TILE), 0) == lax.broadcasted_iota(jnp.int32, (TILE, TILE), 1)
    square = jnp.zeros((1, 1), F32)
    for b, (i, j) in enumerate(order):
        if i == j:
            square = square + jnp.sum(jnp.where(diagonal, own_ref[b] + got_ref[b], 0.0), keepdims=True)
    inverse = 1.0 / (jnp.sqrt(square) + NORM_FLOOR)
    scale = inverse * inverse

    def put(value, i, j, top_ref, rest_ref):
        top = value.astype(BF16)
        top_ref[at(i), at(j)] = top
        if i != j:
            top_ref[at(j), at(i)] = top.T
        if rest_ref is not None:
            rest_ref[at(i), at(j)] = (value - top.astype(F32)).astype(BF16)

    def put_row(value, i, top_ref, rest_ref):
        for j in range(i, count):
            put(value[:, (j - i) * TILE : (j - i + 1) * TILE], i, j, top_ref, rest_ref)

    for b, (i, j) in enumerate(order):
        put((own_ref[b] + got_ref[b]) * scale, i, j, high, low)

    def polynomial(q):
        for i in range(count):
            rest = pl.ds(i * TILE, n - i * TILE)
            value = times(high[at(i), :], high[:, rest])
            put_row(POLY_SECOND * high[at(i), rest].astype(F32) + POLY_THIRD * value, i, q, None)

    def whole(top_ref, rest_ref, i, rest):
        return top_ref[at(i), rest].astype(F32) + rest_ref[at(i), rest].astype(F32)

    def iterate(step, _):
        q = q_ref.at[step]
        polynomial(q)
        for i in range(count):
            rest = pl.ds(i * TILE, n - i * TILE)
            value = times(q[at(i), :], high[:, rest]) + POLY_FIRST * whole(high, low, i, rest)
            put_row(value, i, h_high, h_low)
        for i in range(count):
            rest = pl.ds(i * TILE, n - i * TILE)
            value = times(h_high[at(i), :], q[:, rest]) + POLY_FIRST * whole(h_high, h_low, i, rest)
            put_row(value, i, high, low)
        return 0

    def thin(t, matrix):
        top, rest = parts(t)
        both = times(jnp.concatenate([top, rest], axis=0), matrix)
        return both[: t.shape[0]] + both[t.shape[0] :]

    def multiplied(t, step):
        return POLY_FIRST * t + thin(t, q_ref[step])

    def last_gram(t):
        return multiplied(thin(multiplied(t, NS_STEPS - 2), high[...]), NS_STEPS - 2)

    lax.fori_loop(0, NS_STEPS - 2, iterate, 0)
    polynomial(q_ref.at[NS_STEPS - 2])
    pick = pick_ref[...]
    once = last_gram(pick)
    t = POLY_FIRST * pick + POLY_SECOND * once + POLY_THIRD * last_gram(once)
    for step in reversed(range(NS_STEPS - 1)):
        t = multiplied(t, step)
    t_ref[...] = t * inverse


SMALL = pltpu.CompilerParams(vmem_limit_bytes=20 << 20)
LARGE = pltpu.CompilerParams(vmem_limit_bytes=60 << 20)


def spec(shape, index=None):
    return pl.BlockSpec(shape, index if index is not None else (lambda c: (0,) * len(shape)))


def rows(width, height=SPAN):
    return spec((height, width), lambda c: (c, 0))


def rows_back(width, height=SPAN):
    return spec((height, width), lambda c: (STEPS - 1 - c, 0))


def previous(c):
    return jnp.where(c == 0, (TOKENS + EDGE) // 8 - 1, c * (SPAN // 8) - 1)


def shaped(*shape, dtype=F32):
    return jax.ShapeDtypeStruct(shape, dtype)


def cost(flops, moved):
    return pl.CostEstimate(flops=flops, bytes_accessed=moved, transcendentals=0)


def piece_of(kind):
    size = 4

    def index(c, place):
        return ((place[0] - jnp.minimum(c, size - 1) + size) % size, 0, 0)

    return pl.BlockSpec((1, CHUNK, D), index)


def project(place, own, other, edge, weights, gain):
    total = TOKENS + EDGE
    block = 2 * CHUNK

    def out(width):
        return pl.BlockSpec((block, width), lambda c, place: (c, 0))

    def whole(*shape):
        return pl.BlockSpec(shape, lambda c, place: (0, 0))

    return pl.pallas_call(
        project_kernel,
        grid_spec=pltpu.PrefetchScalarGridSpec(
            num_scalar_prefetch=1,
            grid=(TOKENS // block + 1,),
            in_specs=[
                piece_of("own"),
                piece_of("other"),
                whole(EDGE, D),
                whole(D, FORWARD_COLS),
                whole(1, D),
            ],
            out_specs=[out(D), out(EG), out(VG), out(LANES)],
        ),
        out_shape=[
            shaped(total, D, dtype=BF16),
            shaped(total, EG),
            shaped(total, VG),
            shaped(total, LANES),
        ],
        compiler_params=SMALL,
        cost_estimate=cost(2 * total * D * FORWARD_COLS, 16 << 20),
        name="project",
    )(place, own, other, edge, weights, gain)


def incoming(place, own, other, weights):
    block = 2 * CHUNK

    def out(width):
        return pl.BlockSpec((block, width), lambda c, place: (c, 0))

    return pl.pallas_call(
        incoming_kernel,
        grid_spec=pltpu.PrefetchScalarGridSpec(
            num_scalar_prefetch=1,
            grid=(TOKENS // block,),
            in_specs=[
                piece_of("own"),
                piece_of("other"),
                pl.BlockSpec((D, EG), lambda c, place: (0, FORWARD_COLS // EG)),
            ],
            out_specs=[out(D), out(EG)],
        ),
        out_shape=[shaped(TOKENS, D, dtype=BF16), shaped(TOKENS, EG)],
        compiler_params=SMALL,
        cost_estimate=cost(2 * TOKENS * D * EG, 9 << 20),
        name="incoming",
    )(place, own, other, weights)


def early_products(normed, q, dz, gated):
    return pl.pallas_call(
        early_kernel,
        grid=(D // TILE,),
        in_specs=[
            spec((TOKENS + EDGE, TILE), lambda c: (0, c)),
            spec((TOKENS, TILE), lambda c: (0, c)),
            spec((TOKENS, EG)),
            spec((TOKENS, EG)),
        ],
        out_specs=rows(2 * EG, TILE),
        out_shape=shaped(D, 2 * EG, dtype=BF16),
        compiler_params=SMALL,
        cost_estimate=cost(4 * TOKENS * D * EG, 13 << 20),
        name="early",
    )(normed, q, dz, gated)


def forward(v, r, flags, ids, taps, head):
    return pl.pallas_call(
        forward_kernel,
        grid=(STEPS,),
        in_specs=[
            rows(VG),
            spec((8, VG), lambda c: (previous(c), 0)),
            rows(LANES),
            rows(LANES),
            spec((8, LANES)),
            spec((8, VG)),
            spec((8, LANES)),
        ],
        out_specs=[
            rows(VG),
            rows(LANES),
            rows(LANES),
            rows(EG),
            spec((AT_ONCE, N, EG), lambda c: (c, 0, 0)),
            rows(EG, 8 * AT_ONCE),
            rows(EG, 8 * AT_ONCE),
            spec((STATE_ROWS, EG)),
        ],
        out_shape=[
            shaped(TOKENS, VG),
            shaped(TOKENS, LANES),
            shaped(TOKENS, LANES),
            shaped(TOKENS, EG),
            shaped(PIECES, N, EG),
            shaped(PIECES * 8, EG),
            shaped(PIECES * 8, EG),
            shaped(STATE_ROWS, EG),
        ],
        scratch_shapes=[pltpu.VMEM((N, EG), F32), pltpu.VMEM((8, EG), F32)],
        compiler_params=SMALL,
        cost_estimate=cost(3 << 30, 14 << 20),
        name="forward",
    )(v, v, r, flags, ids, taps, head)


def outputs(y_part, conv, cum, flags, z, d_gated, reach, arrivals, wide):
    return pl.pallas_call(
        output_kernel,
        grid=(STEPS,),
        in_specs=[rows(EG), rows(VG), rows(LANES), rows(LANES), rows(EG), rows(EG), rows(EG, 8 * AT_ONCE)]
        + [spec((STATE_ROWS, EG))] * 3
        + [spec((8, EG))],
        out_specs=[rows(EG), spec((2 * PIECES, LANES)), spec((N, EG))],
        out_shape=[shaped(TOKENS, EG), shaped(2 * PIECES, LANES), shaped(N, EG)],
        compiler_params=SMALL,
        cost_estimate=cost(1 << 28, 12 << 20),
        name="outputs",
    )(y_part, conv, cum, flags, z, d_gated, reach, *arrivals, wide)


def gate(y, z, d_gated, conv, cum, flags, gain, sums, wide):
    return pl.pallas_call(
        gate_kernel,
        grid=(STEPS,),
        in_specs=[rows_back(EG)] * 3
        + [rows_back(VG), rows_back(LANES), rows_back(LANES), rows_back(EG, 8 * AT_ONCE)]
        + [spec((2 * PIECES, LANES)), spec((8, EG))],
        out_specs=[rows_back(EG)] * 3
        + [
            spec((AT_ONCE, N, EG), lambda c: (STEPS - 1 - c, 0, 0)),
            rows_back(EG, 8 * AT_ONCE),
            spec((8, EG)),
            spec((STATE_ROWS, EG)),
        ],
        out_shape=[
            shaped(TOKENS, EG, dtype=BF16),
            shaped(TOKENS, EG, dtype=BF16),
            shaped(TOKENS, EG),
            shaped(PIECES, N, EG),
            shaped(PIECES * 8, EG),
            shaped(8, EG),
            shaped(STATE_ROWS, EG),
        ],
        scratch_shapes=[pltpu.VMEM((N, EG), F32), pltpu.VMEM((8, EG), F32)],
        compiler_params=SMALL,
        cost_estimate=cost(1 << 28, 14 << 20),
        name="gate",
    )(y, z, d_gated, conv, cum, flags, gain, sums, wide)


def inner(dy, conv, dt, cum, flags, ids):
    return pl.pallas_call(
        inner_kernel,
        grid=(STEPS,),
        in_specs=[rows(EG), rows(VG), rows(LANES), rows(LANES), rows(LANES), spec((8, LANES))],
        out_specs=[rows(EG), rows(2 * N)],
        out_shape=[shaped(TOKENS, EG), shaped(TOKENS, 2 * N)],
        compiler_params=SMALL,
        cost_estimate=cost(3 << 30, 9 << 20),
        name="inner",
    )(dy, conv, dt, cum, flags, ids)


def backward(
    place, u, d_bc, dy, y, conv, dt, cum, r, flags, starts, reach, arrived, ends, reach_back, arrivals,
    final, v, wide, taps, head, summer, edge_flags,
):
    def back_state():
        return spec((AT_ONCE, N, EG), lambda c: (STEPS - 1 - c, 0, 0))

    return pl.pallas_call(
        backward_kernel,
        grid=(STEPS,),
        in_specs=[
            pl.BlockSpec(memory_space=pltpu.SMEM),
            rows_back(EG),
            rows_back(2 * N),
            rows_back(EG),
            rows_back(EG),
            rows_back(VG),
            rows_back(LANES),
            rows_back(LANES),
            rows_back(LANES),
            rows_back(LANES),
            back_state(),
            rows_back(EG, 8 * AT_ONCE),
            spec((N, EG)),
            back_state(),
            rows_back(EG, 8 * AT_ONCE),
        ]
        + [spec((STATE_ROWS, EG))] * 4
        + [
            rows_back(EG),
            spec((8, EG), lambda c: (previous(STEPS - 1 - c), 0)),
            spec((8, EG)),
            spec((8, VG)),
            spec((8, LANES)),
            spec((EG, LANES)),
            spec((8, LANES)),
        ],
        out_specs=[
            rows_back(EG),
            spec((EDGE, EG)),
            spec((N, SPAN), lambda c: (0, STEPS - 1 - c)),
            spec((N, SPAN), lambda c: (0, STEPS - 1 - c)),
            rows_back(LANES),
            spec((8, EG)),
            spec((8, LANES)),
        ],
        out_shape=[
            shaped(TOKENS, EG, dtype=BF16),
            shaped(EDGE, EG, dtype=BF16),
            shaped(N, TOKENS),
            shaped(N, TOKENS),
            shaped(TOKENS, LANES),
            shaped(8, EG),
            shaped(8, LANES),
        ],
        scratch_shapes=[
            pltpu.VMEM((8, EG), F32),
            pltpu.VMEM((8, LANES), F32),
            pltpu.VMEM((N, EG), F32),
        ],
        compiler_params=SMALL,
        cost_estimate=cost(3 << 29, 20 << 20),
        name="backward",
    )(
        place, u, d_bc, dy, y, conv, dt, cum, r, flags, starts, reach, arrived, ends, reach_back,
        *arrivals, final, v, v, wide, taps, head, summer, edge_flags,
    )


def shared(team, got, conv, v, dr, dv, d_edge, flags, edge_flags, taps):
    def turned(step):
        return jnp.maximum(STEPS - 1 - step, 0)

    def lanes_of(block):
        return spec((SPAN, LANES), lambda c: (turned(c), block))

    def before(block):
        return spec((8, LANES), lambda c: (previous(turned(c)), block))

    b, c_block = EG // LANES, EG // LANES + 1
    def kernel(team_ref, a, b, c, d, *refs):
        shared_kernel(team_ref, (a, b, c, d), *refs)

    return pl.pallas_call(
        kernel,
        grid=(STEPS + 1,),
        in_specs=[
            pl.BlockSpec(memory_space=pltpu.SMEM),
            *[spec((BG, SPAN), lambda c: (0, turned(c)))] * 4,
            lanes_of(b),
            lanes_of(c_block),
            lanes_of(b),
            lanes_of(c_block),
            before(b),
            before(c_block),
            lanes_of(0),
            spec((SPAN, EG), lambda c: (turned(c), 0)),
            spec((EDGE, EG)),
            lanes_of(0),
            spec((8, LANES)),
            spec((8, LANES)),
        ],
        out_specs=[
            spec((SPAN, LATE_COLS), lambda c: (jnp.where(c == STEPS, STEPS, turned(c)), 0)),
            spec((8, LANES)),
        ],
        out_shape=[shaped(TOKENS + EDGE, LATE_COLS, dtype=BF16), shaped(8, LANES)],
        scratch_shapes=[pltpu.VMEM((8, LANES), F32)],
        compiler_params=SMALL,
        cost_estimate=cost(1 << 27, 6 << 20),
        name="shared",
    )(team, *got, conv, conv, v, v, v, v, dr, dv, d_edge, flags, edge_flags, taps)


def gram(which, x):
    count, n, _ = x.shape
    blocks = len(triangle(n))
    return pl.pallas_call(
        gram_kernel,
        in_specs=[pl.BlockSpec(memory_space=pltpu.SMEM), pl.BlockSpec(memory_space=pl.ANY)],
        out_specs=pl.BlockSpec(memory_space=pl.ANY),
        out_shape=shaped(blocks, TILE, TILE),
        scratch_shapes=[
            pltpu.VMEM((count, n, IN_COLS), BF16),
            pltpu.VMEM((blocks, TILE, TILE), F32),
            pltpu.SemaphoreType.DMA((count,)),
            pltpu.SemaphoreType.DMA((n // TILE,)),
        ],
        compiler_params=LARGE,
        cost_estimate=cost(n * n * count * BLOCK * 3 // 5, 14 << 20),
        name="gram",
    )(which.astype(jnp.int32).reshape(1), x)


def chain(own, got, pick):
    n = pick.shape[1]
    whole = pl.BlockSpec(memory_space=pltpu.VMEM)
    return pl.pallas_call(
        chain_kernel,
        out_shape=jax.ShapeDtypeStruct(pick.shape, F32),
        in_specs=[whole, whole, whole],
        out_specs=whole,
        scratch_shapes=[pltpu.VMEM((n, n), BF16)] * 4
        + [pltpu.VMEM((NS_STEPS - 1, n, n), BF16)],
        compiler_params=pltpu.CompilerParams(vmem_limit_bytes=52 << 20),
        cost_estimate=cost(14 * n * n * n, 11 << 20),
        name="chain",
    )(own, got, pick)


def summaries(packed, direction):
    size = lax.axis_size("x")
    return [
        lax.ppermute(
            packed,
            "x",
            [(s, s + direction * k) for s in range(size) if 0 <= s + direction * k < size],
        )
        for k in range(1, size)
    ]


def blocks_of_columns(in_rows, out_rows):
    count = in_rows.shape[0]
    kind = in_rows.dtype
    z = in_rows[:, :E].reshape(count, G, EG)
    xs = in_rows[:, E : 2 * E].reshape(count, G, EG)
    bc = in_rows[:, 2 * E : 2 * E + 2 * N].reshape(count, G, BG)
    r = in_rows[:, 2 * E + 2 * N :].reshape(count, G, HG)
    fill = jnp.zeros((count, G, LANES - BG - HG), kind)
    out = out_rows.reshape(count, G, EG)
    return jnp.concatenate([z, xs, bc, r, fill, out], axis=2).transpose(1, 0, 2)


def rows_of_blocks(blocks):
    count = blocks.shape[1]
    b = blocks.transpose(1, 0, 2)
    pieces = [
        b[:, :, :EG].reshape(count, E),
        b[:, :, EG : 2 * EG].reshape(count, E),
        b[:, :, 2 * EG : 2 * EG + BG].reshape(count, 2 * N),
        b[:, :, 2 * EG + BG : 2 * EG + BG + HG].reshape(count, H),
    ]
    return jnp.concatenate(pieces, axis=1), b[:, :, IN_COLS:].reshape(count, E)


def along_y(own):
    size = lax.axis_size("y")
    return [own] + [
        lax.ppermute(own, "y", [(s, (s + k) % size) for s in range(size)]) for k in range(1, size)
    ]


def team_sum(values):
    values = values + lax.ppermute(values, "c", [(0, 1), (1, 0)])
    return sum(along_y(values))


def after(value, *others):
    return lax.optimization_barrier((value,) + others)[0]


def local(
    hidden,
    segments,
    norm_gain,
    in_weight,
    conv_weight,
    conv_bias,
    dt_bias,
    a_log,
    skip_scale,
    gate_gain,
    out_weight,
    cotangent,
    in_momentum,
    out_momentum,
    vector_momentum,
):
    zi, xi, yi, ci = (lax.axis_index(a) for a in EVERY)
    team = yi * 2 + ci
    count = in_weight.shape[0]
    team_count = G * count
    swap = [(0, 1), (1, 0)]
    first = ci == 0

    def mine(values, width, start=0, axis=-1):
        return lax.dynamic_slice_in_dim(values, start + team * width, width, axis % values.ndim)

    z_w = in_weight[:, :E].reshape(count, G, EG)
    xs_w = in_weight[:, E : 2 * E].reshape(count, G, EG)
    bc_w = jnp.broadcast_to(in_weight[:, None, 2 * E : 2 * E + 2 * N], (count, G, 2 * N))
    r_w = jnp.pad(
        in_weight[:, 2 * E + 2 * N :].reshape(count, G, HG), ((0, 0), (0, 0), (0, LANES - HG))
    )
    out_w = out_weight.reshape(count, G, EG)
    sent = jnp.concatenate([z_w, xs_w, bc_w, r_w, out_w], axis=2).transpose(1, 0, 2)
    got = lax.all_to_all(sent, TEAM, 0, 0, tiled=True).reshape(team_count, -1)
    weights = lax.all_gather(got, ROWS, axis=0, tiled=True)

    numbers = jnp.pad(segments.astype(BF16)[:, None], ((0, 0), (0, LANES - 1)))
    pieces = along_y(jnp.concatenate([hidden, numbers], axis=1))
    momentum_block = lax.all_to_all(
        blocks_of_columns(
            *(after(m, got).astype(BF16) for m in (in_momentum, out_momentum))
        ),
        TEAM,
        0,
        0,
        tiled=True,
    ).reshape(team_count, BLOCK)
    conv_all = jnp.concatenate([conv_weight, conv_bias[None, :]], axis=0)
    taps = jnp.pad(
        jnp.concatenate([mine(conv_all[:, :E], EG), conv_all[:, E:]], axis=1),
        ((0, 8 - TAPS - 1), (0, 0)),
    )
    taps_shared = jnp.pad(mine(conv_all[:, E:], BG), ((0, 8 - TAPS - 1), (0, LANES - BG)))
    head = jnp.pad(
        jnp.stack([mine(dt_bias, HG), jnp.exp(mine(a_log, HG))]), ((0, 6), (0, LANES - HG))
    )
    wide = jnp.pad(
        jnp.stack([jnp.repeat(mine(skip_scale, HG), HEAD), mine(gate_gain, EG)]), ((0, 6), (0, 0))
    )
    summer = (
        lax.broadcasted_iota(jnp.int32, (EG, LANES), 0) // HEAD
        == lax.broadcasted_iota(jnp.int32, (EG, LANES), 1)
    ).astype(BF16)
    pieces, momentum_block, taps, taps_shared, head, wide, summer = lax.optimization_barrier(
        (pieces, momentum_block, taps, taps_shared, head, wide, summer)
    )
    own_rows = jnp.stack(pieces)
    other_rows = lax.ppermute(own_rows, "c", swap)
    q_pieces = along_y(after(cotangent, own_rows))
    place = jnp.stack([yi, ci]).astype(jnp.int32)
    size_x, size_y = lax.axis_size("x"), lax.axis_size("y")
    end_rows = lax.dynamic_index_in_dim(
        jnp.where(first, other_rows[:, CHUNK - EDGE :], own_rows[:, CHUNK - EDGE :]),
        (yi + 1) % size_y,
        0,
        False,
    )
    edge_rows_in = lax.ppermute(end_rows, "x", [(s, s + 1) for s in range(size_x - 1)])
    by_distance = jnp.stack([own_rows[:, :, D], other_rows[:, :, D]]).astype(F32)
    by_core = jnp.where(first, by_distance, by_distance[::-1])
    team_ids = by_core[:, (yi - jnp.arange(size_y)) % size_y].transpose(1, 0, 2).reshape(-1)
    next_ids = lax.ppermute(team_ids[:LANES], "x", [(s, s - 1) for s in range(1, size_x)])
    ids = jnp.concatenate(
        [
            jnp.where(xi == 0, -1.0, edge_rows_in[EDGE - 8 :, D].astype(F32)),
            team_ids,
            jnp.where(xi == size_x - 1, -1.0, next_ids[:8]),
        ]
    )

    def flag_lanes(at, size):
        own = ids[at : at + size]
        same = [(ids[at - k : at - k + size] == own).astype(F32) for k in range(TAPS)]
        ahead = [(ids[at + k : at + k + size] == own).astype(F32) for k in range(TAPS)]
        return own, same + ahead

    own_ids, lanes = flag_lanes(8, TOKENS)
    by_piece = own_ids.reshape(PIECES, CHUNK)
    before = ids[7 : 7 + TOKENS].reshape(PIECES, CHUNK)[:, :1]
    last = by_piece[:, CHUNK - 1 :]
    lanes = lanes + [
        jnp.zeros((TOKENS,), F32),
        (by_piece == before).astype(F32).reshape(-1),
        (by_piece == last).astype(F32).reshape(-1),
        jnp.broadcast_to((last == before).astype(F32), (PIECES, CHUNK)).reshape(-1),
        own_ids,
    ]
    flags = jnp.pad(jnp.stack(lanes, axis=1), ((0, 0), (0, LANES - len(lanes))))
    edge_ids = jnp.pad(ids, (8, 0), constant_values=-1.0)[: 8 + 16]
    edge_own = edge_ids[8:16]
    edge_flags = jnp.pad(
        jnp.stack(
            [jnp.zeros((8,), F32)] * AHEAD
            + [(edge_ids[8 + k : 16 + k] == edge_own).astype(F32) for k in range(TAPS)],
            axis=1,
        ),
        ((0, 0), (0, LANES - AHEAD - TAPS)),
    )

    q_pieces, flags, edge_flags = lax.optimization_barrier((q_pieces, flags, edge_flags))
    q_own = jnp.stack(q_pieces)
    q_other = lax.ppermute(q_own, "c", swap)

    normed, z, v, r = project(
        place, own_rows, other_rows, edge_rows_in, weights, norm_gain[None, :]
    )
    conv, dt, cum, y_part, starts, reach, gain, packed = forward(v, r, flags, by_piece, taps, head)
    arrivals = summaries(packed, 1)
    q_team, d_gated = incoming(place, q_own, q_other, weights)
    y, sums, arrived = outputs(y_part, conv, cum, flags, z, d_gated, reach, arrivals, wide)
    sums = team_sum(sums)
    gated, dz, dy, ends, reach_back, d_gate, packed_back = gate(
        y, z, d_gated, conv, cum, flags, gain, sums, wide
    )
    early = early_products(normed, q_team, dz, gated)
    dy, packed_back, early = lax.optimization_barrier((dy, packed_back, early))
    early_sum = lax.psum_scatter(early, ROWS, scatter_dimension=0, tiled=True).astype(F32)
    arrivals_back = summaries(packed_back, -1)

    u, d_bc = inner(dy, conv, dt, cum, flags, by_piece)
    dv, d_edge, kept, sent_bc, dr, wide_sums, head_sums_out = backward(
        place, u, d_bc, dy, y, conv, dt, cum, r, flags, starts, reach, arrived, ends, reach_back,
        arrivals_back, packed, v, wide, taps, head, summer, edge_flags,
    )
    summed = (kept + lax.ppermute(sent_bc, "c", swap)).reshape(size_y, BG, TOKENS)

    def piece_for(k):
        return lax.dynamic_index_in_dim(summed, (yi + k) % size_y, 0, False)

    d_bc_got = [piece_for(0)] + [
        lax.ppermute(piece_for(k), "y", [(s, (s + k) % size_y) for s in range(size_y)])
        for k in range(1, size_y)
    ]
    late, shared_sums = shared(
        team.reshape(1), d_bc_got, conv, v, dr, dv, d_edge, flags, edge_flags, taps_shared
    )
    late_partial = dot(normed, late, TN).astype(BF16)
    late_parts = lax.all_to_all(
        late_partial.reshape(16, team_count, LATE_COLS), ROWS, 0, 0, tiled=True
    )
    late_sum = jnp.sum(late_parts.astype(F32), axis=0)

    sums_block = jnp.concatenate([early_sum[:, :EG], late_sum, early_sum[:, EG:]], axis=1)
    momenta = MATRIX_MOMENTUM * momentum_block.astype(F32) + sums_block
    x_all = lax.all_gather(momenta.astype(BF16), ("y", "z", "x")).reshape(4, D, BLOCK)

    late_back = lax.ppermute(
        late[TOKENS:], "x", [(s, s - 1) for s in range(1, lax.axis_size("x"))]
    )
    late, late_back, dz, gated, late_sum = lax.optimization_barrier(
        (late, late_back, dz, gated, late_sum)
    )
    d_projected = jnp.concatenate(
        [
            dz,
            jnp.concatenate(
                [late[: TOKENS - EDGE], late[TOKENS - EDGE : TOKENS] + late_back], axis=0
            ),
        ],
        axis=1,
    )
    w_own = jnp.concatenate(
        [
            weights[:, : 2 * EG],
            mine(weights[:, 2 * EG : 2 * EG + 2 * N], BG),
            weights[:, 2 * EG + 2 * N : 2 * EG + 2 * N + HG],
            jnp.zeros((D, LANES - BG - HG), BF16),
        ],
        axis=1,
    )
    d_normed_part = dot(d_projected, w_own, NT)
    d_norm_gain = jnp.sum(d_normed_part * normed[:TOKENS].astype(F32), axis=0) / norm_gain
    mixed_part = dot(gated, weights[:, FORWARD_COLS:], NT)

    vector = jnp.concatenate(
        [
            d_norm_gain,
            jnp.concatenate(
                [wide_sums[: TAPS + 1], shared_sums[: TAPS + 1, :BG]], axis=1
            ).reshape(-1),
            d_gate[0],
            head_sums_out[:3, :HG].reshape(-1),
        ]
    )
    vector = jnp.pad(vector, (0, -vector.shape[0] % 1024)).reshape(-1, LANES)
    vector = jnp.sum(lax.all_gather(vector, ROWS), axis=0)
    vector = lax.all_gather(vector, TEAM).reshape(G, -1)
    own = EG + BG
    grad_gain = jnp.sum(vector[:, :D], axis=0)
    conv_parts = vector[:, D : D + (TAPS + 1) * own].reshape(G, TAPS + 1, own).transpose(1, 0, 2)
    conv_parts = jnp.concatenate(
        [
            conv_parts[:, :, :EG].reshape(TAPS + 1, E),
            conv_parts[:, :, EG:].reshape(TAPS + 1, 2 * N),
        ],
        axis=1,
    )
    rest = vector[:, D + (TAPS + 1) * own :]
    heads = rest[:, EG : EG + 3 * HG].reshape(G, 3, HG).transpose(1, 0, 2).reshape(-1)
    vector_grad = jnp.concatenate(
        [grad_gain, conv_parts.reshape(-1), heads, rest[:, :EG].reshape(-1)]
    )
    vector_old = jnp.concatenate(
        [norm_gain, conv_weight.reshape(-1), conv_bias, dt_bias, a_log, skip_scale, gate_gain]
    )
    vector_momentum_new = VECTOR_MOMENTUM * vector_momentum + (1.0 - VECTOR_MOMENTUM) * vector_grad
    vector_new = vector_old - VECTOR_RATE * vector_momentum_new
    grad_rows = lax.all_to_all(
        sums_block.reshape(G, count, BLOCK), TEAM, 0, 0, tiled=True
    )
    in_grad, out_grad = rows_of_blocks(grad_rows)
    in_momentum_new = MATRIX_MOMENTUM * in_momentum + in_grad
    out_momentum_new = MATRIX_MOMENTUM * out_momentum + out_grad

    x_all, d_normed_part, mixed_part, vector_grad, in_grad = lax.optimization_barrier(
        (x_all, d_normed_part, mixed_part, vector_grad, in_grad)
    )
    gram_sent = gram(ci == 1, x_all)
    gram_got = lax.ppermute(gram_sent, "c", swap)
    gram_own = gram(after(first, gram_sent), x_all)
    chip_row = (zi * 4 + xi) * team_count + yi * (2 * count)
    pick = (
        lax.broadcasted_iota(jnp.int32, (2 * count, D), 1)
        == lax.broadcasted_iota(jnp.int32, (2 * count, D), 0) + chip_row
    ).astype(F32)
    t_own = chain(gram_own, gram_got, pick)
    d_normed = lax.psum_scatter(d_normed_part, TEAM, scatter_dimension=0, tiled=True)
    mixed = lax.psum_scatter(mixed_part, TEAM, scatter_dimension=0, tiled=True)
    hidden_own = hidden.astype(F32)
    block_output = (hidden_own + mixed).astype(BF16)
    scale_own = lax.rsqrt(jnp.mean(hidden_own * hidden_own, axis=-1, keepdims=True) + EPSILON)
    unit_own = hidden_own * scale_own
    d_unit = d_normed * norm_gain
    d_hidden = scale_own * (
        d_unit - unit_own * jnp.mean(d_unit * unit_own, axis=-1, keepdims=True)
    )
    input_grad = cotangent.astype(F32) + d_hidden

    t_other = lax.ppermute(t_own, "c", swap)
    t_in = jnp.where(first, t_own, t_other)
    t_out = jnp.where(first, t_other, t_own)

    def applied(t, x):
        both = jnp.einsum(
            "rk,ykn->yrn", jnp.concatenate(parts(t), axis=0), x, preferred_element_type=F32
        )
        return both[:, : 2 * count] + both[:, 2 * count :]

    halves = jnp.concatenate(
        [applied(t_in, x_all[:, :, :IN_COLS]), applied(t_out, x_all[:, :, IN_COLS:])], axis=2
    )
    half_own = lax.dynamic_slice_in_dim(halves, ci * count, count, 1)
    half_sent = lax.dynamic_slice_in_dim(halves, (1 - ci) * count, count, 1)
    half_got = lax.ppermute(half_sent, "c", swap)
    both = jnp.stack(
        [jnp.where(first, half_own, half_got), jnp.where(first, half_got, half_own)], axis=1
    ).reshape(G, count, BLOCK)
    step_in, step_out = rows_of_blocks(both)
    in_weight_new = in_weight.astype(F32) - MATRIX_RATE * math.sqrt(PROJ / D) * step_in
    out_weight_new = out_weight.astype(F32) - MATRIX_RATE * math.sqrt(E / D) * step_out
    return (
        block_output,
        input_grad,
        in_grad,
        in_momentum_new,
        in_weight_new,
        out_grad,
        out_momentum_new,
        out_weight_new,
        vector_grad,
        vector_momentum_new,
        vector_new,
    )


def solution(mesh):
    grid = Mesh(mesh.devices.reshape(4, 4, 4, 2), EVERY)
    split = P(EVERY, None)
    return jax.shard_map(
        local,
        mesh=grid,
        in_specs=(
            split,
            P(EVERY),
            P(),
            split,
            P(),
            P(),
            P(),
            P(),
            P(),
            P(),
            split,
            split,
            split,
            split,
            P(),
        ),
        out_specs=(split,) * 8 + (P(),) * 3,
        check_vma=False,
    )
```

```python
import math

import jax
import jax.numpy as jnp
from jax import lax
from jax.experimental import pallas as pl
from jax.experimental.pallas import tpu as pltpu
from jax.sharding import Mesh, PartitionSpec as P

NS_STEPS = 5
EPSILON = 1e-05
NORM_FLOOR = 1e-07
POLY_FIRST = 3.4445
POLY_SECOND = -4.775
POLY_THIRD = 2.0315
MATRIX_MOMENTUM = 0.95
MATRIX_RATE = 0.5
VECTOR_MOMENTUM = 0.9
VECTOR_RATE = 0.05
HIGHEST = lax.Precision.HIGHEST
F32 = jnp.float32
BF16 = jnp.bfloat16

EVERY = ("z", "x", "y", "c")
TEAM = ("y", "c")
ROWS = ("z", "x")

D = 1536
H = 48
HEAD = 64
N = 128
E = 3072
PROJ = 6448
TAPS = 4
G = 8
HG = H // G
EG = E // G
BG = 2 * N // G
TOKENS = 1024
CHUNK = 128
PIECES = TOKENS // CHUNK
AT_ONCE = 4
STEPS = PIECES // AT_ONCE
SPAN = AT_ONCE * CHUNK
EDGE = 16
LANES = 128
VG = EG + 2 * N
IN_COLS = 2 * EG + LANES
BLOCK = IN_COLS + EG
FORWARD_COLS = EG + VG + LANES
LATE_COLS = EG + LANES
STATE_ROWS = N + 8
TILE = 256
AHEAD, KEEP, TAIL, GAIN, SEGMENT = 4, 9, 10, 11, 12


def dot(a, b, dims):
    return lax.dot_general(
        a.astype(BF16), b.astype(BF16), (dims, ((), ())), preferred_element_type=F32
    )


NN = ((1,), (0,))
NT = ((1,), (1,))
TN = ((0,), (0,))


def parts(value):
    top = value.astype(BF16)
    return top, (value - top.astype(F32)).astype(BF16)


def dot3(a, b, dims=NN):
    a_top, a_rest = parts(a)
    b_top, b_rest = parts(b)
    return dot(a_top, b_top, dims) + (dot(a_top, b_rest, dims) + dot(a_rest, b_top, dims))


def lane_of(shape):
    return lax.broadcasted_iota(jnp.int32, shape, 1)


def piece_rows(k, height=CHUNK):
    return pl.ds(k * height, height)


def widen(per_head):
    rows = per_head.shape[0]
    left = lane_of((rows, LANES)) < HEAD
    return jnp.concatenate(
        [
            jnp.where(
                left,
                jnp.broadcast_to(per_head[:, 2 * p : 2 * p + 1], (rows, LANES)),
                jnp.broadcast_to(per_head[:, 2 * p + 1 : 2 * p + 2], (rows, LANES)),
            )
            for p in range(HG // 2)
        ],
        axis=1,
    )


def head_sums(values, summer):
    top, rest = parts(values)
    return dot(top, summer, NN) + dot(rest, summer, NN)


def pair_lanes(p):
    return slice(p * LANES, (p + 1) * LANES)


def stacked_pair(values):
    left = lane_of(values.shape) < HEAD
    zero = jnp.zeros_like(values)
    return jnp.concatenate(
        [jnp.where(left, values, zero), jnp.where(left, zero, values)], axis=0
    )


def running(mask, values):
    top, rest = parts(values)
    least = values - top.astype(F32) - rest.astype(F32)
    return dot(mask, top, NN) + (dot(mask, rest, NN) + dot(mask, least, NN))


def silu_parts(values):
    sig = jax.nn.sigmoid(values)
    return sig, values * sig


def softplus(values):
    return jnp.maximum(values, 0.0) + jnp.log1p(jnp.exp(-jnp.abs(values)))


def square_iota():
    shape = (CHUNK, CHUNK)
    return lax.broadcasted_iota(jnp.int32, shape, 0), lane_of(shape)


def same_document(flags, row):
    return flags[:, SEGMENT : SEGMENT + 1] == row


def in_order(core_ref, own_ref, other_ref):
    own, other = own_ref[0], other_ref[0]
    first = core_ref[1] == 0
    return jnp.concatenate(
        [jnp.where(first, own, other), jnp.where(first, other, own)], axis=0
    )


def project_kernel(
    core_ref, own_ref, other_ref, edge_ref, w_ref, gain_ref, normed_ref, z_ref, v_ref, r_ref
):
    def put(x, at):
        x = x.astype(F32)
        scale = lax.rsqrt(jnp.mean(x * x, axis=1, keepdims=True) + EPSILON)
        normed = (x * scale * gain_ref[...]).astype(BF16)
        normed_ref[at, :] = normed
        out = jnp.dot(normed, w_ref[...], preferred_element_type=F32)
        z_ref[at, :] = out[:, :EG]
        v_ref[at, :] = out[:, EG : EG + VG]
        r_ref[at, :] = out[:, EG + VG :]

    last = pl.num_programs(0) - 1

    @pl.when(pl.program_id(0) < last)
    def _():
        put(in_order(core_ref, own_ref, other_ref), pl.ds(0, 2 * CHUNK))

    @pl.when(pl.program_id(0) == last)
    def _():
        put(edge_ref[...], pl.ds(0, EDGE))


def incoming_kernel(core_ref, own_ref, other_ref, w_ref, q_ref, d_gated_ref):
    q = in_order(core_ref, own_ref, other_ref)
    q_ref[...] = q
    d_gated_ref[...] = jnp.dot(q, w_ref[...], preferred_element_type=F32)


def early_kernel(normed_ref, q_ref, dz_ref, gated_ref, out_ref):
    out_ref[:, :EG] = dot(normed_ref[0:TOKENS, :], dz_ref[...], TN).astype(BF16)
    out_ref[:, EG:] = dot(q_ref[...], gated_ref[...], TN).astype(BF16)


def forward_kernel(
    v_ref,
    before_ref,
    r_ref,
    flags_ref,
    ids_ref,
    taps_ref,
    head_ref,
    conv_ref,
    dt_ref,
    cum_ref,
    y_ref,
    start_ref,
    reach_ref,
    gain_ref,
    packed_ref,
    state,
    reach,
):
    step = pl.program_id(0)

    @pl.when(step == 0)
    def _():
        state[...] = jnp.zeros_like(state)
        reach[...] = jnp.ones_like(reach)

    for k in range(AT_ONCE):
        c = step * AT_ONCE + k
        at, at8 = piece_rows(k), piece_rows(k, 8)
        flags = flags_ref[at, :]
        window = jnp.concatenate([before_ref[...] if k == 0 else v_ref[pl.ds(k * CHUNK - 8, 8), :], v_ref[at, :]], axis=0)
        conv = taps_ref[TAPS : TAPS + 1, :] + taps_ref[0:1, :] * window[8:]
        for lag in range(1, TAPS):
            conv = conv + taps_ref[lag : lag + 1, :] * (
                pltpu.roll(window, lag, 0)[8:] * flags[:, lag : lag + 1]
            )
        conv_ref[at, :] = conv
        act = conv * jax.nn.sigmoid(conv)
        xs, bm, cm = act[:, :EG], act[:, EG : EG + N], act[:, EG + N :]
        dt = softplus(r_ref[at, :] + head_ref[0:1, :])
        dt_ref[at, :] = dt
        ti, si = square_iota()
        lower = (ti >= si).astype(F32)
        cum = running(lower, -head_ref[1:2, :] * dt)
        cum_ref[at, :] = cum
        cum_t = cum.T
        last = cum[CHUNK - 1 : CHUNK, :]
        tail = jnp.exp(last - cum) * flags[:, TAIL : TAIL + 1]
        carry = jnp.exp(cum) * flags[:, KEEP : KEEP + 1]
        gain = widen(jnp.exp(last) * flags[0:1, GAIN : GAIN + 1])
        xdt = xs * widen(dt)
        scores = dot3(cm, bm, NT)
        mask = (ti >= si) & same_document(flags, ids_ref[pl.ds(c, 1), :])
        within = []
        for p in range(HG // 2):
            mix = [
                jnp.exp(jnp.where(mask, cum[:, h : h + 1] - cum_t[h : h + 1, :], -1e30)) * scores
                for h in (2 * p, 2 * p + 1)
            ]
            within.append(
                dot3(jnp.concatenate(mix, axis=1), stacked_pair(xdt[:, pair_lanes(p)]))
            )
        y_ref[at, :] = jnp.concatenate(within, axis=1) + widen(carry) * dot3(cm, state[...])
        start_ref[k] = state[...]
        reach_ref[at8, :] = reach[...]
        gain_ref[at8, :] = jnp.broadcast_to(gain, (8, EG))
        state[...] = gain * state[...] + dot3(bm.T, xdt * widen(tail))
        reach[...] = gain * reach[...]

    @pl.when(step == STEPS - 1)
    def _():
        packed_ref[0:N, :] = state[...]
        packed_ref[N:, :] = reach[...]


def joined_states(first, second, third):
    return first[:N] + first[N : N + 1] * (second[:N] + second[N : N + 1] * third[:N])


def output_kernel(
    y_part_ref,
    conv_ref,
    cum_ref,
    flags_ref,
    z_ref,
    d_gated_ref,
    reach_ref,
    first_ref,
    second_ref,
    third_ref,
    rows_ref,
    y_ref,
    sums_ref,
    arrived_ref,
):
    step = pl.program_id(0)

    @pl.when(step == 0)
    def _():
        arrived_ref[...] = joined_states(first_ref[...], second_ref[...], third_ref[...])

    for k in range(AT_ONCE):
        c = step * AT_ONCE + k
        at = piece_rows(k)
        conv = conv_ref[at, :]
        act = conv * jax.nn.sigmoid(conv)
        carry = widen(jnp.exp(cum_ref[at, :]) * flags_ref[at, KEEP : KEEP + 1]) * reach_ref[pl.ds(8 * k, 1), :]
        y = (
            y_part_ref[at, :]
            + carry * dot3(act[:, EG + N :], arrived_ref[...])
            + rows_ref[0:1, :] * act[:, :EG]
        )
        y_ref[at, :] = y
        _, silu_z = silu_parts(z_ref[at, :])
        g = y * silu_z
        squares = jnp.sum(g * g, axis=1, keepdims=True)
        inner = jnp.sum(d_gated_ref[at, :] * rows_ref[1:2, :] * g, axis=1, keepdims=True)
        lane = lane_of((CHUNK, LANES))
        turned = jnp.where(lane == 0, squares, jnp.where(lane == 1, inner, 0.0)).T
        sums_ref[pl.ds(c, 1), :] = turned[0:1, :]
        sums_ref[pl.ds(PIECES + c, 1), :] = turned[1:2, :]


def gate_kernel(
    y_ref,
    z_ref,
    d_gated_ref,
    conv_ref,
    cum_ref,
    flags_ref,
    gain_ref,
    sums_ref,
    rows_ref,
    gated_ref,
    dz_ref,
    dy_ref,
    end_ref,
    reach_ref,
    d_gate_ref,
    packed_ref,
    state,
    reach,
):
    step = STEPS - 1 - pl.program_id(0)

    @pl.when(step == STEPS - 1)
    def _():
        state[...] = jnp.zeros_like(state)
        reach[...] = jnp.ones_like(reach)
        d_gate_ref[...] = jnp.zeros_like(d_gate_ref)

    for k in reversed(range(AT_ONCE)):
        c = step * AT_ONCE + k
        at, at8 = piece_rows(k), piece_rows(k, 8)
        ti, _ = square_iota()
        turned = jnp.where(
            ti == 0,
            sums_ref[pl.ds(c, 1), :],
            jnp.where(ti == 1, sums_ref[pl.ds(PIECES + c, 1), :], 0.0),
        ).T
        root = lax.rsqrt(turned[:, 0:1] * (1.0 / E) + EPSILON)
        slope = turned[:, 1:2] * (root * root * root) * (1.0 / E)
        gate = rows_ref[1:2, :]
        y = y_ref[at, :]
        sig, silu_z = silu_parts(z_ref[at, :])
        g = y * silu_z
        unit = g * root
        gated_ref[at, :] = (unit * gate).astype(BF16)
        d_gated = d_gated_ref[at, :]
        d_gate_ref[0:1, :] += jnp.sum(d_gated * unit, axis=0, keepdims=True)
        d_g = root * (d_gated * gate) - g * slope
        dy = d_g * silu_z
        dz_ref[at, :] = (d_g * y * (sig + silu_z * (1.0 - sig))).astype(BF16)
        dy_ref[at, :] = dy
        conv = conv_ref[at, EG + N :]
        cm = conv * jax.nn.sigmoid(conv)
        carry = widen(jnp.exp(cum_ref[at, :]) * flags_ref[at, KEEP : KEEP + 1])
        end_ref[k] = state[...]
        reach_ref[at8, :] = reach[...]
        gain = gain_ref[pl.ds(8 * k, 1), :]
        state[...] = gain * state[...] + dot3(cm.T, dy * carry)
        reach[...] = gain * reach[...]

    @pl.when(step == 0)
    def _():
        packed_ref[0:N, :] = state[...]
        packed_ref[N:, :] = reach[...]


def inner_kernel(dy_ref, conv_ref, dt_ref, cum_ref, flags_ref, ids_ref, u_ref, d_bc_ref):
    for k in range(AT_ONCE):
        c = pl.program_id(0) * AT_ONCE + k
        at = piece_rows(k)
        flags = flags_ref[at, :]
        conv = conv_ref[at, :]
        act = conv * jax.nn.sigmoid(conv)
        xs, bm, cm = act[:, :EG], act[:, EG : EG + N], act[:, EG + N :]
        cum = cum_ref[at, :]
        cum_t = cum.T
        dy = dy_ref[at, :]
        xdt = xs * widen(dt_ref[at, :])
        scores_t = dot3(bm, cm, NT)
        ti, si = square_iota()
        same = same_document(flags, ids_ref[pl.ds(c, 1), :])
        mask = (ti >= si) & same
        mask_t = (ti <= si) & same
        d_scores = jnp.zeros((CHUNK, CHUNK), F32)
        u = []
        for p in range(HG // 2):
            own = stacked_pair(dy[:, pair_lanes(p)])
            pairs = dot3(own, xdt[:, pair_lanes(p)], NT)
            mix_t = []
            for k in range(2):
                h = 2 * p + k
                gap = cum[:, h : h + 1] - cum_t[h : h + 1, :]
                d_scores = d_scores + jnp.exp(jnp.where(mask, gap, -1e30)) * (
                    pairs[k * CHUNK : (k + 1) * CHUNK]
                )
                mix_t.append(jnp.exp(jnp.where(mask_t, -gap, -1e30)) * scores_t)
            u.append(dot(jnp.concatenate(mix_t, axis=1), own, NN))
        u_ref[at, :] = jnp.concatenate(u, axis=1)
        d_bc_ref[at, :N] = dot3(d_scores.T, cm)
        d_bc_ref[at, N:] = dot3(d_scores, bm)


def backward_kernel(
    core_ref,
    u_ref,
    d_bc_ref,
    dy_ref,
    y_ref,
    conv_ref,
    dt_ref,
    cum_ref,
    r_ref,
    flags_ref,
    start_ref,
    reach_ref,
    arrived_ref,
    end_ref,
    reach_back_ref,
    first_ref,
    second_ref,
    third_ref,
    final_ref,
    v_ref,
    before_ref,
    rows_ref,
    taps_ref,
    head_ref,
    summer_ref,
    edge_flags_ref,
    dv_ref,
    d_edge_ref,
    kept_ref,
    sent_ref,
    dr_ref,
    wide_ref,
    heads_ref,
    following,
    flowing,
    adjoint_in,
):
    step = STEPS - 1 - pl.program_id(0)
    summer = summer_ref[...]

    @pl.when(step == STEPS - 1)
    def _():
        adjoint = joined_states(first_ref[...], second_ref[...], third_ref[...])
        adjoint_in[...] = adjoint
        final = final_ref[0:N, :] + final_ref[N : N + 1, :] * arrived_ref[...]
        inner = jnp.sum(adjoint * final, axis=0, keepdims=True)
        flowing[...] = head_sums(jnp.broadcast_to(inner, (8, EG)), summer)
        following[...] = jnp.zeros_like(following)
        wide_ref[...] = jnp.zeros_like(wide_ref)
        heads_ref[...] = jnp.zeros_like(heads_ref)

    for k in reversed(range(AT_ONCE)):
        at = piece_rows(k)
        flags = flags_ref[at, :]
        conv = conv_ref[at, :]
        sig, act = silu_parts(conv)
        xs, bm = act[:, :EG], act[:, EG : EG + N]
        cum = cum_ref[at, :]
        dt = dt_ref[at, :]
        dy = dy_ref[at, :]
        skip = rows_ref[0:1, :]
        rate = head_ref[1:2, :]
        last = cum[CHUNK - 1 : CHUNK, :]
        tail = widen(jnp.exp(last - cum) * flags[:, TAIL : TAIL + 1])
        carry = widen(jnp.exp(cum) * flags[:, KEEP : KEEP + 1])
        dt_wide = widen(dt)
        start = start_ref[k] + reach_ref[pl.ds(8 * k, 1), :] * arrived_ref[...]
        adjoint = end_ref[k] + reach_back_ref[pl.ds(8 * k, 1), :] * adjoint_in[...]
        u = u_ref[at, :] + tail * dot3(bm, adjoint)
        d_xs = u * dt_wide + skip * dy
        d_dt = head_sums(xs * u, summer)
        d_bm = d_bc_ref[at, :N] + dot3(xs * dt_wide * tail, adjoint, NT)
        d_cm = d_bc_ref[at, N:] + dot3(dy * carry, start, NT)
        turned = jnp.concatenate([d_bm.T, d_cm.T], axis=0)
        of_core = [
            jnp.concatenate(
                [turned[(2 * y + c) * BG : (2 * y + c + 1) * BG] for y in range(G // 2)], axis=0
            )
            for c in range(2)
        ]
        first = core_ref[1] == 0
        kept_ref[:, at] = jnp.where(first, of_core[0], of_core[1])
        sent_ref[:, at] = jnp.where(first, of_core[1], of_core[0])
        flow = head_sums(dy * (y_ref[at, :] - skip * xs), summer) - dt * d_dt
        ti, si = square_iota()
        upper = (si >= ti).astype(F32)
        d_la = running(upper, flow) + flowing[0:1, :]
        flowing[...] = jnp.broadcast_to(d_la[0:1, :], flowing.shape)
        d_la = d_la * flags[:, 1:2]
        d_r = (d_dt - rate * d_la) * jax.nn.sigmoid(r_ref[at, :] + head_ref[0:1, :])
        dr_ref[at, :] = d_r
        heads_ref[0:1, :] += jnp.sum(d_r, axis=0, keepdims=True)
        heads_ref[1:2, :] += jnp.sum(d_la * (-rate * dt), axis=0, keepdims=True)
        heads_ref[2:3, :] += jnp.sum(head_sums(dy * xs, summer), axis=0, keepdims=True)

        sig, conv = sig[:, :EG], conv[:, :EG]
        d_conv = d_xs * (sig + conv * sig * (1.0 - sig))
        window = jnp.concatenate([before_ref[...] if k == 0 else v_ref[pl.ds(k * CHUNK - 8, 8), :], v_ref[at, :]], axis=0)
        ahead = jnp.concatenate([d_conv, following[...]], axis=0)
        wide_ref[0:1, :] += jnp.sum(d_conv * window[8:], axis=0, keepdims=True)
        wide_ref[TAPS : TAPS + 1, :] += jnp.sum(d_conv, axis=0, keepdims=True)
        dv = taps_ref[0:1, :EG] * d_conv
        for lag in range(1, TAPS):
            wide_ref[lag : lag + 1, :] += jnp.sum(
                d_conv * pltpu.roll(window, lag, 0)[8:] * flags[:, lag : lag + 1],
                axis=0,
                keepdims=True,
            )
            dv = dv + taps_ref[lag : lag + 1, :EG] * (
                pltpu.roll(ahead, CHUNK + 8 - lag, 0)[:CHUNK] * flags[:, AHEAD + lag : AHEAD + lag + 1]
            )
        dv_ref[at, :] = dv.astype(BF16)
        following[...] = d_conv[0:8]

    @pl.when(step == 0)
    def _():
        d_edge_ref[...] = edge_rows(following[...], taps_ref[:, :EG], edge_flags_ref[...])


def edge_rows(d_conv, taps, flags):
    zero = jnp.zeros_like(d_conv)
    ahead = jnp.concatenate([zero, d_conv], axis=0)
    total = zero
    for lag in range(1, TAPS):
        total = total + taps[lag : lag + 1, :] * (
            pltpu.roll(ahead, EDGE - lag, 0)[0:8] * flags[:, AHEAD + lag : AHEAD + lag + 1]
        )
    return jnp.concatenate([zero, total], axis=0).astype(BF16)


def shared_kernel(
    team_ref,
    got_refs,
    conv_b_ref,
    conv_c_ref,
    v_b_ref,
    v_c_ref,
    before_b_ref,
    before_c_ref,
    dr_ref,
    dv_ref,
    d_edge_ref,
    flags_ref,
    edge_flags_ref,
    taps_ref,
    late_ref,
    wide_ref,
    following,
):
    step = pl.program_id(0)
    turn = (2 * N - BG * team_ref[0]) % (2 * N)

    def own(b, c):
        return pltpu.roll(jnp.concatenate([b, c], axis=1), turn, 1)[:, :LANES]

    def before(k):
        if k == 0:
            return own(before_b_ref[...], before_c_ref[...])
        last = pl.ds(k * CHUNK - 8, 8)
        return own(v_b_ref[last, :], v_c_ref[last, :])

    @pl.when(step == 0)
    def _():
        following[...] = jnp.zeros_like(following)
        wide_ref[...] = jnp.zeros_like(wide_ref)

    def piece(k):
        at = piece_rows(k)
        flags = flags_ref[at, :]
        total = sum(ref[:, at] for ref in got_refs)
        d_act = jnp.concatenate([total, jnp.zeros((LANES - BG, CHUNK), F32)], axis=0).T
        conv = own(conv_b_ref[at, :], conv_c_ref[at, :])
        sig = jax.nn.sigmoid(conv)
        d_conv = d_act * (sig + conv * sig * (1.0 - sig))
        window = jnp.concatenate(
            [before(k), own(v_b_ref[at, :], v_c_ref[at, :])], axis=0
        )
        ahead = jnp.concatenate([d_conv, following[...]], axis=0)
        wide_ref[0:1, :] += jnp.sum(d_conv * window[8:], axis=0, keepdims=True)
        wide_ref[TAPS : TAPS + 1, :] += jnp.sum(d_conv, axis=0, keepdims=True)
        dv = taps_ref[0:1, :] * d_conv
        for lag in range(1, TAPS):
            wide_ref[lag : lag + 1, :] += jnp.sum(
                d_conv * pltpu.roll(window, lag, 0)[8:] * flags[:, lag : lag + 1],
                axis=0,
                keepdims=True,
            )
            dv = dv + taps_ref[lag : lag + 1, :] * (
                pltpu.roll(ahead, CHUNK + 8 - lag, 0)[:CHUNK]
                * flags[:, AHEAD + lag : AHEAD + lag + 1]
            )
        following[...] = d_conv[0:8]
        late_ref[at, :EG] = dv_ref[at, :]
        late_ref[at, EG:] = (dv + pltpu.roll(dr_ref[at, :], BG, 1)).astype(BF16)

    @pl.when(step < STEPS)
    def _():
        for k in reversed(range(AT_ONCE)):
            piece(k)

    @pl.when(step == STEPS)
    def _():
        late_ref[0:EDGE, :EG] = d_edge_ref[...]
        late_ref[0:EDGE, EG:] = edge_rows(following[...], taps_ref[...], edge_flags_ref[...])


def finish_kernel(hidden_ref, cotangent_ref, d_normed_ref, mixed_ref, gain_ref, out_ref, grad_ref):
    x = hidden_ref[...].astype(F32)
    scale = lax.rsqrt(jnp.mean(x * x, axis=1, keepdims=True) + EPSILON)
    unit = x * scale
    d_unit = d_normed_ref[...] * gain_ref[...]
    inner = jnp.mean(d_unit * unit, axis=1, keepdims=True)
    grad_ref[...] = cotangent_ref[...].astype(F32) + scale * (d_unit - unit * inner)
    out_ref[...] = (x + mixed_ref[...]).astype(BF16)


def triangle(n):
    return [(i, j) for i in range(n // TILE) for j in range(i, n // TILE)]


def solve_kernel(
    which_ref, x_ref, pick_ref, out_ref, total, high, low, h_high, h_low, q_ref, sems
):
    pieces = x_ref.shape[0]
    slots = q_ref.shape[0]
    n = high.shape[0]
    count = n // TILE
    order = triangle(n)

    def at(i):
        return pl.ds(i * TILE, TILE) if isinstance(i, int) else pl.ds(pl.multiple_of(i * TILE, TILE), TILE)

    def times(a, b):
        return jnp.dot(a, b, preferred_element_type=F32)

    def arriving(y, slot, columns):
        width = columns.stop - columns.start
        return pltpu.make_async_copy(
            x_ref.at[y, :, columns], q_ref.at[slot, :, pl.ds(0, width)], sems.at[slot]
        )

    def gram(columns):
        width = columns.stop - columns.start
        for slot in range(slots):
            arriving(slot, slot, columns).start()

        def two(step, _):
            slot = 2 * (step % (slots // 2))
            for k in range(2):
                arriving(2 * step + k, slot + k, columns).wait()

            def taken(rows):
                return jnp.concatenate(
                    [q_ref[slot, rows, :width], q_ref[slot + 1, rows, :width]], axis=1
                )

            for i in range(count):
                product = dot(taken(at(i)), taken(pl.ds(i * TILE, n - i * TILE)), NT)
                for j in range(i, count):
                    b = order.index((i, j))
                    total[b] = total[b] + product[:, (j - i) * TILE : (j - i + 1) * TILE]

            @pl.when(step < (pieces - slots) // 2)
            def _():
                for k in range(2):
                    arriving(2 * step + slots + k, slot + k, columns).start()

            return 0

        lax.fori_loop(0, pieces // 2, two, 0)

    def apply(columns, t):
        width = columns.stop - columns.start
        both = jnp.concatenate(parts(t), axis=0)
        for slot in range(slots):
            arriving(slot, slot, columns).start()

        def one(y, _):
            slot = y % slots
            arriving(y, slot, columns).wait()
            product = times(both, q_ref[slot, :, :width])
            out_ref[y, :, :width] = product[: t.shape[0]] + product[t.shape[0] :]

            @pl.when(y < pieces - slots)
            def _():
                arriving(y + slots, slot, columns).start()

            return 0

        lax.fori_loop(0, pieces, one, 0)

    total[...] = jnp.zeros_like(total)
    out_ref[...] = jnp.zeros_like(out_ref)

    @pl.when(which_ref[0] == 1)
    def _():
        gram(slice(0, IN_COLS))

    @pl.when(which_ref[0] != 1)
    def _():
        gram(slice(IN_COLS, BLOCK))

    diagonal = lax.broadcasted_iota(jnp.int32, (TILE, TILE), 0) == lax.broadcasted_iota(jnp.int32, (TILE, TILE), 1)
    square = jnp.zeros((1, 1), F32)
    for b, (i, j) in enumerate(order):
        if i == j:
            square = square + jnp.sum(jnp.where(diagonal, total[b], 0.0), keepdims=True)
    inverse = 1.0 / (jnp.sqrt(square) + NORM_FLOOR)
    scale = inverse * inverse

    def put(value, i, j, top_ref, rest_ref):
        top = value.astype(BF16)
        top_ref[at(i), at(j)] = top
        if i != j:
            top_ref[at(j), at(i)] = top.T
        if rest_ref is not None:
            rest_ref[at(i), at(j)] = (value - top.astype(F32)).astype(BF16)

    def put_row(value, i, top_ref, rest_ref):
        for j in range(i, count):
            put(value[:, (j - i) * TILE : (j - i + 1) * TILE], i, j, top_ref, rest_ref)

    for b, (i, j) in enumerate(order):
        put(total[b] * scale, i, j, high, low)

    def polynomial(q):
        for i in range(count):
            rest = pl.ds(i * TILE, n - i * TILE)
            value = times(high[at(i), :], high[:, rest])
            put_row(POLY_SECOND * high[at(i), rest].astype(F32) + POLY_THIRD * value, i, q, None)

    def whole(top_ref, rest_ref, i, rest):
        return top_ref[at(i), rest].astype(F32) + rest_ref[at(i), rest].astype(F32)

    def iterate(step, _):
        q = q_ref.at[step]
        polynomial(q)
        for i in range(count):
            rest = pl.ds(i * TILE, n - i * TILE)
            value = times(q[at(i), :], high[:, rest]) + POLY_FIRST * whole(high, low, i, rest)
            put_row(value, i, h_high, h_low)
        for i in range(count):
            rest = pl.ds(i * TILE, n - i * TILE)
            value = times(h_high[at(i), :], q[:, rest]) + POLY_FIRST * whole(h_high, h_low, i, rest)
            put_row(value, i, high, low)
        return 0

    def thin(t, matrix):
        top, rest = parts(t)
        both = times(jnp.concatenate([top, rest], axis=0), matrix)
        return both[: t.shape[0]] + both[t.shape[0] :]

    def multiplied(t, step):
        return POLY_FIRST * t + thin(t, q_ref[step])

    def last_gram(t):
        return multiplied(thin(multiplied(t, NS_STEPS - 2), high[...]), NS_STEPS - 2)

    lax.fori_loop(0, NS_STEPS - 2, iterate, 0)
    polynomial(q_ref.at[NS_STEPS - 2])
    pick = pick_ref[...]
    once = last_gram(pick)
    t = POLY_FIRST * pick + POLY_SECOND * once + POLY_THIRD * last_gram(once)
    for step in reversed(range(NS_STEPS - 1)):
        t = multiplied(t, step)
    t = t * inverse

    @pl.when(which_ref[0] == 1)
    def _():
        apply(slice(0, IN_COLS), t)

    @pl.when(which_ref[0] != 1)
    def _():
        apply(slice(IN_COLS, BLOCK), t)


SMALL = pltpu.CompilerParams(vmem_limit_bytes=20 << 20)
LARGE = pltpu.CompilerParams(vmem_limit_bytes=60 << 20)


def spec(shape, index=None):
    return pl.BlockSpec(shape, index if index is not None else (lambda c: (0,) * len(shape)))


def rows(width, height=SPAN):
    return spec((height, width), lambda c: (c, 0))


def rows_back(width, height=SPAN):
    return spec((height, width), lambda c: (STEPS - 1 - c, 0))


def previous(c):
    return jnp.where(c == 0, (TOKENS + EDGE) // 8 - 1, c * (SPAN // 8) - 1)


def shaped(*shape, dtype=F32):
    return jax.ShapeDtypeStruct(shape, dtype)


def cost(flops, moved):
    return pl.CostEstimate(flops=flops, bytes_accessed=moved, transcendentals=0)


def piece_of(kind):
    size = 4

    def index(c, place):
        return ((place[0] - jnp.minimum(c, size - 1) + size) % size, 0, 0)

    return pl.BlockSpec((1, CHUNK, D), index)


def project(place, own, other, edge, weights, gain):
    total = TOKENS + EDGE
    block = 2 * CHUNK

    def out(width):
        return pl.BlockSpec((block, width), lambda c, place: (c, 0))

    def whole(*shape):
        return pl.BlockSpec(shape, lambda c, place: (0, 0))

    return pl.pallas_call(
        project_kernel,
        grid_spec=pltpu.PrefetchScalarGridSpec(
            num_scalar_prefetch=1,
            grid=(TOKENS // block + 1,),
            in_specs=[
                piece_of("own"),
                piece_of("other"),
                whole(EDGE, D),
                whole(D, FORWARD_COLS),
                whole(1, D),
            ],
            out_specs=[out(D), out(EG), out(VG), out(LANES)],
        ),
        out_shape=[
            shaped(total, D, dtype=BF16),
            shaped(total, EG),
            shaped(total, VG),
            shaped(total, LANES),
        ],
        compiler_params=SMALL,
        cost_estimate=cost(2 * total * D * FORWARD_COLS, 16 << 20),
        name="project",
    )(place, own, other, edge, weights, gain)


def incoming(place, own, other, weights):
    block = 2 * CHUNK

    def out(width):
        return pl.BlockSpec((block, width), lambda c, place: (c, 0))

    return pl.pallas_call(
        incoming_kernel,
        grid_spec=pltpu.PrefetchScalarGridSpec(
            num_scalar_prefetch=1,
            grid=(TOKENS // block,),
            in_specs=[
                piece_of("own"),
                piece_of("other"),
                pl.BlockSpec((D, EG), lambda c, place: (0, FORWARD_COLS // EG)),
            ],
            out_specs=[out(D), out(EG)],
        ),
        out_shape=[shaped(TOKENS, D, dtype=BF16), shaped(TOKENS, EG)],
        compiler_params=SMALL,
        cost_estimate=cost(2 * TOKENS * D * EG, 9 << 20),
        name="incoming",
    )(place, own, other, weights)


def early_products(normed, q, dz, gated):
    return pl.pallas_call(
        early_kernel,
        grid=(D // TILE,),
        in_specs=[
            spec((TOKENS + EDGE, TILE), lambda c: (0, c)),
            spec((TOKENS, TILE), lambda c: (0, c)),
            spec((TOKENS, EG)),
            spec((TOKENS, EG)),
        ],
        out_specs=rows(2 * EG, TILE),
        out_shape=shaped(D, 2 * EG, dtype=BF16),
        compiler_params=SMALL,
        cost_estimate=cost(4 * TOKENS * D * EG, 13 << 20),
        name="early",
    )(normed, q, dz, gated)


def forward(v, r, flags, ids, taps, head):
    return pl.pallas_call(
        forward_kernel,
        grid=(STEPS,),
        in_specs=[
            rows(VG),
            spec((8, VG), lambda c: (previous(c), 0)),
            rows(LANES),
            rows(LANES),
            spec((8, LANES)),
            spec((8, VG)),
            spec((8, LANES)),
        ],
        out_specs=[
            rows(VG),
            rows(LANES),
            rows(LANES),
            rows(EG),
            spec((AT_ONCE, N, EG), lambda c: (c, 0, 0)),
            rows(EG, 8 * AT_ONCE),
            rows(EG, 8 * AT_ONCE),
            spec((STATE_ROWS, EG)),
        ],
        out_shape=[
            shaped(TOKENS, VG),
            shaped(TOKENS, LANES),
            shaped(TOKENS, LANES),
            shaped(TOKENS, EG),
            shaped(PIECES, N, EG),
            shaped(PIECES * 8, EG),
            shaped(PIECES * 8, EG),
            shaped(STATE_ROWS, EG),
        ],
        scratch_shapes=[pltpu.VMEM((N, EG), F32), pltpu.VMEM((8, EG), F32)],
        compiler_params=SMALL,
        cost_estimate=cost(3 << 30, 14 << 20),
        name="forward",
    )(v, v, r, flags, ids, taps, head)


def outputs(y_part, conv, cum, flags, z, d_gated, reach, arrivals, wide):
    return pl.pallas_call(
        output_kernel,
        grid=(STEPS,),
        in_specs=[rows(EG), rows(VG), rows(LANES), rows(LANES), rows(EG), rows(EG), rows(EG, 8 * AT_ONCE)]
        + [spec((STATE_ROWS, EG))] * 3
        + [spec((8, EG))],
        out_specs=[rows(EG), spec((2 * PIECES, LANES)), spec((N, EG))],
        out_shape=[shaped(TOKENS, EG), shaped(2 * PIECES, LANES), shaped(N, EG)],
        compiler_params=SMALL,
        cost_estimate=cost(1 << 28, 12 << 20),
        name="outputs",
    )(y_part, conv, cum, flags, z, d_gated, reach, *arrivals, wide)


def gate(y, z, d_gated, conv, cum, flags, gain, sums, wide):
    return pl.pallas_call(
        gate_kernel,
        grid=(STEPS,),
        in_specs=[rows_back(EG)] * 3
        + [rows_back(VG), rows_back(LANES), rows_back(LANES), rows_back(EG, 8 * AT_ONCE)]
        + [spec((2 * PIECES, LANES)), spec((8, EG))],
        out_specs=[rows_back(EG)] * 3
        + [
            spec((AT_ONCE, N, EG), lambda c: (STEPS - 1 - c, 0, 0)),
            rows_back(EG, 8 * AT_ONCE),
            spec((8, EG)),
            spec((STATE_ROWS, EG)),
        ],
        out_shape=[
            shaped(TOKENS, EG, dtype=BF16),
            shaped(TOKENS, EG, dtype=BF16),
            shaped(TOKENS, EG),
            shaped(PIECES, N, EG),
            shaped(PIECES * 8, EG),
            shaped(8, EG),
            shaped(STATE_ROWS, EG),
        ],
        scratch_shapes=[pltpu.VMEM((N, EG), F32), pltpu.VMEM((8, EG), F32)],
        compiler_params=SMALL,
        cost_estimate=cost(1 << 28, 14 << 20),
        name="gate",
    )(y, z, d_gated, conv, cum, flags, gain, sums, wide)


def inner(dy, conv, dt, cum, flags, ids):
    return pl.pallas_call(
        inner_kernel,
        grid=(STEPS,),
        in_specs=[rows(EG), rows(VG), rows(LANES), rows(LANES), rows(LANES), spec((8, LANES))],
        out_specs=[rows(EG), rows(2 * N)],
        out_shape=[shaped(TOKENS, EG), shaped(TOKENS, 2 * N)],
        compiler_params=SMALL,
        cost_estimate=cost(3 << 30, 9 << 20),
        name="inner",
    )(dy, conv, dt, cum, flags, ids)


def backward(
    place, u, d_bc, dy, y, conv, dt, cum, r, flags, starts, reach, arrived, ends, reach_back, arrivals,
    final, v, wide, taps, head, summer, edge_flags,
):
    def back_state():
        return spec((AT_ONCE, N, EG), lambda c: (STEPS - 1 - c, 0, 0))

    return pl.pallas_call(
        backward_kernel,
        grid=(STEPS,),
        in_specs=[
            pl.BlockSpec(memory_space=pltpu.SMEM),
            rows_back(EG),
            rows_back(2 * N),
            rows_back(EG),
            rows_back(EG),
            rows_back(VG),
            rows_back(LANES),
            rows_back(LANES),
            rows_back(LANES),
            rows_back(LANES),
            back_state(),
            rows_back(EG, 8 * AT_ONCE),
            spec((N, EG)),
            back_state(),
            rows_back(EG, 8 * AT_ONCE),
        ]
        + [spec((STATE_ROWS, EG))] * 4
        + [
            rows_back(EG),
            spec((8, EG), lambda c: (previous(STEPS - 1 - c), 0)),
            spec((8, EG)),
            spec((8, VG)),
            spec((8, LANES)),
            spec((EG, LANES)),
            spec((8, LANES)),
        ],
        out_specs=[
            rows_back(EG),
            spec((EDGE, EG)),
            spec((N, SPAN), lambda c: (0, STEPS - 1 - c)),
            spec((N, SPAN), lambda c: (0, STEPS - 1 - c)),
            rows_back(LANES),
            spec((8, EG)),
            spec((8, LANES)),
        ],
        out_shape=[
            shaped(TOKENS, EG, dtype=BF16),
            shaped(EDGE, EG, dtype=BF16),
            shaped(N, TOKENS),
            shaped(N, TOKENS),
            shaped(TOKENS, LANES),
            shaped(8, EG),
            shaped(8, LANES),
        ],
        scratch_shapes=[
            pltpu.VMEM((8, EG), F32),
            pltpu.VMEM((8, LANES), F32),
            pltpu.VMEM((N, EG), F32),
        ],
        compiler_params=SMALL,
        cost_estimate=cost(3 << 29, 20 << 20),
        name="backward",
    )(
        place, u, d_bc, dy, y, conv, dt, cum, r, flags, starts, reach, arrived, ends, reach_back,
        *arrivals, final, v, v, wide, taps, head, summer, edge_flags,
    )


def shared(team, got, conv, v, dr, dv, d_edge, flags, edge_flags, taps):
    def turned(step):
        return jnp.maximum(STEPS - 1 - step, 0)

    def lanes_of(block):
        return spec((SPAN, LANES), lambda c: (turned(c), block))

    def before(block):
        return spec((8, LANES), lambda c: (previous(turned(c)), block))

    b, c_block = EG // LANES, EG // LANES + 1
    def kernel(team_ref, a, b, c, d, *refs):
        shared_kernel(team_ref, (a, b, c, d), *refs)

    return pl.pallas_call(
        kernel,
        grid=(STEPS + 1,),
        in_specs=[
            pl.BlockSpec(memory_space=pltpu.SMEM),
            *[spec((BG, SPAN), lambda c: (0, turned(c)))] * 4,
            lanes_of(b),
            lanes_of(c_block),
            lanes_of(b),
            lanes_of(c_block),
            before(b),
            before(c_block),
            lanes_of(0),
            spec((SPAN, EG), lambda c: (turned(c), 0)),
            spec((EDGE, EG)),
            lanes_of(0),
            spec((8, LANES)),
            spec((8, LANES)),
        ],
        out_specs=[
            spec((SPAN, LATE_COLS), lambda c: (jnp.where(c == STEPS, STEPS, turned(c)), 0)),
            spec((8, LANES)),
        ],
        out_shape=[shaped(TOKENS + EDGE, LATE_COLS, dtype=BF16), shaped(8, LANES)],
        scratch_shapes=[pltpu.VMEM((8, LANES), F32)],
        compiler_params=SMALL,
        cost_estimate=cost(1 << 27, 6 << 20),
        name="shared",
    )(team, *got, conv, conv, v, v, v, v, dr, dv, d_edge, flags, edge_flags, taps)


def finish(hidden, cotangent, d_normed, mixed, gain):
    count = hidden.shape[0]
    return pl.pallas_call(
        finish_kernel,
        grid=(2,),
        in_specs=[rows(D, count // 2)] * 4 + [spec((1, D))],
        out_specs=[rows(D, count // 2)] * 2,
        out_shape=[shaped(count, D, dtype=BF16), shaped(count, D)],
        compiler_params=SMALL,
        cost_estimate=cost(20 * count * D, 4 << 20),
        name="finish",
    )(hidden, cotangent, d_normed, mixed, gain)


def solve(which, x, pick):
    pieces, n, _ = x.shape
    return pl.pallas_call(
        solve_kernel,
        out_shape=shaped(pieces, pick.shape[0], IN_COLS),
        in_specs=[
            pl.BlockSpec(memory_space=pltpu.SMEM),
            pl.BlockSpec(memory_space=pl.ANY),
            pl.BlockSpec(memory_space=pltpu.VMEM),
        ],
        out_specs=pl.BlockSpec(memory_space=pltpu.VMEM),
        scratch_shapes=[pltpu.VMEM((len(triangle(n)), TILE, TILE), F32)]
        + [pltpu.VMEM((n, n), BF16)] * 4
        + [pltpu.VMEM((NS_STEPS - 1, n, n), BF16), pltpu.SemaphoreType.DMA((NS_STEPS - 1,))],
        compiler_params=pltpu.CompilerParams(vmem_limit_bytes=62 << 20),
        cost_estimate=cost(20 * n * n * n, 44 << 20),
        name="solve",
    )(which.astype(jnp.int32).reshape(1), x, pick)


def summaries(packed, direction):
    size = lax.axis_size("x")
    return [
        lax.ppermute(
            packed,
            "x",
            [(s, s + direction * k) for s in range(size) if 0 <= s + direction * k < size],
        )
        for k in range(1, size)
    ]


def blocks_of_columns(in_rows, out_rows):
    count = in_rows.shape[0]
    kind = in_rows.dtype
    z = in_rows[:, :E].reshape(count, G, EG)
    xs = in_rows[:, E : 2 * E].reshape(count, G, EG)
    bc = in_rows[:, 2 * E : 2 * E + 2 * N].reshape(count, G, BG)
    r = in_rows[:, 2 * E + 2 * N :].reshape(count, G, HG)
    fill = jnp.zeros((count, G, LANES - BG - HG), kind)
    out = out_rows.reshape(count, G, EG)
    return jnp.concatenate([z, xs, bc, r, fill, out], axis=2).transpose(1, 0, 2)


def rows_of_blocks(blocks):
    count = blocks.shape[1]
    b = blocks.transpose(1, 0, 2)
    pieces = [
        b[:, :, :EG].reshape(count, E),
        b[:, :, EG : 2 * EG].reshape(count, E),
        b[:, :, 2 * EG : 2 * EG + BG].reshape(count, 2 * N),
        b[:, :, 2 * EG + BG : 2 * EG + BG + HG].reshape(count, H),
    ]
    return jnp.concatenate(pieces, axis=1), b[:, :, IN_COLS:].reshape(count, E)


def along_y(own):
    size = lax.axis_size("y")
    return [own] + [
        lax.ppermute(own, "y", [(s, (s + k) % size) for s in range(size)]) for k in range(1, size)
    ]


def team_sum(values):
    values = values + lax.ppermute(values, "c", [(0, 1), (1, 0)])
    return sum(along_y(values))


def after(value, *others):
    return lax.optimization_barrier((value,) + others)[0]


def local(
    hidden,
    segments,
    norm_gain,
    in_weight,
    conv_weight,
    conv_bias,
    dt_bias,
    a_log,
    skip_scale,
    gate_gain,
    out_weight,
    cotangent,
    in_momentum,
    out_momentum,
    vector_momentum,
):
    zi, xi, yi, ci = (lax.axis_index(a) for a in EVERY)
    team = yi * 2 + ci
    count = in_weight.shape[0]
    team_count = G * count
    swap = [(0, 1), (1, 0)]
    first = ci == 0

    def mine(values, width, start=0, axis=-1):
        return lax.dynamic_slice_in_dim(values, start + team * width, width, axis % values.ndim)

    z_w = in_weight[:, :E].reshape(count, G, EG)
    xs_w = in_weight[:, E : 2 * E].reshape(count, G, EG)
    bc_w = jnp.broadcast_to(in_weight[:, None, 2 * E : 2 * E + 2 * N], (count, G, 2 * N))
    r_w = jnp.pad(
        in_weight[:, 2 * E + 2 * N :].reshape(count, G, HG), ((0, 0), (0, 0), (0, LANES - HG))
    )
    out_w = out_weight.reshape(count, G, EG)
    sent = jnp.concatenate([z_w, xs_w, bc_w, r_w, out_w], axis=2).transpose(1, 0, 2)
    got = lax.all_to_all(sent, TEAM, 0, 0, tiled=True).reshape(team_count, -1)
    weights = lax.all_gather(got, ROWS, axis=0, tiled=True)

    numbers = jnp.pad(segments.astype(BF16)[:, None], ((0, 0), (0, LANES - 1)))
    pieces = along_y(jnp.concatenate([hidden, numbers], axis=1))
    momentum_block = lax.all_to_all(
        blocks_of_columns(
            *(after(m, got).astype(BF16) for m in (in_momentum, out_momentum))
        ),
        TEAM,
        0,
        0,
        tiled=True,
    ).reshape(team_count, BLOCK)
    conv_all = jnp.concatenate([conv_weight, conv_bias[None, :]], axis=0)
    taps = jnp.pad(
        jnp.concatenate([mine(conv_all[:, :E], EG), conv_all[:, E:]], axis=1),
        ((0, 8 - TAPS - 1), (0, 0)),
    )
    taps_shared = jnp.pad(mine(conv_all[:, E:], BG), ((0, 8 - TAPS - 1), (0, LANES - BG)))
    head = jnp.pad(
        jnp.stack([mine(dt_bias, HG), jnp.exp(mine(a_log, HG))]), ((0, 6), (0, LANES - HG))
    )
    wide = jnp.pad(
        jnp.stack([jnp.repeat(mine(skip_scale, HG), HEAD), mine(gate_gain, EG)]), ((0, 6), (0, 0))
    )
    summer = (
        lax.broadcasted_iota(jnp.int32, (EG, LANES), 0) // HEAD
        == lax.broadcasted_iota(jnp.int32, (EG, LANES), 1)
    ).astype(BF16)
    pieces, momentum_block, taps, taps_shared, head, wide, summer = lax.optimization_barrier(
        (pieces, momentum_block, taps, taps_shared, head, wide, summer)
    )
    own_rows = jnp.stack(pieces)
    other_rows = lax.ppermute(own_rows, "c", swap)
    q_pieces = along_y(after(cotangent, own_rows))
    place = jnp.stack([yi, ci]).astype(jnp.int32)
    size_x, size_y = lax.axis_size("x"), lax.axis_size("y")
    end_rows = lax.dynamic_index_in_dim(
        jnp.where(first, other_rows[:, CHUNK - EDGE :], own_rows[:, CHUNK - EDGE :]),
        (yi + 1) % size_y,
        0,
        False,
    )
    edge_rows_in = lax.ppermute(end_rows, "x", [(s, s + 1) for s in range(size_x - 1)])
    by_distance = jnp.stack([own_rows[:, :, D], other_rows[:, :, D]]).astype(F32)
    by_core = jnp.where(first, by_distance, by_distance[::-1])
    team_ids = by_core[:, (yi - jnp.arange(size_y)) % size_y].transpose(1, 0, 2).reshape(-1)
    next_ids = lax.ppermute(team_ids[:LANES], "x", [(s, s - 1) for s in range(1, size_x)])
    ids = jnp.concatenate(
        [
            jnp.where(xi == 0, -1.0, edge_rows_in[EDGE - 8 :, D].astype(F32)),
            team_ids,
            jnp.where(xi == size_x - 1, -1.0, next_ids[:8]),
        ]
    )

    def flag_lanes(at, size):
        own = ids[at : at + size]
        same = [(ids[at - k : at - k + size] == own).astype(F32) for k in range(TAPS)]
        ahead = [(ids[at + k : at + k + size] == own).astype(F32) for k in range(TAPS)]
        return own, same + ahead

    own_ids, lanes = flag_lanes(8, TOKENS)
    by_piece = own_ids.reshape(PIECES, CHUNK)
    before = ids[7 : 7 + TOKENS].reshape(PIECES, CHUNK)[:, :1]
    last = by_piece[:, CHUNK - 1 :]
    lanes = lanes + [
        jnp.zeros((TOKENS,), F32),
        (by_piece == before).astype(F32).reshape(-1),
        (by_piece == last).astype(F32).reshape(-1),
        jnp.broadcast_to((last == before).astype(F32), (PIECES, CHUNK)).reshape(-1),
        own_ids,
    ]
    flags = jnp.pad(jnp.stack(lanes, axis=1), ((0, 0), (0, LANES - len(lanes))))
    edge_ids = jnp.pad(ids, (8, 0), constant_values=-1.0)[: 8 + 16]
    edge_own = edge_ids[8:16]
    edge_flags = jnp.pad(
        jnp.stack(
            [jnp.zeros((8,), F32)] * AHEAD
            + [(edge_ids[8 + k : 16 + k] == edge_own).astype(F32) for k in range(TAPS)],
            axis=1,
        ),
        ((0, 0), (0, LANES - AHEAD - TAPS)),
    )

    q_pieces, flags, edge_flags = lax.optimization_barrier((q_pieces, flags, edge_flags))
    q_own = jnp.stack(q_pieces)
    q_other = lax.ppermute(q_own, "c", swap)

    normed, z, v, r = project(
        place, own_rows, other_rows, edge_rows_in, weights, norm_gain[None, :]
    )
    conv, dt, cum, y_part, starts, reach, gain, packed = forward(v, r, flags, by_piece, taps, head)
    arrivals = summaries(packed, 1)
    q_team, d_gated = incoming(place, q_own, q_other, weights)
    y, sums, arrived = outputs(y_part, conv, cum, flags, z, d_gated, reach, arrivals, wide)
    sums = team_sum(sums)
    gated, dz, dy, ends, reach_back, d_gate, packed_back = gate(
        y, z, d_gated, conv, cum, flags, gain, sums, wide
    )
    early = early_products(normed, q_team, dz, gated)
    dy, packed_back, early = lax.optimization_barrier((dy, packed_back, early))
    early_sum = lax.psum_scatter(early, ROWS, scatter_dimension=0, tiled=True).astype(F32)
    arrivals_back = summaries(packed_back, -1)

    u, d_bc = inner(dy, conv, dt, cum, flags, by_piece)
    dv, d_edge, kept, sent_bc, dr, wide_sums, head_sums_out = backward(
        place, u, d_bc, dy, y, conv, dt, cum, r, flags, starts, reach, arrived, ends, reach_back,
        arrivals_back, packed, v, wide, taps, head, summer, edge_flags,
    )
    summed = (kept + lax.ppermute(sent_bc, "c", swap)).reshape(size_y, BG, TOKENS)

    def piece_for(k):
        return lax.dynamic_index_in_dim(summed, (yi + k) % size_y, 0, False)

    d_bc_got = [piece_for(0)] + [
        lax.ppermute(piece_for(k), "y", [(s, (s + k) % size_y) for s in range(size_y)])
        for k in range(1, size_y)
    ]
    late, shared_sums = shared(
        team.reshape(1), d_bc_got, conv, v, dr, dv, d_edge, flags, edge_flags, taps_shared
    )
    late_partial = dot(normed, late, TN).astype(BF16)
    late_parts = lax.all_to_all(
        late_partial.reshape(16, team_count, LATE_COLS), ROWS, 0, 0, tiled=True
    )
    late_sum = jnp.sum(late_parts.astype(F32), axis=0)

    ahead = MATRIX_MOMENTUM * momentum_block.astype(F32)
    late_new = (ahead[:, EG:IN_COLS] + late_sum).astype(BF16)
    late_new, ahead = lax.optimization_barrier((late_new, ahead))
    momenta = jnp.concatenate(
        [
            (ahead[:, :EG] + early_sum[:, :EG]).astype(BF16),
            late_new,
            (ahead[:, IN_COLS:] + early_sum[:, EG:]).astype(BF16),
        ],
        axis=1,
    )
    sums_block = jnp.concatenate([early_sum[:, :EG], late_sum, early_sum[:, EG:]], axis=1)
    x_all = lax.all_gather(momenta, TEAM + ROWS).reshape(G, D, BLOCK)

    late_back = lax.ppermute(
        late[TOKENS:], "x", [(s, s - 1) for s in range(1, lax.axis_size("x"))]
    )
    late, late_back, dz, gated, late_sum = lax.optimization_barrier(
        (late, late_back, dz, gated, late_sum)
    )
    d_projected = jnp.concatenate(
        [
            dz,
            jnp.concatenate(
                [late[: TOKENS - EDGE], late[TOKENS - EDGE : TOKENS] + late_back], axis=0
            ),
        ],
        axis=1,
    )
    w_own = jnp.concatenate(
        [
            weights[:, : 2 * EG],
            mine(weights[:, 2 * EG : 2 * EG + 2 * N], BG),
            weights[:, 2 * EG + 2 * N : 2 * EG + 2 * N + HG],
            jnp.zeros((D, LANES - BG - HG), BF16),
        ],
        axis=1,
    )
    d_normed_part = dot(d_projected, w_own, NT)
    d_norm_gain = jnp.sum(d_normed_part * normed[:TOKENS].astype(F32), axis=0) / norm_gain
    mixed_part = dot(gated, weights[:, FORWARD_COLS:], NT)

    vector = jnp.concatenate(
        [
            d_norm_gain,
            jnp.concatenate(
                [wide_sums[: TAPS + 1], shared_sums[: TAPS + 1, :BG]], axis=1
            ).reshape(-1),
            d_gate[0],
            head_sums_out[:3, :HG].reshape(-1),
        ]
    )
    vector = jnp.pad(vector, (0, -vector.shape[0] % 1024)).reshape(-1, LANES)
    vector = jnp.sum(lax.all_gather(vector, ROWS), axis=0)
    vector = lax.all_gather(vector, TEAM).reshape(G, -1)
    own = EG + BG
    grad_gain = jnp.sum(vector[:, :D], axis=0)
    conv_parts = vector[:, D : D + (TAPS + 1) * own].reshape(G, TAPS + 1, own).transpose(1, 0, 2)
    conv_parts = jnp.concatenate(
        [
            conv_parts[:, :, :EG].reshape(TAPS + 1, E),
            conv_parts[:, :, EG:].reshape(TAPS + 1, 2 * N),
        ],
        axis=1,
    )
    rest = vector[:, D + (TAPS + 1) * own :]
    heads = rest[:, EG : EG + 3 * HG].reshape(G, 3, HG).transpose(1, 0, 2).reshape(-1)
    vector_grad = jnp.concatenate(
        [grad_gain, conv_parts.reshape(-1), heads, rest[:, :EG].reshape(-1)]
    )
    vector_old = jnp.concatenate(
        [norm_gain, conv_weight.reshape(-1), conv_bias, dt_bias, a_log, skip_scale, gate_gain]
    )
    vector_momentum_new = VECTOR_MOMENTUM * vector_momentum + (1.0 - VECTOR_MOMENTUM) * vector_grad
    vector_new = vector_old - VECTOR_RATE * vector_momentum_new
    grad_rows = lax.all_to_all(
        sums_block.reshape(G, count, BLOCK), TEAM, 0, 0, tiled=True
    )
    in_grad, out_grad = rows_of_blocks(grad_rows)
    in_momentum_new = MATRIX_MOMENTUM * in_momentum + in_grad
    out_momentum_new = MATRIX_MOMENTUM * out_momentum + out_grad

    chip_row = (zi * 4 + xi) * team_count + yi * (2 * count)
    pick = (
        lax.broadcasted_iota(jnp.int32, (2 * count, D), 1)
        == lax.broadcasted_iota(jnp.int32, (2 * count, D), 0) + chip_row
    ).astype(F32)
    (
        x_all, pick, d_normed_part, mixed_part,
        vector_grad, vector_momentum_new, vector_new,
        in_grad, in_momentum_new, out_grad, out_momentum_new,
    ) = lax.optimization_barrier(
        (
            x_all, pick, d_normed_part, mixed_part,
            vector_grad, vector_momentum_new, vector_new,
            in_grad, in_momentum_new, out_grad, out_momentum_new,
        )
    )
    steps = solve(first, x_all, pick)
    d_normed = lax.psum_scatter(d_normed_part, TEAM, scatter_dimension=0, tiled=True)
    mixed = lax.psum_scatter(mixed_part, TEAM, scatter_dimension=0, tiled=True)
    block_output, input_grad = finish(hidden, cotangent, d_normed, mixed, norm_gain[None, :])

    own_steps = lax.dynamic_slice_in_dim(steps, ci * count, count, 1)
    got_steps = lax.ppermute(
        lax.dynamic_slice_in_dim(steps, (1 - ci) * count, count, 1), "c", swap
    )
    both = jnp.concatenate(
        [
            jnp.where(first, own_steps, got_steps),
            jnp.where(first, got_steps, own_steps)[:, :, : BLOCK - IN_COLS],
        ],
        axis=2,
    )
    step_in, step_out = rows_of_blocks(both)
    in_weight_new = in_weight.astype(F32) - MATRIX_RATE * math.sqrt(PROJ / D) * step_in
    out_weight_new = out_weight.astype(F32) - MATRIX_RATE * math.sqrt(E / D) * step_out
    return (
        block_output,
        input_grad,
        in_grad,
        in_momentum_new,
        in_weight_new,
        out_grad,
        out_momentum_new,
        out_weight_new,
        vector_grad,
        vector_momentum_new,
        vector_new,
    )


def solution(mesh):
    grid = Mesh(mesh.devices.reshape(4, 4, 4, 2), EVERY)
    split = P(EVERY, None)
    return jax.shard_map(
        local,
        mesh=grid,
        in_specs=(
            split,
            P(EVERY),
            P(),
            split,
            P(),
            P(),
            P(),
            P(),
            P(),
            P(),
            split,
            split,
            split,
            split,
            P(),
        ),
        out_specs=(split,) * 8 + (P(),) * 3,
        check_vma=False,
    )
```

```python
import math

import jax
import jax.numpy as jnp
from jax import lax
from jax.experimental import pallas as pl
from jax.experimental.pallas import tpu as pltpu
from jax.sharding import Mesh, PartitionSpec as P

NS_STEPS = 5
EPSILON = 1e-05
NORM_FLOOR = 1e-07
POLY_FIRST = 3.4445
POLY_SECOND = -4.775
POLY_THIRD = 2.0315
MATRIX_MOMENTUM = 0.95
MATRIX_RATE = 0.5
VECTOR_MOMENTUM = 0.9
VECTOR_RATE = 0.05
HIGHEST = lax.Precision.HIGHEST
F32 = jnp.float32
BF16 = jnp.bfloat16

EVERY = ("z", "x", "y", "c")
TEAM = ("y", "c")
ROWS = ("z", "x")

D = 1536
H = 48
HEAD = 64
N = 128
E = 3072
PROJ = 6448
TAPS = 4
G = 8
HG = H // G
EG = E // G
BG = 2 * N // G
TOKENS = 1024
CHUNK = 128
PIECES = TOKENS // CHUNK
AT_ONCE = 4
STEPS = PIECES // AT_ONCE
SPAN = AT_ONCE * CHUNK
EDGE = 16
LANES = 128
VG = EG + 2 * N
IN_COLS = 2 * EG + LANES
BLOCK = IN_COLS + EG
FORWARD_COLS = EG + VG + LANES
LATE_COLS = EG + LANES
STATE_ROWS = N + 8
TILE = 256
AHEAD, KEEP, TAIL, GAIN, SEGMENT = 4, 9, 10, 11, 12


def dot(a, b, dims):
    return lax.dot_general(
        a.astype(BF16), b.astype(BF16), (dims, ((), ())), preferred_element_type=F32
    )


NN = ((1,), (0,))
NT = ((1,), (1,))
TN = ((0,), (0,))


def parts(value):
    top = value.astype(BF16)
    return top, (value - top.astype(F32)).astype(BF16)


def dot3(a, b, dims=NN):
    a_top, a_rest = parts(a)
    b_top, b_rest = parts(b)
    return dot(a_top, b_top, dims) + (dot(a_top, b_rest, dims) + dot(a_rest, b_top, dims))


def lane_of(shape):
    return lax.broadcasted_iota(jnp.int32, shape, 1)


def piece_rows(k, height=CHUNK):
    return pl.ds(k * height, height)


def widen(per_head):
    rows = per_head.shape[0]
    left = lane_of((rows, LANES)) < HEAD
    return jnp.concatenate(
        [
            jnp.where(
                left,
                jnp.broadcast_to(per_head[:, 2 * p : 2 * p + 1], (rows, LANES)),
                jnp.broadcast_to(per_head[:, 2 * p + 1 : 2 * p + 2], (rows, LANES)),
            )
            for p in range(HG // 2)
        ],
        axis=1,
    )


def head_sums(values, summer):
    top, rest = parts(values)
    return dot(top, summer, NN) + dot(rest, summer, NN)


def pair_lanes(p):
    return slice(p * LANES, (p + 1) * LANES)


def stacked_pair(values):
    left = lane_of(values.shape) < HEAD
    zero = jnp.zeros_like(values)
    return jnp.concatenate(
        [jnp.where(left, values, zero), jnp.where(left, zero, values)], axis=0
    )


def running(mask, values):
    top, rest = parts(values)
    least = values - top.astype(F32) - rest.astype(F32)
    return dot(mask, top, NN) + (dot(mask, rest, NN) + dot(mask, least, NN))


def silu_parts(values):
    sig = jax.nn.sigmoid(values)
    return sig, values * sig


def softplus(values):
    return jnp.maximum(values, 0.0) + jnp.log1p(jnp.exp(-jnp.abs(values)))


def square_iota():
    shape = (CHUNK, CHUNK)
    return lax.broadcasted_iota(jnp.int32, shape, 0), lane_of(shape)


def same_document(flags, row):
    return flags[:, SEGMENT : SEGMENT + 1] == row


def in_order(core_ref, own_ref, other_ref):
    own, other = own_ref[0], other_ref[0]
    first = core_ref[1] == 0
    return jnp.concatenate(
        [jnp.where(first, own, other), jnp.where(first, other, own)], axis=0
    )


def project_kernel(
    core_ref, own_ref, other_ref, edge_ref, w_ref, gain_ref, normed_ref, z_ref, v_ref, r_ref
):
    def put(x, at):
        x = x.astype(F32)
        scale = lax.rsqrt(jnp.mean(x * x, axis=1, keepdims=True) + EPSILON)
        normed = (x * scale * gain_ref[...]).astype(BF16)
        normed_ref[at, :] = normed
        out = jnp.dot(normed, w_ref[...], preferred_element_type=F32)
        z_ref[at, :] = out[:, :EG]
        v_ref[at, :] = out[:, EG : EG + VG]
        r_ref[at, :] = out[:, EG + VG :]

    last = pl.num_programs(0) - 1

    @pl.when(pl.program_id(0) < last)
    def _():
        put(in_order(core_ref, own_ref, other_ref), pl.ds(0, 2 * CHUNK))

    @pl.when(pl.program_id(0) == last)
    def _():
        put(edge_ref[...], pl.ds(0, EDGE))


def incoming_kernel(core_ref, own_ref, other_ref, w_ref, q_ref, d_gated_ref):
    q = in_order(core_ref, own_ref, other_ref)
    q_ref[...] = q
    d_gated_ref[...] = jnp.dot(q, w_ref[...], preferred_element_type=F32)


def early_kernel(normed_ref, q_ref, dz_ref, gated_ref, out_ref):
    out_ref[:, :EG] = dot(normed_ref[0:TOKENS, :], dz_ref[...], TN).astype(BF16)
    out_ref[:, EG:] = dot(q_ref[...], gated_ref[...], TN).astype(BF16)


def forward_kernel(
    v_ref,
    before_ref,
    r_ref,
    flags_ref,
    ids_ref,
    taps_ref,
    head_ref,
    conv_ref,
    dt_ref,
    cum_ref,
    y_ref,
    start_ref,
    reach_ref,
    gain_ref,
    packed_ref,
    state,
    reach,
):
    step = pl.program_id(0)

    @pl.when(step == 0)
    def _():
        state[...] = jnp.zeros_like(state)
        reach[...] = jnp.ones_like(reach)

    for k in range(AT_ONCE):
        c = step * AT_ONCE + k
        at, at8 = piece_rows(k), piece_rows(k, 8)
        flags = flags_ref[at, :]
        window = jnp.concatenate([before_ref[...] if k == 0 else v_ref[pl.ds(k * CHUNK - 8, 8), :], v_ref[at, :]], axis=0)
        conv = taps_ref[TAPS : TAPS + 1, :] + taps_ref[0:1, :] * window[8:]
        for lag in range(1, TAPS):
            conv = conv + taps_ref[lag : lag + 1, :] * (
                pltpu.roll(window, lag, 0)[8:] * flags[:, lag : lag + 1]
            )
        conv_ref[at, :] = conv
        act = conv * jax.nn.sigmoid(conv)
        xs, bm, cm = act[:, :EG], act[:, EG : EG + N], act[:, EG + N :]
        dt = softplus(r_ref[at, :] + head_ref[0:1, :])
        dt_ref[at, :] = dt
        ti, si = square_iota()
        lower = (ti >= si).astype(F32)
        cum = running(lower, -head_ref[1:2, :] * dt)
        cum_ref[at, :] = cum
        cum_t = cum.T
        last = cum[CHUNK - 1 : CHUNK, :]
        tail = jnp.exp(last - cum) * flags[:, TAIL : TAIL + 1]
        carry = jnp.exp(cum) * flags[:, KEEP : KEEP + 1]
        gain = widen(jnp.exp(last) * flags[0:1, GAIN : GAIN + 1])
        xdt = xs * widen(dt)
        scores = dot3(cm, bm, NT)
        mask = (ti >= si) & same_document(flags, ids_ref[pl.ds(c, 1), :])
        within = []
        for p in range(HG // 2):
            mix = [
                jnp.exp(jnp.where(mask, cum[:, h : h + 1] - cum_t[h : h + 1, :], -1e30)) * scores
                for h in (2 * p, 2 * p + 1)
            ]
            within.append(
                dot3(jnp.concatenate(mix, axis=1), stacked_pair(xdt[:, pair_lanes(p)]))
            )
        y_ref[at, :] = jnp.concatenate(within, axis=1) + widen(carry) * dot3(cm, state[...])
        start_ref[k] = state[...]
        reach_ref[at8, :] = reach[...]
        gain_ref[at8, :] = jnp.broadcast_to(gain, (8, EG))
        state[...] = gain * state[...] + dot3(bm.T, xdt * widen(tail))
        reach[...] = gain * reach[...]

    @pl.when(step == STEPS - 1)
    def _():
        packed_ref[0:N, :] = state[...]
        packed_ref[N:, :] = reach[...]


def joined_states(first, second, third):
    return first[:N] + first[N : N + 1] * (second[:N] + second[N : N + 1] * third[:N])


def output_kernel(
    y_part_ref,
    conv_ref,
    cum_ref,
    flags_ref,
    z_ref,
    d_gated_ref,
    reach_ref,
    first_ref,
    second_ref,
    third_ref,
    rows_ref,
    y_ref,
    sums_ref,
    arrived_ref,
):
    step = pl.program_id(0)

    @pl.when(step == 0)
    def _():
        arrived_ref[...] = joined_states(first_ref[...], second_ref[...], third_ref[...])

    for k in range(AT_ONCE):
        c = step * AT_ONCE + k
        at = piece_rows(k)
        conv = conv_ref[at, :]
        act = conv * jax.nn.sigmoid(conv)
        carry = widen(jnp.exp(cum_ref[at, :]) * flags_ref[at, KEEP : KEEP + 1]) * reach_ref[pl.ds(8 * k, 1), :]
        y = (
            y_part_ref[at, :]
            + carry * dot3(act[:, EG + N :], arrived_ref[...])
            + rows_ref[0:1, :] * act[:, :EG]
        )
        y_ref[at, :] = y
        _, silu_z = silu_parts(z_ref[at, :])
        g = y * silu_z
        squares = jnp.sum(g * g, axis=1, keepdims=True)
        inner = jnp.sum(d_gated_ref[at, :] * rows_ref[1:2, :] * g, axis=1, keepdims=True)
        lane = lane_of((CHUNK, LANES))
        turned = jnp.where(lane == 0, squares, jnp.where(lane == 1, inner, 0.0)).T
        sums_ref[pl.ds(c, 1), :] = turned[0:1, :]
        sums_ref[pl.ds(PIECES + c, 1), :] = turned[1:2, :]


def gate_kernel(
    y_ref,
    z_ref,
    d_gated_ref,
    conv_ref,
    cum_ref,
    flags_ref,
    gain_ref,
    sums_ref,
    rows_ref,
    gated_ref,
    dz_ref,
    dy_ref,
    end_ref,
    reach_ref,
    d_gate_ref,
    packed_ref,
    state,
    reach,
):
    step = STEPS - 1 - pl.program_id(0)

    @pl.when(step == STEPS - 1)
    def _():
        state[...] = jnp.zeros_like(state)
        reach[...] = jnp.ones_like(reach)
        d_gate_ref[...] = jnp.zeros_like(d_gate_ref)

    for k in reversed(range(AT_ONCE)):
        c = step * AT_ONCE + k
        at, at8 = piece_rows(k), piece_rows(k, 8)
        ti, _ = square_iota()
        turned = jnp.where(
            ti == 0,
            sums_ref[pl.ds(c, 1), :],
            jnp.where(ti == 1, sums_ref[pl.ds(PIECES + c, 1), :], 0.0),
        ).T
        root = lax.rsqrt(turned[:, 0:1] * (1.0 / E) + EPSILON)
        slope = turned[:, 1:2] * (root * root * root) * (1.0 / E)
        gate = rows_ref[1:2, :]
        y = y_ref[at, :]
        sig, silu_z = silu_parts(z_ref[at, :])
        g = y * silu_z
        unit = g * root
        gated_ref[at, :] = (unit * gate).astype(BF16)
        d_gated = d_gated_ref[at, :]
        d_gate_ref[0:1, :] += jnp.sum(d_gated * unit, axis=0, keepdims=True)
        d_g = root * (d_gated * gate) - g * slope
        dy = d_g * silu_z
        dz_ref[at, :] = (d_g * y * (sig + silu_z * (1.0 - sig))).astype(BF16)
        dy_ref[at, :] = dy
        conv = conv_ref[at, EG + N :]
        cm = conv * jax.nn.sigmoid(conv)
        carry = widen(jnp.exp(cum_ref[at, :]) * flags_ref[at, KEEP : KEEP + 1])
        end_ref[k] = state[...]
        reach_ref[at8, :] = reach[...]
        gain = gain_ref[pl.ds(8 * k, 1), :]
        state[...] = gain * state[...] + dot3(cm.T, dy * carry)
        reach[...] = gain * reach[...]

    @pl.when(step == 0)
    def _():
        packed_ref[0:N, :] = state[...]
        packed_ref[N:, :] = reach[...]


def inner_kernel(dy_ref, conv_ref, dt_ref, cum_ref, flags_ref, ids_ref, u_ref, d_bc_ref):
    for k in range(AT_ONCE):
        c = pl.program_id(0) * AT_ONCE + k
        at = piece_rows(k)
        flags = flags_ref[at, :]
        conv = conv_ref[at, :]
        act = conv * jax.nn.sigmoid(conv)
        xs, bm, cm = act[:, :EG], act[:, EG : EG + N], act[:, EG + N :]
        cum = cum_ref[at, :]
        cum_t = cum.T
        dy = dy_ref[at, :]
        xdt = xs * widen(dt_ref[at, :])
        scores_t = dot3(bm, cm, NT)
        ti, si = square_iota()
        same = same_document(flags, ids_ref[pl.ds(c, 1), :])
        mask = (ti >= si) & same
        mask_t = (ti <= si) & same
        d_scores = jnp.zeros((CHUNK, CHUNK), F32)
        u = []
        for p in range(HG // 2):
            own = stacked_pair(dy[:, pair_lanes(p)])
            pairs = dot3(own, xdt[:, pair_lanes(p)], NT)
            mix_t = []
            for k in range(2):
                h = 2 * p + k
                gap = cum[:, h : h + 1] - cum_t[h : h + 1, :]
                d_scores = d_scores + jnp.exp(jnp.where(mask, gap, -1e30)) * (
                    pairs[k * CHUNK : (k + 1) * CHUNK]
                )
                mix_t.append(jnp.exp(jnp.where(mask_t, -gap, -1e30)) * scores_t)
            u.append(dot(jnp.concatenate(mix_t, axis=1), own, NN))
        u_ref[at, :] = jnp.concatenate(u, axis=1)
        d_bc_ref[at, :N] = dot3(d_scores.T, cm)
        d_bc_ref[at, N:] = dot3(d_scores, bm)


def backward_kernel(
    core_ref,
    u_ref,
    d_bc_ref,
    dy_ref,
    y_ref,
    conv_ref,
    dt_ref,
    cum_ref,
    r_ref,
    flags_ref,
    start_ref,
    reach_ref,
    arrived_ref,
    end_ref,
    reach_back_ref,
    first_ref,
    second_ref,
    third_ref,
    final_ref,
    v_ref,
    before_ref,
    rows_ref,
    taps_ref,
    head_ref,
    summer_ref,
    edge_flags_ref,
    dv_ref,
    d_edge_ref,
    kept_ref,
    sent_ref,
    dr_ref,
    wide_ref,
    heads_ref,
    following,
    flowing,
    adjoint_in,
):
    step = STEPS - 1 - pl.program_id(0)
    summer = summer_ref[...]

    @pl.when(step == STEPS - 1)
    def _():
        adjoint = joined_states(first_ref[...], second_ref[...], third_ref[...])
        adjoint_in[...] = adjoint
        final = final_ref[0:N, :] + final_ref[N : N + 1, :] * arrived_ref[...]
        inner = jnp.sum(adjoint * final, axis=0, keepdims=True)
        flowing[...] = head_sums(jnp.broadcast_to(inner, (8, EG)), summer)
        following[...] = jnp.zeros_like(following)
        wide_ref[...] = jnp.zeros_like(wide_ref)
        heads_ref[...] = jnp.zeros_like(heads_ref)

    for k in reversed(range(AT_ONCE)):
        at = piece_rows(k)
        flags = flags_ref[at, :]
        conv = conv_ref[at, :]
        sig, act = silu_parts(conv)
        xs, bm = act[:, :EG], act[:, EG : EG + N]
        cum = cum_ref[at, :]
        dt = dt_ref[at, :]
        dy = dy_ref[at, :]
        skip = rows_ref[0:1, :]
        rate = head_ref[1:2, :]
        last = cum[CHUNK - 1 : CHUNK, :]
        tail = widen(jnp.exp(last - cum) * flags[:, TAIL : TAIL + 1])
        carry = widen(jnp.exp(cum) * flags[:, KEEP : KEEP + 1])
        dt_wide = widen(dt)
        start = start_ref[k] + reach_ref[pl.ds(8 * k, 1), :] * arrived_ref[...]
        adjoint = end_ref[k] + reach_back_ref[pl.ds(8 * k, 1), :] * adjoint_in[...]
        u = u_ref[at, :] + tail * dot3(bm, adjoint)
        d_xs = u * dt_wide + skip * dy
        d_dt = head_sums(xs * u, summer)
        d_bm = d_bc_ref[at, :N] + dot3(xs * dt_wide * tail, adjoint, NT)
        d_cm = d_bc_ref[at, N:] + dot3(dy * carry, start, NT)
        turned = jnp.concatenate([d_bm.T, d_cm.T], axis=0)
        of_core = [
            jnp.concatenate(
                [turned[(2 * y + c) * BG : (2 * y + c + 1) * BG] for y in range(G // 2)], axis=0
            )
            for c in range(2)
        ]
        first = core_ref[1] == 0
        kept_ref[:, at] = jnp.where(first, of_core[0], of_core[1])
        sent_ref[:, at] = jnp.where(first, of_core[1], of_core[0])
        flow = head_sums(dy * (y_ref[at, :] - skip * xs), summer) - dt * d_dt
        ti, si = square_iota()
        upper = (si >= ti).astype(F32)
        d_la = running(upper, flow) + flowing[0:1, :]
        flowing[...] = jnp.broadcast_to(d_la[0:1, :], flowing.shape)
        d_la = d_la * flags[:, 1:2]
        d_r = (d_dt - rate * d_la) * jax.nn.sigmoid(r_ref[at, :] + head_ref[0:1, :])
        dr_ref[at, :] = d_r
        heads_ref[0:1, :] += jnp.sum(d_r, axis=0, keepdims=True)
        heads_ref[1:2, :] += jnp.sum(d_la * (-rate * dt), axis=0, keepdims=True)
        heads_ref[2:3, :] += jnp.sum(head_sums(dy * xs, summer), axis=0, keepdims=True)

        sig, conv = sig[:, :EG], conv[:, :EG]
        d_conv = d_xs * (sig + conv * sig * (1.0 - sig))
        window = jnp.concatenate([before_ref[...] if k == 0 else v_ref[pl.ds(k * CHUNK - 8, 8), :], v_ref[at, :]], axis=0)
        ahead = jnp.concatenate([d_conv, following[...]], axis=0)
        wide_ref[0:1, :] += jnp.sum(d_conv * window[8:], axis=0, keepdims=True)
        wide_ref[TAPS : TAPS + 1, :] += jnp.sum(d_conv, axis=0, keepdims=True)
        dv = taps_ref[0:1, :EG] * d_conv
        for lag in range(1, TAPS):
            wide_ref[lag : lag + 1, :] += jnp.sum(
                d_conv * pltpu.roll(window, lag, 0)[8:] * flags[:, lag : lag + 1],
                axis=0,
                keepdims=True,
            )
            dv = dv + taps_ref[lag : lag + 1, :EG] * (
                pltpu.roll(ahead, CHUNK + 8 - lag, 0)[:CHUNK] * flags[:, AHEAD + lag : AHEAD + lag + 1]
            )
        dv_ref[at, :] = dv.astype(BF16)
        following[...] = d_conv[0:8]

    @pl.when(step == 0)
    def _():
        d_edge_ref[...] = edge_rows(following[...], taps_ref[:, :EG], edge_flags_ref[...])


def edge_rows(d_conv, taps, flags):
    zero = jnp.zeros_like(d_conv)
    ahead = jnp.concatenate([zero, d_conv], axis=0)
    total = zero
    for lag in range(1, TAPS):
        total = total + taps[lag : lag + 1, :] * (
            pltpu.roll(ahead, EDGE - lag, 0)[0:8] * flags[:, AHEAD + lag : AHEAD + lag + 1]
        )
    return jnp.concatenate([zero, total], axis=0).astype(BF16)


def shared_kernel(
    team_ref,
    got_refs,
    conv_b_ref,
    conv_c_ref,
    v_b_ref,
    v_c_ref,
    before_b_ref,
    before_c_ref,
    dr_ref,
    flags_ref,
    edge_flags_ref,
    taps_ref,
    late_ref,
    wide_ref,
    following,
):
    step = pl.program_id(0)
    turn = (2 * N - BG * team_ref[0]) % (2 * N)

    def own(b, c):
        return pltpu.roll(jnp.concatenate([b, c], axis=1), turn, 1)[:, :LANES]

    def before(k):
        if k == 0:
            return own(before_b_ref[...], before_c_ref[...])
        last = pl.ds(k * CHUNK - 8, 8)
        return own(v_b_ref[last, :], v_c_ref[last, :])

    @pl.when(step == 0)
    def _():
        following[...] = jnp.zeros_like(following)
        wide_ref[...] = jnp.zeros_like(wide_ref)

    def piece(k):
        at = piece_rows(k)
        flags = flags_ref[at, :]
        total = sum(ref[:, at] for ref in got_refs)
        d_act = jnp.concatenate([total, jnp.zeros((LANES - BG, CHUNK), F32)], axis=0).T
        conv = own(conv_b_ref[at, :], conv_c_ref[at, :])
        sig = jax.nn.sigmoid(conv)
        d_conv = d_act * (sig + conv * sig * (1.0 - sig))
        window = jnp.concatenate(
            [before(k), own(v_b_ref[at, :], v_c_ref[at, :])], axis=0
        )
        ahead = jnp.concatenate([d_conv, following[...]], axis=0)
        wide_ref[0:1, :] += jnp.sum(d_conv * window[8:], axis=0, keepdims=True)
        wide_ref[TAPS : TAPS + 1, :] += jnp.sum(d_conv, axis=0, keepdims=True)
        dv = taps_ref[0:1, :] * d_conv
        for lag in range(1, TAPS):
            wide_ref[lag : lag + 1, :] += jnp.sum(
                d_conv * pltpu.roll(window, lag, 0)[8:] * flags[:, lag : lag + 1],
                axis=0,
                keepdims=True,
            )
            dv = dv + taps_ref[lag : lag + 1, :] * (
                pltpu.roll(ahead, CHUNK + 8 - lag, 0)[:CHUNK]
                * flags[:, AHEAD + lag : AHEAD + lag + 1]
            )
        following[...] = d_conv[0:8]
        late_ref[at, :] = (dv + pltpu.roll(dr_ref[at, :], BG, 1)).astype(BF16)

    @pl.when(step < STEPS)
    def _():
        for k in reversed(range(AT_ONCE)):
            piece(k)

    @pl.when(step == STEPS)
    def _():
        late_ref[0:EDGE, :] = edge_rows(following[...], taps_ref[...], edge_flags_ref[...])


def finish_kernel(hidden_ref, cotangent_ref, d_normed_ref, mixed_ref, gain_ref, out_ref, grad_ref):
    x = hidden_ref[...].astype(F32)
    scale = lax.rsqrt(jnp.mean(x * x, axis=1, keepdims=True) + EPSILON)
    unit = x * scale
    d_unit = d_normed_ref[...] * gain_ref[...]
    inner = jnp.mean(d_unit * unit, axis=1, keepdims=True)
    grad_ref[...] = cotangent_ref[...].astype(F32) + scale * (d_unit - unit * inner)
    out_ref[...] = (x + mixed_ref[...]).astype(BF16)


def triangle(n):
    return [(i, j) for i in range(n // TILE) for j in range(i, n // TILE)]


def solve_kernel(
    which_ref, x_ref, pick_ref, own_ref, other_ref, total, high, low, h_high, h_low, q_ref, sems
):
    pieces = x_ref.shape[0]
    slots = q_ref.shape[0]
    n = high.shape[0]
    count = n // TILE
    order = triangle(n)

    def at(i):
        return pl.ds(i * TILE, TILE) if isinstance(i, int) else pl.ds(pl.multiple_of(i * TILE, TILE), TILE)

    def times(a, b):
        return jnp.dot(a, b, preferred_element_type=F32)

    def arriving(y, slot, columns):
        width = columns.stop - columns.start
        return pltpu.make_async_copy(
            x_ref.at[y, :, columns], q_ref.at[slot, :, pl.ds(0, width)], sems.at[slot]
        )

    def gram(columns):
        width = columns.stop - columns.start
        for slot in range(slots):
            arriving(slot, slot, columns).start()

        def two(step, _):
            slot = 2 * (step % (slots // 2))
            for k in range(2):
                arriving(2 * step + k, slot + k, columns).wait()

            def taken(rows):
                return jnp.concatenate(
                    [q_ref[slot, rows, :width], q_ref[slot + 1, rows, :width]], axis=1
                )

            for i in range(count):
                product = dot(taken(at(i)), taken(pl.ds(i * TILE, n - i * TILE)), NT)
                for j in range(i, count):
                    b = order.index((i, j))
                    total[b] = total[b] + product[:, (j - i) * TILE : (j - i + 1) * TILE]

            @pl.when(step < (pieces - slots) // 2)
            def _():
                for k in range(2):
                    arriving(2 * step + slots + k, slot + k, columns).start()

            return 0

        lax.fori_loop(0, pieces // 2, two, 0)

    def apply(columns, t, core):
        half = t.shape[0] // 2
        width = columns.stop - columns.start
        both = jnp.concatenate(parts(t), axis=0)
        for slot in range(slots):
            arriving(slot, slot, columns).start()

        def one(y, _):
            slot = y % slots
            arriving(y, slot, columns).wait()
            product = times(both, q_ref[slot, :, :width])
            product = product[: t.shape[0]] + product[t.shape[0] :]
            own_ref[y, :, :width] = product[core * half : (core + 1) * half]
            other_ref[y, :, :width] = product[(1 - core) * half : (2 - core) * half]

            @pl.when(y < pieces - slots)
            def _():
                arriving(y + slots, slot, columns).start()

            return 0

        lax.fori_loop(0, pieces, one, 0)

    total[...] = jnp.zeros_like(total)
    own_ref[...] = jnp.zeros_like(own_ref)
    other_ref[...] = jnp.zeros_like(other_ref)

    @pl.when(which_ref[0] == 1)
    def _():
        gram(slice(0, IN_COLS))

    @pl.when(which_ref[0] != 1)
    def _():
        gram(slice(IN_COLS, BLOCK))

    diagonal = lax.broadcasted_iota(jnp.int32, (TILE, TILE), 0) == lax.broadcasted_iota(jnp.int32, (TILE, TILE), 1)
    square = jnp.zeros((1, 1), F32)
    for b, (i, j) in enumerate(order):
        if i == j:
            square = square + jnp.sum(jnp.where(diagonal, total[b], 0.0), keepdims=True)
    inverse = 1.0 / (jnp.sqrt(square) + NORM_FLOOR)
    scale = inverse * inverse

    def put(value, i, j, top_ref, rest_ref):
        top = value.astype(BF16)
        top_ref[at(i), at(j)] = top
        if i != j:
            top_ref[at(j), at(i)] = top.T
        if rest_ref is not None:
            rest_ref[at(i), at(j)] = (value - top.astype(F32)).astype(BF16)

    def put_row(value, i, top_ref, rest_ref):
        for j in range(i, count):
            put(value[:, (j - i) * TILE : (j - i + 1) * TILE], i, j, top_ref, rest_ref)

    for b, (i, j) in enumerate(order):
        put(total[b] * scale, i, j, high, low)

    def polynomial(q):
        for i in range(count):
            rest = pl.ds(i * TILE, n - i * TILE)
            value = times(high[at(i), :], high[:, rest])
            put_row(POLY_SECOND * high[at(i), rest].astype(F32) + POLY_THIRD * value, i, q, None)

    def whole(top_ref, rest_ref, i, rest):
        return top_ref[at(i), rest].astype(F32) + rest_ref[at(i), rest].astype(F32)

    def iterate(step, _):
        q = q_ref.at[step]
        polynomial(q)
        for i in range(count):
            rest = pl.ds(i * TILE, n - i * TILE)
            value = times(q[at(i), :], high[:, rest]) + POLY_FIRST * whole(high, low, i, rest)
            put_row(value, i, h_high, h_low)
        for i in range(count):
            rest = pl.ds(i * TILE, n - i * TILE)
            value = times(h_high[at(i), :], q[:, rest]) + POLY_FIRST * whole(h_high, h_low, i, rest)
            put_row(value, i, high, low)
        return 0

    def thin(t, matrix):
        top, rest = parts(t)
        both = times(jnp.concatenate([top, rest], axis=0), matrix)
        return both[: t.shape[0]] + both[t.shape[0] :]

    def multiplied(t, step):
        return POLY_FIRST * t + thin(t, q_ref[step])

    def last_gram(t):
        return multiplied(thin(multiplied(t, NS_STEPS - 2), high[...]), NS_STEPS - 2)

    lax.fori_loop(0, NS_STEPS - 2, iterate, 0)
    polynomial(q_ref.at[NS_STEPS - 2])
    pick = pick_ref[...]
    once = last_gram(pick)
    t = POLY_FIRST * pick + POLY_SECOND * once + POLY_THIRD * last_gram(once)
    for step in reversed(range(NS_STEPS - 1)):
        t = multiplied(t, step)
    t = t * inverse

    @pl.when(which_ref[0] == 1)
    def _():
        apply(slice(0, IN_COLS), t, 0)

    @pl.when(which_ref[0] != 1)
    def _():
        apply(slice(IN_COLS, BLOCK), t, 1)


SMALL = pltpu.CompilerParams(vmem_limit_bytes=20 << 20)
LARGE = pltpu.CompilerParams(vmem_limit_bytes=60 << 20)


def spec(shape, index=None):
    return pl.BlockSpec(shape, index if index is not None else (lambda c: (0,) * len(shape)))


def rows(width, height=SPAN):
    return spec((height, width), lambda c: (c, 0))


def rows_back(width, height=SPAN):
    return spec((height, width), lambda c: (STEPS - 1 - c, 0))


def previous(c):
    return jnp.where(c == 0, (TOKENS + EDGE) // 8 - 1, c * (SPAN // 8) - 1)


def shaped(*shape, dtype=F32):
    return jax.ShapeDtypeStruct(shape, dtype)


def cost(flops, moved):
    return pl.CostEstimate(flops=flops, bytes_accessed=moved, transcendentals=0)


def piece_of(kind):
    size = 4

    def index(c, place):
        return ((place[0] - jnp.minimum(c, size - 1) + size) % size, 0, 0)

    return pl.BlockSpec((1, CHUNK, D), index)


def project(place, own, other, edge, weights, gain):
    total = TOKENS + EDGE
    block = 2 * CHUNK

    def out(width):
        return pl.BlockSpec((block, width), lambda c, place: (c, 0))

    def whole(*shape):
        return pl.BlockSpec(shape, lambda c, place: (0, 0))

    return pl.pallas_call(
        project_kernel,
        grid_spec=pltpu.PrefetchScalarGridSpec(
            num_scalar_prefetch=1,
            grid=(TOKENS // block + 1,),
            in_specs=[
                piece_of("own"),
                piece_of("other"),
                whole(EDGE, D),
                whole(D, FORWARD_COLS),
                whole(1, D),
            ],
            out_specs=[out(D), out(EG), out(VG), out(LANES)],
        ),
        out_shape=[
            shaped(total, D, dtype=BF16),
            shaped(total, EG),
            shaped(total, VG),
            shaped(total, LANES),
        ],
        compiler_params=SMALL,
        cost_estimate=cost(2 * total * D * FORWARD_COLS, 16 << 20),
        name="project",
    )(place, own, other, edge, weights, gain)


def incoming(place, own, other, weights):
    block = 2 * CHUNK

    def out(width):
        return pl.BlockSpec((block, width), lambda c, place: (c, 0))

    return pl.pallas_call(
        incoming_kernel,
        grid_spec=pltpu.PrefetchScalarGridSpec(
            num_scalar_prefetch=1,
            grid=(TOKENS // block,),
            in_specs=[
                piece_of("own"),
                piece_of("other"),
                pl.BlockSpec((D, EG), lambda c, place: (0, FORWARD_COLS // EG)),
            ],
            out_specs=[out(D), out(EG)],
        ),
        out_shape=[shaped(TOKENS, D, dtype=BF16), shaped(TOKENS, EG)],
        compiler_params=SMALL,
        cost_estimate=cost(2 * TOKENS * D * EG, 9 << 20),
        name="incoming",
    )(place, own, other, weights)


def early_products(normed, q, dz, gated):
    return pl.pallas_call(
        early_kernel,
        grid=(D // TILE,),
        in_specs=[
            spec((TOKENS + EDGE, TILE), lambda c: (0, c)),
            spec((TOKENS, TILE), lambda c: (0, c)),
            spec((TOKENS, EG)),
            spec((TOKENS, EG)),
        ],
        out_specs=rows(2 * EG, TILE),
        out_shape=shaped(D, 2 * EG, dtype=BF16),
        compiler_params=SMALL,
        cost_estimate=cost(4 * TOKENS * D * EG, 13 << 20),
        name="early",
    )(normed, q, dz, gated)


def forward(v, r, flags, ids, taps, head):
    return pl.pallas_call(
        forward_kernel,
        grid=(STEPS,),
        in_specs=[
            rows(VG),
            spec((8, VG), lambda c: (previous(c), 0)),
            rows(LANES),
            rows(LANES),
            spec((8, LANES)),
            spec((8, VG)),
            spec((8, LANES)),
        ],
        out_specs=[
            rows(VG),
            rows(LANES),
            rows(LANES),
            rows(EG),
            spec((AT_ONCE, N, EG), lambda c: (c, 0, 0)),
            rows(EG, 8 * AT_ONCE),
            rows(EG, 8 * AT_ONCE),
            spec((STATE_ROWS, EG)),
        ],
        out_shape=[
            shaped(TOKENS, VG),
            shaped(TOKENS, LANES),
            shaped(TOKENS, LANES),
            shaped(TOKENS, EG),
            shaped(PIECES, N, EG),
            shaped(PIECES * 8, EG),
            shaped(PIECES * 8, EG),
            shaped(STATE_ROWS, EG),
        ],
        scratch_shapes=[pltpu.VMEM((N, EG), F32), pltpu.VMEM((8, EG), F32)],
        compiler_params=SMALL,
        cost_estimate=cost(3 << 30, 14 << 20),
        name="forward",
    )(v, v, r, flags, ids, taps, head)


def outputs(y_part, conv, cum, flags, z, d_gated, reach, arrivals, wide):
    return pl.pallas_call(
        output_kernel,
        grid=(STEPS,),
        in_specs=[rows(EG), rows(VG), rows(LANES), rows(LANES), rows(EG), rows(EG), rows(EG, 8 * AT_ONCE)]
        + [spec((STATE_ROWS, EG))] * 3
        + [spec((8, EG))],
        out_specs=[rows(EG), spec((2 * PIECES, LANES)), spec((N, EG))],
        out_shape=[shaped(TOKENS, EG), shaped(2 * PIECES, LANES), shaped(N, EG)],
        compiler_params=SMALL,
        cost_estimate=cost(1 << 28, 12 << 20),
        name="outputs",
    )(y_part, conv, cum, flags, z, d_gated, reach, *arrivals, wide)


def gate(y, z, d_gated, conv, cum, flags, gain, sums, wide):
    return pl.pallas_call(
        gate_kernel,
        grid=(STEPS,),
        in_specs=[rows_back(EG)] * 3
        + [rows_back(VG), rows_back(LANES), rows_back(LANES), rows_back(EG, 8 * AT_ONCE)]
        + [spec((2 * PIECES, LANES)), spec((8, EG))],
        out_specs=[rows_back(EG)] * 3
        + [
            spec((AT_ONCE, N, EG), lambda c: (STEPS - 1 - c, 0, 0)),
            rows_back(EG, 8 * AT_ONCE),
            spec((8, EG)),
            spec((STATE_ROWS, EG)),
        ],
        out_shape=[
            shaped(TOKENS, EG, dtype=BF16),
            shaped(TOKENS, EG, dtype=BF16),
            shaped(TOKENS, EG),
            shaped(PIECES, N, EG),
            shaped(PIECES * 8, EG),
            shaped(8, EG),
            shaped(STATE_ROWS, EG),
        ],
        scratch_shapes=[pltpu.VMEM((N, EG), F32), pltpu.VMEM((8, EG), F32)],
        compiler_params=SMALL,
        cost_estimate=cost(1 << 28, 14 << 20),
        name="gate",
    )(y, z, d_gated, conv, cum, flags, gain, sums, wide)


def inner(dy, conv, dt, cum, flags, ids):
    return pl.pallas_call(
        inner_kernel,
        grid=(STEPS,),
        in_specs=[rows(EG), rows(VG), rows(LANES), rows(LANES), rows(LANES), spec((8, LANES))],
        out_specs=[rows(EG), rows(2 * N)],
        out_shape=[shaped(TOKENS, EG), shaped(TOKENS, 2 * N)],
        compiler_params=SMALL,
        cost_estimate=cost(3 << 30, 9 << 20),
        name="inner",
    )(dy, conv, dt, cum, flags, ids)


def backward(
    place, u, d_bc, dy, y, conv, dt, cum, r, flags, starts, reach, arrived, ends, reach_back, arrivals,
    final, v, wide, taps, head, summer, edge_flags,
):
    def back_state():
        return spec((AT_ONCE, N, EG), lambda c: (STEPS - 1 - c, 0, 0))

    return pl.pallas_call(
        backward_kernel,
        grid=(STEPS,),
        in_specs=[
            pl.BlockSpec(memory_space=pltpu.SMEM),
            rows_back(EG),
            rows_back(2 * N),
            rows_back(EG),
            rows_back(EG),
            rows_back(VG),
            rows_back(LANES),
            rows_back(LANES),
            rows_back(LANES),
            rows_back(LANES),
            back_state(),
            rows_back(EG, 8 * AT_ONCE),
            spec((N, EG)),
            back_state(),
            rows_back(EG, 8 * AT_ONCE),
        ]
        + [spec((STATE_ROWS, EG))] * 4
        + [
            rows_back(EG),
            spec((8, EG), lambda c: (previous(STEPS - 1 - c), 0)),
            spec((8, EG)),
            spec((8, VG)),
            spec((8, LANES)),
            spec((EG, LANES)),
            spec((8, LANES)),
        ],
        out_specs=[
            rows_back(EG),
            spec((EDGE, EG)),
            spec((N, SPAN), lambda c: (0, STEPS - 1 - c)),
            spec((N, SPAN), lambda c: (0, STEPS - 1 - c)),
            rows_back(LANES),
            spec((8, EG)),
            spec((8, LANES)),
        ],
        out_shape=[
            shaped(TOKENS, EG, dtype=BF16),
            shaped(EDGE, EG, dtype=BF16),
            shaped(N, TOKENS),
            shaped(N, TOKENS),
            shaped(TOKENS, LANES),
            shaped(8, EG),
            shaped(8, LANES),
        ],
        scratch_shapes=[
            pltpu.VMEM((8, EG), F32),
            pltpu.VMEM((8, LANES), F32),
            pltpu.VMEM((N, EG), F32),
        ],
        compiler_params=SMALL,
        cost_estimate=cost(3 << 29, 20 << 20),
        name="backward",
    )(
        place, u, d_bc, dy, y, conv, dt, cum, r, flags, starts, reach, arrived, ends, reach_back,
        *arrivals, final, v, v, wide, taps, head, summer, edge_flags,
    )


def shared(team, got, conv, v, dr, flags, edge_flags, taps):
    def turned(step):
        return jnp.maximum(STEPS - 1 - step, 0)

    def lanes_of(block):
        return spec((SPAN, LANES), lambda c: (turned(c), block))

    def before(block):
        return spec((8, LANES), lambda c: (previous(turned(c)), block))

    b, c_block = EG // LANES, EG // LANES + 1
    def kernel(team_ref, a, b, c, d, *refs):
        shared_kernel(team_ref, (a, b, c, d), *refs)

    return pl.pallas_call(
        kernel,
        grid=(STEPS + 1,),
        in_specs=[
            pl.BlockSpec(memory_space=pltpu.SMEM),
            *[spec((BG, SPAN), lambda c: (0, turned(c)))] * 4,
            lanes_of(b),
            lanes_of(c_block),
            lanes_of(b),
            lanes_of(c_block),
            before(b),
            before(c_block),
            lanes_of(0),
            lanes_of(0),
            spec((8, LANES)),
            spec((8, LANES)),
        ],
        out_specs=[
            spec((SPAN, LANES), lambda c: (jnp.where(c == STEPS, STEPS, turned(c)), 0)),
            spec((8, LANES)),
        ],
        out_shape=[shaped(TOKENS + EDGE, LANES, dtype=BF16), shaped(8, LANES)],
        scratch_shapes=[pltpu.VMEM((8, LANES), F32)],
        compiler_params=SMALL,
        cost_estimate=cost(1 << 27, 6 << 20),
        name="shared",
    )(team, *got, conv, conv, v, v, v, v, dr, flags, edge_flags, taps)


def finish(hidden, cotangent, d_normed, mixed, gain):
    count = hidden.shape[0]
    return pl.pallas_call(
        finish_kernel,
        grid=(2,),
        in_specs=[rows(D, count // 2)] * 4 + [spec((1, D))],
        out_specs=[rows(D, count // 2)] * 2,
        out_shape=[shaped(count, D, dtype=BF16), shaped(count, D)],
        compiler_params=pltpu.CompilerParams(vmem_limit_bytes=60 << 20),
        cost_estimate=cost(20 * count * D, 4 << 20),
        name="finish",
    )(hidden, cotangent, d_normed, mixed, gain)


def solve(which, x, pick):
    pieces, n, _ = x.shape
    return pl.pallas_call(
        solve_kernel,
        out_shape=[shaped(pieces, pick.shape[0] // 2, IN_COLS)] * 2,
        in_specs=[
            pl.BlockSpec(memory_space=pltpu.SMEM),
            pl.BlockSpec(memory_space=pl.ANY),
            pl.BlockSpec(memory_space=pltpu.VMEM),
        ],
        out_specs=[pl.BlockSpec(memory_space=pltpu.VMEM)] * 2,
        scratch_shapes=[pltpu.VMEM((len(triangle(n)), TILE, TILE), F32)]
        + [pltpu.VMEM((n, n), BF16)] * 4
        + [pltpu.VMEM((NS_STEPS - 1, n, n), BF16), pltpu.SemaphoreType.DMA((NS_STEPS - 1,))],
        compiler_params=pltpu.CompilerParams(vmem_limit_bytes=62 << 20),
        cost_estimate=cost(20 * n * n * n, 44 << 20),
        name="solve",
    )(which.astype(jnp.int32).reshape(1), x, pick)


def summaries(packed, direction):
    size = lax.axis_size("x")
    return [
        lax.ppermute(
            packed,
            "x",
            [(s, s + direction * k) for s in range(size) if 0 <= s + direction * k < size],
        )
        for k in range(1, size)
    ]


def blocks_of_columns(in_rows, out_rows):
    count = in_rows.shape[0]
    kind = in_rows.dtype
    z = in_rows[:, :E].reshape(count, G, EG)
    xs = in_rows[:, E : 2 * E].reshape(count, G, EG)
    bc = in_rows[:, 2 * E : 2 * E + 2 * N].reshape(count, G, BG)
    r = in_rows[:, 2 * E + 2 * N :].reshape(count, G, HG)
    fill = jnp.zeros((count, G, LANES - BG - HG), kind)
    out = out_rows.reshape(count, G, EG)
    return jnp.concatenate([z, xs, bc, r, fill, out], axis=2).transpose(1, 0, 2)


def rows_of_blocks(blocks):
    count = blocks.shape[1]
    b = blocks.transpose(1, 0, 2)
    pieces = [
        b[:, :, :EG].reshape(count, E),
        b[:, :, EG : 2 * EG].reshape(count, E),
        b[:, :, 2 * EG : 2 * EG + BG].reshape(count, 2 * N),
        b[:, :, 2 * EG + BG : 2 * EG + BG + HG].reshape(count, H),
    ]
    return jnp.concatenate(pieces, axis=1), b[:, :, IN_COLS:].reshape(count, E)


def along_y(own):
    size = lax.axis_size("y")
    return [own] + [
        lax.ppermute(own, "y", [(s, (s + k) % size) for s in range(size)]) for k in range(1, size)
    ]


def team_sum(values):
    values = values + lax.ppermute(values, "c", [(0, 1), (1, 0)])
    return sum(along_y(values))


def summands(normed, gradient):
    part = dot(normed, gradient, TN).astype(BF16)
    return lax.all_to_all(
        part.reshape(16, D // 16, part.shape[1]), ROWS, 0, 0, tiled=True
    )


def after(value, *others):
    return lax.optimization_barrier((value,) + others)[0]


def local(
    hidden,
    segments,
    norm_gain,
    in_weight,
    conv_weight,
    conv_bias,
    dt_bias,
    a_log,
    skip_scale,
    gate_gain,
    out_weight,
    cotangent,
    in_momentum,
    out_momentum,
    vector_momentum,
):
    zi, xi, yi, ci = (lax.axis_index(a) for a in EVERY)
    team = yi * 2 + ci
    count = in_weight.shape[0]
    team_count = G * count
    swap = [(0, 1), (1, 0)]
    first = ci == 0

    def mine(values, width, start=0, axis=-1):
        return lax.dynamic_slice_in_dim(values, start + team * width, width, axis % values.ndim)

    z_w = in_weight[:, :E].reshape(count, G, EG)
    xs_w = in_weight[:, E : 2 * E].reshape(count, G, EG)
    bc_w = jnp.broadcast_to(in_weight[:, None, 2 * E : 2 * E + 2 * N], (count, G, 2 * N))
    r_w = jnp.pad(
        in_weight[:, 2 * E + 2 * N :].reshape(count, G, HG), ((0, 0), (0, 0), (0, LANES - HG))
    )
    out_w = out_weight.reshape(count, G, EG)
    sent = jnp.concatenate([z_w, xs_w, bc_w, r_w, out_w], axis=2).transpose(1, 0, 2)
    got = lax.all_to_all(sent, TEAM, 0, 0, tiled=True).reshape(team_count, -1)
    weights = lax.all_gather(got, ROWS, axis=0, tiled=True)

    numbers = jnp.pad(segments.astype(BF16)[:, None], ((0, 0), (0, LANES - 1)))
    pieces = along_y(jnp.concatenate([hidden, numbers], axis=1))
    momentum_block = lax.all_to_all(
        blocks_of_columns(
            *(after(m, got).astype(BF16) for m in (in_momentum, out_momentum))
        ),
        TEAM,
        0,
        0,
        tiled=True,
    ).reshape(team_count, BLOCK)
    conv_all = jnp.concatenate([conv_weight, conv_bias[None, :]], axis=0)
    taps = jnp.pad(
        jnp.concatenate([mine(conv_all[:, :E], EG), conv_all[:, E:]], axis=1),
        ((0, 8 - TAPS - 1), (0, 0)),
    )
    taps_shared = jnp.pad(mine(conv_all[:, E:], BG), ((0, 8 - TAPS - 1), (0, LANES - BG)))
    head = jnp.pad(
        jnp.stack([mine(dt_bias, HG), jnp.exp(mine(a_log, HG))]), ((0, 6), (0, LANES - HG))
    )
    wide = jnp.pad(
        jnp.stack([jnp.repeat(mine(skip_scale, HG), HEAD), mine(gate_gain, EG)]), ((0, 6), (0, 0))
    )
    summer = (
        lax.broadcasted_iota(jnp.int32, (EG, LANES), 0) // HEAD
        == lax.broadcasted_iota(jnp.int32, (EG, LANES), 1)
    ).astype(BF16)
    pieces, momentum_block, taps, taps_shared, head, wide, summer = lax.optimization_barrier(
        (pieces, momentum_block, taps, taps_shared, head, wide, summer)
    )
    own_rows = jnp.stack(pieces)
    other_rows = lax.ppermute(own_rows, "c", swap)
    q_pieces = along_y(after(cotangent, own_rows))
    place = jnp.stack([yi, ci]).astype(jnp.int32)
    size_x, size_y = lax.axis_size("x"), lax.axis_size("y")
    end_rows = lax.dynamic_index_in_dim(
        jnp.where(first, other_rows[:, CHUNK - EDGE :], own_rows[:, CHUNK - EDGE :]),
        (yi + 1) % size_y,
        0,
        False,
    )
    edge_rows_in = lax.ppermute(end_rows, "x", [(s, s + 1) for s in range(size_x - 1)])
    by_distance = jnp.stack([own_rows[:, :, D], other_rows[:, :, D]]).astype(F32)
    by_core = jnp.where(first, by_distance, by_distance[::-1])
    team_ids = by_core[:, (yi - jnp.arange(size_y)) % size_y].transpose(1, 0, 2).reshape(-1)
    next_ids = lax.ppermute(team_ids[:LANES], "x", [(s, s - 1) for s in range(1, size_x)])
    ids = jnp.concatenate(
        [
            jnp.where(xi == 0, -1.0, edge_rows_in[EDGE - 8 :, D].astype(F32)),
            team_ids,
            jnp.where(xi == size_x - 1, -1.0, next_ids[:8]),
        ]
    )

    def flag_lanes(at, size):
        own = ids[at : at + size]
        same = [(ids[at - k : at - k + size] == own).astype(F32) for k in range(TAPS)]
        ahead = [(ids[at + k : at + k + size] == own).astype(F32) for k in range(TAPS)]
        return own, same + ahead

    own_ids, lanes = flag_lanes(8, TOKENS)
    by_piece = own_ids.reshape(PIECES, CHUNK)
    before = ids[7 : 7 + TOKENS].reshape(PIECES, CHUNK)[:, :1]
    last = by_piece[:, CHUNK - 1 :]
    lanes = lanes + [
        jnp.zeros((TOKENS,), F32),
        (by_piece == before).astype(F32).reshape(-1),
        (by_piece == last).astype(F32).reshape(-1),
        jnp.broadcast_to((last == before).astype(F32), (PIECES, CHUNK)).reshape(-1),
        own_ids,
    ]
    flags = jnp.pad(jnp.stack(lanes, axis=1), ((0, 0), (0, LANES - len(lanes))))
    edge_ids = jnp.pad(ids, (8, 0), constant_values=-1.0)[: 8 + 16]
    edge_own = edge_ids[8:16]
    edge_flags = jnp.pad(
        jnp.stack(
            [jnp.zeros((8,), F32)] * AHEAD
            + [(edge_ids[8 + k : 16 + k] == edge_own).astype(F32) for k in range(TAPS)],
            axis=1,
        ),
        ((0, 0), (0, LANES - AHEAD - TAPS)),
    )

    q_pieces, flags, edge_flags = lax.optimization_barrier((q_pieces, flags, edge_flags))
    q_own = jnp.stack(q_pieces)
    q_other = lax.ppermute(q_own, "c", swap)

    normed, z, v, r = project(
        place, own_rows, other_rows, edge_rows_in, weights, norm_gain[None, :]
    )
    conv, dt, cum, y_part, starts, reach, gain, packed = forward(v, r, flags, by_piece, taps, head)
    arrivals = summaries(packed, 1)
    q_team, d_gated = incoming(place, q_own, q_other, weights)
    y, sums, arrived = outputs(y_part, conv, cum, flags, z, d_gated, reach, arrivals, wide)
    sums = team_sum(sums)
    gated, dz, dy, ends, reach_back, d_gate, packed_back = gate(
        y, z, d_gated, conv, cum, flags, gain, sums, wide
    )
    early = early_products(normed, q_team, dz, gated)
    dy, packed_back, early = lax.optimization_barrier((dy, packed_back, early))
    early_sum = lax.psum_scatter(early, ROWS, scatter_dimension=0, tiled=True).astype(F32)
    arrivals_back = summaries(packed_back, -1)

    u, d_bc = inner(dy, conv, dt, cum, flags, by_piece)
    dv, d_edge, kept, sent_bc, dr, wide_sums, head_sums_out = backward(
        place, u, d_bc, dy, y, conv, dt, cum, r, flags, starts, reach, arrived, ends, reach_back,
        arrivals_back, packed, v, wide, taps, head, summer, edge_flags,
    )
    summed = (kept + lax.ppermute(sent_bc, "c", swap)).reshape(size_y, BG, TOKENS)

    def piece_for(k):
        return lax.dynamic_index_in_dim(summed, (yi + k) % size_y, 0, False)

    d_bc_got = [piece_for(0)] + [
        lax.ppermute(piece_for(k), "y", [(s, (s + k) % size_y) for s in range(size_y)])
        for k in range(1, size_y)
    ]
    late_x = jnp.concatenate([dv, d_edge], axis=0)
    x_parts = summands(normed, late_x)
    d_bc_got, x_parts = lax.optimization_barrier((d_bc_got, x_parts))
    late_shared, shared_sums = shared(
        team.reshape(1), d_bc_got, conv, v, dr, flags, edge_flags, taps_shared
    )
    late_sum = jnp.concatenate(
        [jnp.sum(p.astype(F32), axis=0) for p in (x_parts, summands(normed, late_shared))], axis=1
    )

    ahead = MATRIX_MOMENTUM * momentum_block.astype(F32)
    late_new = (ahead[:, EG:IN_COLS] + late_sum).astype(BF16)
    late_new, ahead = lax.optimization_barrier((late_new, ahead))
    momenta = jnp.concatenate(
        [
            (ahead[:, :EG] + early_sum[:, :EG]).astype(BF16),
            late_new,
            (ahead[:, IN_COLS:] + early_sum[:, EG:]).astype(BF16),
        ],
        axis=1,
    )
    sums_block = jnp.concatenate([early_sum[:, :EG], late_sum, early_sum[:, EG:]], axis=1)
    x_all = lax.all_gather(momenta, TEAM + ROWS).reshape(G, D, BLOCK)

    late = jnp.concatenate([late_x, late_shared], axis=1)
    late_back = lax.ppermute(
        late[TOKENS:], "x", [(s, s - 1) for s in range(1, lax.axis_size("x"))]
    )
    late, late_back, dz, gated, late_sum = lax.optimization_barrier(
        (late, late_back, dz, gated, late_sum)
    )
    d_projected = jnp.concatenate(
        [
            dz,
            jnp.concatenate(
                [late[: TOKENS - EDGE], late[TOKENS - EDGE : TOKENS] + late_back], axis=0
            ),
        ],
        axis=1,
    )
    w_own = jnp.concatenate(
        [
            weights[:, : 2 * EG],
            mine(weights[:, 2 * EG : 2 * EG + 2 * N], BG),
            weights[:, 2 * EG + 2 * N : 2 * EG + 2 * N + HG],
            jnp.zeros((D, LANES - BG - HG), BF16),
        ],
        axis=1,
    )
    d_normed_part = dot(d_projected, w_own, NT)
    d_norm_gain = jnp.sum(d_normed_part * normed[:TOKENS].astype(F32), axis=0) / norm_gain
    mixed_part = dot(gated, weights[:, FORWARD_COLS:], NT)

    vector = jnp.concatenate(
        [
            d_norm_gain,
            jnp.concatenate(
                [wide_sums[: TAPS + 1], shared_sums[: TAPS + 1, :BG]], axis=1
            ).reshape(-1),
            d_gate[0],
            head_sums_out[:3, :HG].reshape(-1),
        ]
    )
    vector = jnp.pad(vector, (0, -vector.shape[0] % 1024)).reshape(-1, LANES)
    vector = jnp.sum(lax.all_gather(vector, ROWS), axis=0)
    vector = lax.all_gather(vector, TEAM).reshape(G, -1)
    own = EG + BG
    grad_gain = jnp.sum(vector[:, :D], axis=0)
    conv_parts = vector[:, D : D + (TAPS + 1) * own].reshape(G, TAPS + 1, own).transpose(1, 0, 2)
    conv_parts = jnp.concatenate(
        [
            conv_parts[:, :, :EG].reshape(TAPS + 1, E),
            conv_parts[:, :, EG:].reshape(TAPS + 1, 2 * N),
        ],
        axis=1,
    )
    rest = vector[:, D + (TAPS + 1) * own :]
    heads = rest[:, EG : EG + 3 * HG].reshape(G, 3, HG).transpose(1, 0, 2).reshape(-1)
    vector_grad = jnp.concatenate(
        [grad_gain, conv_parts.reshape(-1), heads, rest[:, :EG].reshape(-1)]
    )
    vector_old = jnp.concatenate(
        [norm_gain, conv_weight.reshape(-1), conv_bias, dt_bias, a_log, skip_scale, gate_gain]
    )
    vector_momentum_new = VECTOR_MOMENTUM * vector_momentum + (1.0 - VECTOR_MOMENTUM) * vector_grad
    vector_new = vector_old - VECTOR_RATE * vector_momentum_new
    grad_rows = lax.all_to_all(
        sums_block.reshape(G, count, BLOCK), TEAM, 0, 0, tiled=True
    )
    in_grad, out_grad = rows_of_blocks(grad_rows)
    in_momentum_new = MATRIX_MOMENTUM * in_momentum + in_grad
    out_momentum_new = MATRIX_MOMENTUM * out_momentum + out_grad

    chip_row = (zi * 4 + xi) * team_count + yi * (2 * count)
    pick = (
        lax.broadcasted_iota(jnp.int32, (2 * count, D), 1)
        == lax.broadcasted_iota(jnp.int32, (2 * count, D), 0) + chip_row
    ).astype(F32)
    (
        x_all, pick, d_normed_part, mixed_part,
        vector_grad, vector_momentum_new, vector_new,
        in_grad, in_momentum_new, out_grad, out_momentum_new,
    ) = lax.optimization_barrier(
        (
            x_all, pick, d_normed_part, mixed_part,
            vector_grad, vector_momentum_new, vector_new,
            in_grad, in_momentum_new, out_grad, out_momentum_new,
        )
    )
    own_steps, other_steps = solve(first, x_all, pick)
    d_normed = lax.psum_scatter(d_normed_part, TEAM, scatter_dimension=0, tiled=True)
    mixed = lax.psum_scatter(mixed_part, TEAM, scatter_dimension=0, tiled=True)
    block_output, input_grad = finish(hidden, cotangent, d_normed, mixed, norm_gain[None, :])

    got_steps = lax.ppermute(other_steps, "c", swap)
    both = jnp.concatenate(
        [
            jnp.where(first, own_steps, got_steps),
            jnp.where(first, got_steps, own_steps)[:, :, : BLOCK - IN_COLS],
        ],
        axis=2,
    )
    step_in, step_out = rows_of_blocks(both)
    in_weight_new = in_weight.astype(F32) - MATRIX_RATE * math.sqrt(PROJ / D) * step_in
    out_weight_new = out_weight.astype(F32) - MATRIX_RATE * math.sqrt(E / D) * step_out
    return (
        block_output,
        input_grad,
        in_grad,
        in_momentum_new,
        in_weight_new,
        out_grad,
        out_momentum_new,
        out_weight_new,
        vector_grad,
        vector_momentum_new,
        vector_new,
    )


def solution(mesh):
    grid = Mesh(mesh.devices.reshape(4, 4, 4, 2), EVERY)
    split = P(EVERY, None)
    return jax.shard_map(
        local,
        mesh=grid,
        in_specs=(
            split,
            P(EVERY),
            P(),
            split,
            P(),
            P(),
            P(),
            P(),
            P(),
            P(),
            split,
            split,
            split,
            split,
            P(),
        ),
        out_specs=(split,) * 8 + (P(),) * 3,
        check_vma=False,
    )
```
